32 devices in a mesh: seq: 8 (over z, y), head: 4 (over x, core).
Axes of the slice: x: 2, y: 2, z: 4, core: 2. Of those that a mesh axis runs over, the one named last changes fastest.
Arguments:
- hidden: float32 [8192, 2048], P('seq'), may hold values from -6 to 6
- doc_starts: int32 [7], replicated, may hold values from 0 to 8191, as said below
- norm_gain: float32 [2048], replicated, may hold values from 0.1 to 1.9
- w_query: bfloat16 [2048, 2048], P(None, 'head'), may hold values from -0.125 to 0.125
- w_key: bfloat16 [2048, 2048], P(None, 'head'), may hold values from -0.125 to 0.125
- w_value: bfloat16 [2048, 2048], P(None, 'head'), may hold values from -0.125 to 0.125
- w_strength: bfloat16 [2048, 16], P(None, 'head'), may hold values from -0.125 to 0.125
- strength_bias: float32 [16], P('head'), may hold values from -8.5 to -0.8
- conv_query: bfloat16 [4, 2048], P(None, 'head'), may hold values from -2.5 to 2.5
- conv_key: bfloat16 [4, 2048], P(None, 'head'), may hold values from -2.5 to 2.5
- conv_value: bfloat16 [4, 2048], P(None, 'head'), may hold values from -2.5 to 2.5
- head_gain: float32 [128], replicated, may hold values from 0.1 to 1.9
- w_output: bfloat16 [2048, 2048], P('head'), may hold values from -0.125 to 0.125
- ffn_gain: float32 [2048], replicated, may hold values from 0.1 to 1.9
- w_gate: bfloat16 [2048, 5632], P(None, 'head'), may hold values from -0.125 to 0.125
- w_up: bfloat16 [2048, 5632], P(None, 'head'), may hold values from -0.125 to 0.125
- w_down: bfloat16 [5632, 2048], P('head'), may hold values from -0.078125 to 0.078125
- out_grad: float32 [8192, 2048], P('seq'), may hold values from -6 to 6
Outputs:
- block_output: float32 [8192, 2048], P('seq')
- hidden_grad: float32 [8192, 2048], P('seq')
- norm_gain_grad: float32 [2048], P('seq')
- w_query_grad: float32 [2048, 2048], P('seq', 'head')
- w_key_grad: float32 [2048, 2048], P('seq', 'head')
- w_value_grad: float32 [2048, 2048], P('seq', 'head')
- w_strength_grad: float32 [2048, 16], P('seq', 'head')
- strength_bias_grad: float32 [16], P('head')
- conv_query_grad: float32 [4, 2048], P(None, 'head')
- conv_key_grad: float32 [4, 2048], P(None, 'head')
- conv_value_grad: float32 [4, 2048], P(None, 'head')
- head_gain_grad: float32 [128], replicated
- w_output_grad: float32 [2048, 2048], P('head', 'seq')
- ffn_gain_grad: float32 [2048], P('seq')
- w_gate_grad: float32 [2048, 5632], P('seq', 'head')
- w_up_grad: float32 [2048, 5632], P('seq', 'head')
- w_down_grad: float32 [5632, 2048], P('head', 'seq')
The draws below stay inside these ranges and needn't reach their ends.
Inputs may be any that keep to these rules, and one draw needn't show every extreme that they name: doc_starts rise strictly; the first is 0; the next two lie in tokens 1 to 1023; the fourth lies in tokens 8192 // 2 - 1024 // 2 to 4095; the fifth in tokens 8192 - 1023 to 7680; the sixth in tokens 8192 - 1024 // 2 + 1 to 8190; the last is token 8191.
All inputs are finite; a program needn't handle non-finite values.
Results may differ from the reference program's by a relative error of at most 0.014.
Values sent between devices are 32-bit elements; how exact they have to be, the bound alone decides.
No kernel may reach another device: no remote copies, remote signals or barrier semaphores. Data moves between devices by JAX's collectives and lax.ppermute only.
A program may use at most 320 MiB of HBM per device.

```python
import jax
import jax.numpy as jnp
from jax import lax

D = 2048
HEADS = 16
HEAD_DIM = 128
FF = 5632
CONV = 4
GROUP = 64
TOK_DEV = 1024
TOKENS = 8192


def draw_doc_starts(key, part):
    key = jax.random.fold_in(key, 11)
    first_key, middle_key, early_key, late_key = jax.random.split(key, 4)
    half_shard = TOK_DEV // 2
    opening = jnp.sort(jax.random.permutation(first_key, TOK_DEV - 1)[:2].astype(jnp.int32) + 1)
    middle = TOKENS // 2 - half_shard + jax.random.randint(middle_key, (1,), 0, half_shard, dtype=jnp.int32)
    closing_one = TOKENS - TOK_DEV + 1 + jax.random.randint(early_key, (1,), 0, half_shard, dtype=jnp.int32)
    closing_two = TOKENS - half_shard + 1 + jax.random.randint(late_key, (1,), 0, half_shard - 2, dtype=jnp.int32)
    closing_last = jnp.full((1,), TOKENS - 1, jnp.int32)
    return jnp.concatenate([jnp.zeros((1,), jnp.int32), opening.astype(jnp.int32), middle.astype(jnp.int32), closing_one.astype(jnp.int32), closing_two.astype(jnp.int32), closing_last])


def draw_strength_bias(key, part):
    key = jax.random.fold_in(key, 23)
    return jax.random.uniform(key, (HEADS,), jnp.float32, -8.0, -0.8)


def level_of(key, shape, cuts, low, high):
    level, own = 1.0, jax.random.fold_in(key, 6)
    for dim, parts in cuts:
        steps = jnp.exp(jax.random.uniform(jax.random.fold_in(own, dim), (parts,), jnp.float32, low / len(cuts), high / len(cuts)))
        level = level * jnp.repeat(steps, shape[dim] // parts).reshape([-1 if axis == dim else 1 for axis in range(len(shape))])
    return level


def gaussian(key, dims, deviation, limit, cuts=(), kind=jnp.bfloat16):
    result = deviation * jax.random.normal(key, dims, jnp.float32)
    if cuts:
        result = result * level_of(key, dims, cuts, -0.22, 0.18)
    return jnp.clip(result, -limit, limit).astype(kind)


def setup_inputs(seed: int = 0) -> dict:
    seeds = jax.random.split(jax.random.key(seed), 19)
    return {
        "hidden": gaussian(seeds[0], (TOKENS, D), 1.0, 6.0, ((0, 8),), jnp.float32),
        "doc_starts": draw_doc_starts(jax.random.fold_in(seeds[18], 71), 0),
        "norm_gain": jnp.clip(1.0 + 0.18 * jax.random.normal(seeds[2], (D,), jnp.float32), 0.1, 1.9),
        "w_query": gaussian(seeds[3], (D, D), D ** -0.5, 0.125, ((1, 4),)),
        "w_key": gaussian(seeds[4], (D, D), D ** -0.5, 0.125, ((1, 4),)),
        "w_value": gaussian(seeds[5], (D, D), D ** -0.5, 0.125, ((1, 4),)),
        "w_strength": gaussian(seeds[6], (D, HEADS), D ** -0.5, 0.125, ((1, 4),)),
        "strength_bias": draw_strength_bias(jax.random.fold_in(seeds[18], 71), 0),
        "conv_query": gaussian(seeds[8], (CONV, D), 0.5, 2.5, ((1, 4),)),
        "conv_key": gaussian(seeds[9], (CONV, D), 0.5, 2.5, ((1, 4),)),
        "conv_value": gaussian(seeds[10], (CONV, D), 0.5, 2.5, ((1, 4),)),
        "head_gain": jnp.clip(1.0 + 0.18 * jax.random.normal(seeds[11], (HEAD_DIM,), jnp.float32), 0.1, 1.9),
        "w_output": gaussian(seeds[12], (D, D), D ** -0.5, 0.125, ((0, 4),)),
        "ffn_gain": jnp.clip(1.0 + 0.18 * jax.random.normal(seeds[13], (D,), jnp.float32), 0.1, 1.9),
        "w_gate": gaussian(seeds[14], (D, FF), D ** -0.5, 0.125, ((1, 4),)),
        "w_up": gaussian(seeds[15], (D, FF), D ** -0.5, 0.125, ((1, 4),)),
        "w_down": gaussian(seeds[16], (FF, D), FF ** -0.5, 0.078125, ((0, 4),)),
        "out_grad": gaussian(seeds[17], (TOKENS, D), 1.0, 6.0, ((0, 8),), jnp.float32),
    }


HIGH = lax.Precision.HIGHEST

@jax.custom_vjp
def low(v):
    return lax.optimization_barrier(v.astype(jnp.bfloat16)).astype(jnp.float32)

@jax.custom_vjp
def low_back(v):
    return v

def low_keep(v):
    return (low(v), None)

def low_pass(kept, grad):
    return (grad,)

def back_keep(v):
    return (v, None)

def back_low(kept, grad):
    return (low(grad),)
low.defvjp(low_keep, low_pass)
low_back.defvjp(back_keep, back_low)

def doc_index(starts, places):
    return lax.optimization_barrier(jnp.sum((starts[None, :] <= places[:, None]).astype(jnp.int32), axis=1)) - 1

def rms_norm(values, scaling):
    return values * lax.rsqrt(lax.optimization_barrier(jnp.mean(values * values, axis=-1, keepdims=True)) + 1e-05) * scaling

def unit_rows(values):
    return values * lax.rsqrt(lax.optimization_barrier(jnp.sum(values * values, axis=-1, keepdims=True)) + 1e-06)

def matmul(left, right):
    return jnp.dot(left, right, precision=HIGH, preferred_element_type=jnp.float32)

def short_conv(linear, border, kernel, doc_ids, border_ids):
    length = linear.shape[0]
    joined = jnp.concatenate([border, linear], axis=0)
    joined_ids = jnp.concatenate([border_ids, doc_ids])
    summed = jnp.zeros_like(linear)
    for offset in range(kernel.shape[0]):
        same_doc = (joined_ids[offset:offset + length] == doc_ids).astype(jnp.float32)
        summed = summed + kernel[offset][None, :] * joined[offset:offset + length] * same_doc[:, None]
    return summed

def prepare(lin_query, lin_key, lin_value, border, conv_query, conv_key, conv_value, logits, doc_ids, border_ids, head_size):
    length = lin_query.shape[0]
    inner_width = lin_query.shape[1]
    pieces = []
    for number, (linear, kernel) in enumerate(((lin_query, conv_query), (lin_key, conv_key), (lin_value, conv_value))):
        edge_part = border[:, number * inner_width:(number + 1) * inner_width]
        mixed_rows = jax.nn.silu(short_conv(linear, edge_part, kernel, doc_ids, border_ids))
        pieces.append(mixed_rows.reshape(length, inner_width // head_size, head_size))
    return (unit_rows(pieces[0]), unit_rows(pieces[1]), pieces[2], jax.nn.sigmoid(logits))

def nilpotent_inverse(strict):
    extent = strict.shape[-1]
    eye_block = jnp.eye(extent, dtype=jnp.float32)
    inverse = eye_block - strict
    square = strict
    covered = 2
    while covered < extent:
        square = jnp.einsum('hij,hjk->hik', square, square, precision=HIGH)
        inverse = jnp.einsum('hij,hjk->hik', inverse, eye_block + square, precision=HIGH)
        covered = covered * 2
    return inverse

def group_terms(queries, key_rows, values, strength, carried, same_doc):
    extent = queries.shape[0]
    below = jnp.tril(jnp.ones((extent, extent), jnp.float32), -1)
    through = below + jnp.eye(extent, dtype=jnp.float32)
    key_key = jnp.einsum('ihd,jhd->hij', key_rows, key_rows, precision=HIGH)
    query_key = jnp.einsum('ihd,jhd->hij', queries, key_rows, precision=HIGH)
    rates = jnp.transpose(strength)
    strict = key_key * rates[:, :, None] * (same_doc * below)[None]
    solved = nilpotent_inverse(strict) * rates[:, None, :]
    write_keys = jnp.einsum('hij,jhd->hid', solved, key_rows * carried[:, None, None], precision=HIGH)
    write_values = jnp.einsum('hij,jhd->hid', solved, values, precision=HIGH)
    scores = query_key * (same_doc * through)[None]
    return (write_keys, write_values, scores)

def group_state(memory, queries, key_rows, write_keys, write_values, scores, carried, final_doc):
    residue = write_values - jnp.einsum('hid,hde->hie', write_keys, memory, precision=HIGH)
    outputs = jnp.einsum('ihd,hde->ihe', queries * carried[:, None, None], memory, precision=HIGH)
    outputs = outputs + jnp.einsum('hij,hje->ihe', scores, residue, precision=HIGH)
    updated = carried[-1] * memory + jnp.einsum('ihd,hie->hde', key_rows * final_doc[:, None, None], residue, precision=HIGH)
    return (updated, outputs)

def group_masks(doc_ids, prior_ids):
    carried = (doc_ids == prior_ids[:, None]).astype(jnp.float32)
    same_doc = (doc_ids[:, :, None] == doc_ids[:, None, :]).astype(jnp.float32)
    final_doc = (doc_ids == doc_ids[:, -1:]).astype(jnp.float32)
    return (carried, same_doc, final_doc)

def run_groups(memory, queries, key_rows, values, strength, carried, same_doc, final_doc):

    @jax.checkpoint
    def advance(carry_mem, pieces):
        write_keys, write_values, scores = group_terms(pieces[0], pieces[1], pieces[2], pieces[3], pieces[4], pieces[5])
        return group_state(carry_mem, pieces[0], pieces[1], write_keys, write_values, scores, pieces[4], pieces[6])
    return lax.scan(advance, memory, (queries, key_rows, values, strength, carried, same_doc, final_doc))

def reference(hidden, doc_starts, norm_gain, w_query, w_key, w_value, w_strength, strength_bias, conv_query, conv_key, conv_value, head_gain, w_output, ffn_gain, w_gate, w_up, w_down, out_grad):
    length = hidden.shape[0]
    head_size = head_gain.shape[0]
    group_count = length // GROUP
    places = jnp.arange(length, dtype=jnp.int32)
    doc_ids = doc_index(doc_starts, places)
    prior_ids = doc_index(doc_starts, places[::GROUP] - 1)
    mask_set = group_masks(doc_ids.reshape(group_count, GROUP), prior_ids)
    border_ids = -jnp.ones((CONV - 1,), jnp.int32)

    def reshape_groups(member):
        return member.reshape((group_count, GROUP) + member.shape[1:])

    def block(hidden, norm_gain, w_query, w_key, w_value, w_strength, strength_bias, conv_query, conv_key, conv_value, head_gain, w_output, ffn_gain, w_gate, w_up, w_down):
        normed = low(rms_norm(hidden, norm_gain))
        lin_query = low_back(matmul(normed, w_query))
        lin_key = low_back(matmul(normed, w_key))
        lin_value = low_back(matmul(normed, w_value))
        logits = low_back(matmul(normed, w_strength)) + strength_bias
        border = jnp.zeros((CONV - 1, 3 * lin_query.shape[1]), jnp.float32)
        queries, key_rows, values, strength = prepare(lin_query, lin_key, lin_value, border, conv_query, conv_key, conv_value, logits, doc_ids, border_ids, head_size)
        head_count = queries.shape[1]
        start_memory = jnp.zeros((head_count, head_size, head_size), jnp.float32)
        scanned = run_groups(start_memory, reshape_groups(queries), reshape_groups(key_rows), reshape_groups(values), reshape_groups(strength), mask_set[0], mask_set[1], mask_set[2])
        mixed_rows = scanned[1].reshape(length, head_count, head_size)
        headed = rms_norm(mixed_rows, head_gain).reshape(length, head_count * head_size)
        branch = low_back(matmul(low(headed), w_output))
        middle = hidden + branch
        normed_two = low(rms_norm(middle, ffn_gain))
        gate_rows = low_back(matmul(normed_two, w_gate))
        upward = low_back(matmul(normed_two, w_up))
        active = low(jax.nn.silu(gate_rows) * upward)
        return middle + low_back(matmul(active, w_down))
    inputs = (hidden, norm_gain, w_query, w_key, w_value, w_strength, strength_bias, conv_query, conv_key, conv_value, head_gain, w_output, ffn_gain, w_gate, w_up, w_down)
    floats = tuple((member.astype(jnp.float32) for member in inputs))
    output, pull = jax.vjp(block, *floats)
    grads = pull(out_grad.astype(jnp.float32))
    return (output, grads[0], grads[1], grads[2], grads[3], grads[4], grads[5], grads[6], grads[7], grads[8], grads[9], grads[10], grads[11], grads[12], grads[13], grads[14], grads[15])
```

```python
import jax
import jax.numpy as jnp
from jax import lax
from jax.experimental import pallas as pl
from jax.experimental.pallas import tpu as pltpu
from jax.sharding import PartitionSpec as P

BLOCK = 128
SUB = 32
EDGE = 8
F32 = jnp.float32
BF16 = jnp.bfloat16


def mm(left, right, left_dim=1, right_dim=0, passes=3):
    dims = (((left_dim,), (right_dim,)), ((), ()))
    if passes == 1:
        return lax.dot_general(
            left.astype(BF16), right.astype(BF16), dims, preferred_element_type=F32
        )
    precision = lax.Precision.HIGH if passes == 3 else lax.Precision.HIGHEST
    return lax.dot_general(left, right, dims, precision=precision, preferred_element_type=F32)


def doc_of(places, starts, count):
    total = jnp.full(places.shape, -1, jnp.int32) if places.shape else jnp.int32(-1)
    for index in range(count):
        total = total + jnp.where(starts[index] <= places, 1, 0).astype(jnp.int32)
    return total


def sigmoid(value):
    return 1.0 / (1.0 + jnp.exp(-value))


def block_masks(first, starts, count):
    rows = lax.broadcasted_iota(jnp.int32, (BLOCK, BLOCK), 0)
    columns = lax.broadcasted_iota(jnp.int32, (BLOCK, BLOCK), 1)
    row_docs = doc_of(first + rows, starts, count)
    column_docs = doc_of(first + columns, starts, count)
    same = row_docs == column_docs
    prior_doc = doc_of(first - 1, starts, count)
    last_doc = doc_of(first + BLOCK - 1, starts, count)
    carried = (row_docs == prior_doc).astype(F32)
    final = (row_docs == last_doc).astype(F32)
    through = jnp.where(prior_doc == last_doc, 1.0, 0.0).astype(F32)
    reach = [None]
    for back in range(1, 4):
        reach.append((row_docs == doc_of(first - back + rows, starts, count)).astype(F32))
    return rows, columns, same, carried, final, through, reach


def short_conv(joined, taps, reach):
    total = taps[3:4] * joined[EDGE:]
    for back in range(1, 4):
        total = total + taps[3 - back : 4 - back] * (
            joined[EDGE - back : EDGE - back + BLOCK] * reach[back]
        )
    return total


def block_inverse(strict, rows, columns, passes=3):
    near = jnp.where(rows // SUB == columns // SUB, strict, 0.0)
    far = strict - near
    eye = jnp.where(rows == columns, 1.0, 0.0)
    inverse = eye - near
    power = mm(near, near, passes=passes)
    covered = 2
    while covered * 2 < SUB:
        both = mm(jnp.concatenate([power, inverse], axis=0), power, passes=passes)
        power, inverse = both[:BLOCK], inverse + both[BLOCK:]
        covered *= 2
    inverse = inverse + mm(inverse, power, passes=passes)
    chain = mm(inverse, far, passes=passes)
    both = mm(chain, jnp.concatenate([inverse, chain], axis=1), passes=passes)
    partial = inverse - both[:, :BLOCK]
    return partial + mm(both[:, BLOCK:], partial, passes=passes)


def forward_kernel(
    starts,
    base,
    lin_query,
    lin_key,
    lin_value,
    edge,
    taps_query,
    taps_key,
    taps_value,
    rates,
    inverse_out,
    effective_out,
    local_out,
    memory_out,
    final_out,
    before,
    memory,
):
    heads, size = memory.shape[0], memory.shape[1]
    width = heads * size
    step = pl.program_id(0)
    count = starts.shape[0]

    @pl.when(step == 0)
    def _():
        before[...] = edge[...]
        line = lax.broadcasted_iota(jnp.int32, (size, 2 * size), 0)
        lane = lax.broadcasted_iota(jnp.int32, (size, 2 * size), 1)
        start = jnp.where(line == lane, 1.0, 0.0).astype(F32)
        for head in range(heads):
            memory[head] = start

    first = base[0] + step * BLOCK
    rows, columns, same, carried, final, through, reach = block_masks(first, starts, count)
    below = jnp.logical_and(same, columns < rows)
    upto = jnp.logical_and(same, columns <= rows)
    for head in range(heads):
        span = slice(head * size, (head + 1) * size)
        pieces = []
        for number, (lin, taps) in enumerate(
            ((lin_query, taps_query), (lin_key, taps_key), (lin_value, taps_value))
        ):
            place = slice(number * width + head * size, number * width + (head + 1) * size)
            joined = jnp.concatenate([before[:, place], lin[:, span]], axis=0)
            conv = short_conv(joined, taps[:, span], reach)
            pieces.append(conv * sigmoid(conv))
        query = pieces[0] * lax.rsqrt(jnp.sum(pieces[0] * pieces[0], axis=1, keepdims=True) + 1e-6)
        key = pieces[1] * lax.rsqrt(jnp.sum(pieces[1] * pieces[1], axis=1, keepdims=True) + 1e-6)
        value = pieces[2]
        rate = jnp.broadcast_to(rates[:, head : head + 1], (BLOCK, size))
        products = mm(jnp.concatenate([query, key], axis=0), key, 1, 1)
        scores = jnp.where(upto, products[:BLOCK], 0.0)
        strict = jnp.where(below, products[BLOCK:] * rate, 0.0)
        inverse = block_inverse(strict, rows, columns)
        inverse_out[0, head] = inverse
        writes = mm(inverse, jnp.concatenate([rate * carried * key, rate * value], axis=1))
        held = memory[head]
        memory_out[0, head] = held
        read = mm(jnp.concatenate([writes[:, :size], carried * query], axis=0), held)
        residue = (
            jnp.concatenate([jnp.zeros((BLOCK, size), F32), writes[:, size:]], axis=1)
            - read[:BLOCK]
        )
        result = read[BLOCK:] + mm(scores, residue)
        effective_out[:, span] = result[:, :size]
        local_out[:, span] = result[:, size:]
        updated = through * held + mm(final * key, residue, 0, 0)
        memory[head] = updated
        final_out[head] = updated
    for number, lin in enumerate((lin_query, lin_key, lin_value)):
        before[:, number * width : (number + 1) * width] = lin[BLOCK - EDGE :, :]


def output_kernel(effective, local, entering, gain, mixed_out, headed_out):
    heads, size = entering.shape[0], entering.shape[1]
    for head in range(heads):
        span = slice(head * size, (head + 1) * size)
        mixed = local[:, span] + mm(effective[:, span], entering[head])
        mixed_out[:, span] = mixed
        scale = lax.rsqrt(jnp.mean(mixed * mixed, axis=1, keepdims=True) + 1e-5)
        headed_out[:, span] = (mixed * scale * gain[...]).astype(headed_out.dtype)


def norm_back_kernel(headed_grad, mixed_rows, effective, gain, grad_out, gain_out, local_out):
    heads, size = local_out.shape[0], local_out.shape[1]
    step = pl.program_id(0)

    @pl.when(step == 0)
    def _():
        gain_out[...] = jnp.zeros_like(gain_out)
        local_out[...] = jnp.zeros_like(local_out)

    for head in range(heads):
        span = slice(head * size, (head + 1) * size)
        mixed = mixed_rows[:, span]
        scale = lax.rsqrt(jnp.mean(mixed * mixed, axis=1, keepdims=True) + 1e-5)
        given = headed_grad[:, span]
        gain_out[...] += jnp.sum(given * mixed * scale, axis=0, keepdims=True)
        scaled = gain[...] * given
        along = jnp.mean(mixed * scaled, axis=1, keepdims=True)
        grad = scale * scaled - mixed * (scale * scale * scale * along)
        grad_out[:, span] = grad
        local_out[head] += mm(effective[:, span], grad, 0, 0)


def backward_kernel(
    starts,
    base,
    lin_query,
    lin_key,
    lin_value,
    prior_query,
    prior_key,
    prior_value,
    edge,
    taps_query,
    taps_key,
    taps_value,
    rates,
    inverse_in,
    memory_in,
    entering,
    leaving,
    mixed_grad,
    query_out,
    key_out,
    value_out,
    edge_out,
    logit_out,
    taps_query_out,
    taps_key_out,
    taps_value_out,
    after,
    memory_grad,
):
    heads, size = entering.shape[0], entering.shape[1]
    width = heads * size
    step = pl.program_id(0)
    blocks = pl.num_programs(0)
    here = blocks - 1 - step
    count = starts.shape[0]

    @pl.when(step == 0)
    def _():
        after[...] = jnp.zeros_like(after)
        memory_grad[...] = leaving[...]
        taps_query_out[...] = jnp.zeros_like(taps_query_out)
        taps_key_out[...] = jnp.zeros_like(taps_key_out)
        taps_value_out[...] = jnp.zeros_like(taps_value_out)

    first = base[0] + here * BLOCK
    rows, columns, same, carried, final, through, reach = block_masks(first, starts, count)
    below = jnp.logical_and(same, columns < rows)
    upto = jnp.logical_and(same, columns <= rows)
    lanes = lax.broadcasted_iota(jnp.int32, (BLOCK, rates.shape[1]), 1)
    logit_grad = jnp.zeros((BLOCK, rates.shape[1]), F32)
    for head in range(heads):
        span = slice(head * size, (head + 1) * size)
        joins, convs, gates, pieces = [], [], [], []
        for number, (lin, prior, taps) in enumerate(
            (
                (lin_query, prior_query, taps_query),
                (lin_key, prior_key, taps_key),
                (lin_value, prior_value, taps_value),
            )
        ):
            place = slice(number * width + head * size, number * width + (head + 1) * size)
            border = jnp.where(here == 0, edge[:, place], prior[:, span])
            joined = jnp.concatenate([border, lin[:, span]], axis=0)
            conv = short_conv(joined, taps[:, span], reach)
            gate = sigmoid(conv)
            joins.append(joined)
            convs.append(conv)
            gates.append(gate)
            pieces.append(conv * gate)
        query_scale = lax.rsqrt(jnp.sum(pieces[0] * pieces[0], axis=1, keepdims=True) + 1e-6)
        key_scale = lax.rsqrt(jnp.sum(pieces[1] * pieces[1], axis=1, keepdims=True) + 1e-6)
        query = pieces[0] * query_scale
        key = pieces[1] * key_scale
        value = pieces[2]
        rate_column = rates[:, head : head + 1]
        rate = jnp.broadcast_to(rate_column, (BLOCK, size))
        products = mm(jnp.concatenate([query, key], axis=0), key, 1, 1)
        scores = jnp.where(upto, products[:BLOCK], 0.0)
        gram = products[BLOCK:]
        inverse = inverse_in[0, head]
        held = memory_in[0, head]
        memory = mm(held[:, :size], entering[head]) + held[:, size:]
        left = carried * key
        wanted = value - mm(left, memory)
        residue = mm(inverse, rate * wanted)
        grad_out = mixed_grad[:, span]
        grad_memory = memory_grad[head]
        last_keys = final * key
        residue_grad = mm(scores, grad_out, 0, 0) + mm(last_keys, grad_memory)
        solved_grad = mm(inverse, residue_grad, 0, 0)
        wanted_grad = rate * solved_grad
        outer = mm(jnp.concatenate([grad_out, solved_grad], axis=0), residue, 1, 1)
        scores_grad = jnp.where(upto, outer[:BLOCK], 0.0)
        strict_grad = jnp.where(below, -outer[BLOCK:], 0.0)
        gram_grad = rate * strict_grad
        rate_grad = jnp.sum(solved_grad * wanted + strict_grad * gram, axis=1, keepdims=True)
        state_side = mm(jnp.concatenate([grad_out, wanted_grad], axis=0), memory, 1, 1)
        key_side = mm(jnp.concatenate([scores_grad, gram_grad], axis=0), key)
        query_grad = carried * state_side[:BLOCK] + key_side[:BLOCK]
        key_grad = (
            key_side[BLOCK:]
            - carried * state_side[BLOCK:]
            + mm(
                jnp.concatenate([scores_grad, gram_grad], axis=0),
                jnp.concatenate([query, key], axis=0),
                0,
                0,
            )
            + final * mm(residue, grad_memory, 1, 1)
        )
        memory_grad[head] = through * grad_memory + mm(
            jnp.concatenate([carried * query, -left], axis=0),
            jnp.concatenate([grad_out, wanted_grad], axis=0),
            0,
            0,
        )
        logit_grad = jnp.where(
            lanes == head, rate_grad * rate_column * (1.0 - rate_column), logit_grad
        )
        query_grad = query_scale * (
            query_grad - query * jnp.sum(query * query_grad, axis=1, keepdims=True)
        )
        key_grad = key_scale * (key_grad - key * jnp.sum(key * key_grad, axis=1, keepdims=True))
        for number, (grad, taps, lin_out, taps_out) in enumerate(
            (
                (query_grad, taps_query, query_out, taps_query_out),
                (key_grad, taps_key, key_out, taps_key_out),
                (wanted_grad, taps_value, value_out, taps_value_out),
            )
        ):
            place = slice(number * width + head * size, number * width + (head + 1) * size)
            gate, conv, joined = gates[number], convs[number], joins[number]
            conv_grad = grad * gate * (1.0 + conv * (1.0 - gate))
            spare = jnp.zeros((EDGE, size), F32)
            lin_grad = taps[3:4, span] * conv_grad
            tail = jnp.zeros((EDGE, size), F32)
            taps_grad = [jnp.sum(conv_grad * joined[EDGE:], axis=0, keepdims=True)]
            for back in range(1, 4):
                part = conv_grad * reach[back]
                tap = taps[3 - back : 4 - back, span]
                lin_grad = lin_grad + tap * jnp.concatenate([part, spare], axis=0)[
                    back : back + BLOCK
                ]
                tail = tail + tap * jnp.concatenate([spare, part[:EDGE]], axis=0)[
                    back : back + EDGE
                ]
                taps_grad.append(
                    jnp.sum(part * joined[EDGE - back : EDGE - back + BLOCK], axis=0, keepdims=True)
                )
            taps_out[:, span] += jnp.concatenate(taps_grad[::-1], axis=0)
            carry = jnp.concatenate(
                [jnp.zeros((BLOCK - EDGE, size), F32), after[:, place]], axis=0
            )
            lin_out[:, span] = lin_grad + carry
            after[:, place] = tail
            edge_out[:, place] = tail
    logit_out[...] = logit_grad


def on_chip(kernel, name, **settings):
    return pl.pallas_call(
        kernel,
        name=name,
        compiler_params=pltpu.CompilerParams(
            dimension_semantics=("arbitrary",), vmem_limit_bytes=48 * 1024 * 1024
        ),
        **settings,
    )


def whole(shape):
    return pl.BlockSpec(shape, lambda i: (0,) * len(shape))


def scalars():
    return pl.BlockSpec(memory_space=pltpu.SMEM)


def delta_forward(starts, base, lins, edge, taps, rates, heads, size):
    length, width = lins[0].shape
    blocks = length // BLOCK
    row_block = pl.BlockSpec((BLOCK, width), lambda i: (i, 0))
    return on_chip(
        forward_kernel,
        "delta_forward",
        grid=(blocks,),
        in_specs=[scalars(), scalars()]
        + [row_block] * 3
        + [whole((EDGE, 3 * width))]
        + [whole((4, width))] * 3
        + [pl.BlockSpec((BLOCK, heads), lambda i: (i, 0))],
        out_specs=[
            pl.BlockSpec((1, heads, BLOCK, BLOCK), lambda i: (i, 0, 0, 0)),
            row_block,
            row_block,
            pl.BlockSpec((1, heads, size, 2 * size), lambda i: (i, 0, 0, 0)),
            whole((heads, size, 2 * size)),
        ],
        out_shape=[
            jax.ShapeDtypeStruct((blocks, heads, BLOCK, BLOCK), F32),
            jax.ShapeDtypeStruct((length, width), F32),
            jax.ShapeDtypeStruct((length, width), F32),
            jax.ShapeDtypeStruct((blocks, heads, size, 2 * size), F32),
            jax.ShapeDtypeStruct((heads, size, 2 * size), F32),
        ],
        scratch_shapes=[
            pltpu.VMEM((EDGE, 3 * width), F32),
            pltpu.VMEM((heads, size, 2 * size), F32),
        ],
    )(starts, base, *lins, edge, *taps, rates)


def delta_output(effective, local, entering, gain):
    length, width = local.shape
    heads, size = entering.shape[0], entering.shape[1]
    rows = min(length, 256)
    row_block = pl.BlockSpec((rows, width), lambda i: (i, 0))
    return on_chip(
        output_kernel,
        "delta_output",
        grid=(length // rows,),
        in_specs=[row_block, row_block, whole((heads, size, size)), whole((1, size))],
        out_specs=[row_block, row_block],
        out_shape=[
            jax.ShapeDtypeStruct((length, width), F32),
            jax.ShapeDtypeStruct((length, width), BF16),
        ],
    )(effective, local, entering, gain)


def norm_back(headed_grad, mixed_rows, effective, gain, heads, size):
    length, width = headed_grad.shape
    rows = min(length, 256)
    row_block = pl.BlockSpec((rows, width), lambda i: (i, 0))
    return on_chip(
        norm_back_kernel,
        "norm_back",
        grid=(length // rows,),
        in_specs=[row_block, row_block, row_block, whole((1, size))],
        out_specs=[row_block, whole((1, size)), whole((heads, size, size))],
        out_shape=[
            jax.ShapeDtypeStruct((length, width), F32),
            jax.ShapeDtypeStruct((1, size), F32),
            jax.ShapeDtypeStruct((heads, size, size), F32),
        ],
    )(headed_grad, mixed_rows, effective, gain)


def delta_backward(
    starts, base, lins, edge, taps, rates, inverse, memories, entering, leaving, mixed_grad
):
    length, width = lins[0].shape
    heads, size = entering.shape[0], entering.shape[1]
    blocks = length // BLOCK
    ratio = BLOCK // EDGE
    row_block = pl.BlockSpec((BLOCK, width), lambda i: (blocks - 1 - i, 0))
    prior = pl.BlockSpec(
        (EDGE, width), lambda i: (jnp.maximum((blocks - 1 - i) * ratio - 1, 0), 0)
    )
    rate_block = pl.BlockSpec((BLOCK, heads), lambda i: (blocks - 1 - i, 0))
    return on_chip(
        backward_kernel,
        "delta_backward",
        grid=(blocks,),
        in_specs=[scalars(), scalars()]
        + [row_block] * 3
        + [prior] * 3
        + [whole((EDGE, 3 * width))]
        + [whole((4, width))] * 3
        + [
            rate_block,
            pl.BlockSpec((1, heads, BLOCK, BLOCK), lambda i: (blocks - 1 - i, 0, 0, 0)),
            pl.BlockSpec((1, heads, size, 2 * size), lambda i: (blocks - 1 - i, 0, 0, 0)),
            whole((heads, size, size)),
            whole((heads, size, size)),
            row_block,
        ],
        out_specs=[row_block] * 3
        + [whole((EDGE, 3 * width)), rate_block]
        + [whole((4, width))] * 3,
        out_shape=[jax.ShapeDtypeStruct((length, width), F32)] * 3
        + [
            jax.ShapeDtypeStruct((EDGE, 3 * width), F32),
            jax.ShapeDtypeStruct((length, heads), F32),
        ]
        + [jax.ShapeDtypeStruct((4, width), F32)] * 3,
        scratch_shapes=[
            pltpu.VMEM((EDGE, 3 * width), F32),
            pltpu.VMEM((heads, size, size), F32),
        ],
    )(starts, base, *lins, *lins, edge, *taps, rates, inverse, memories, entering, leaving, mixed_grad)


def swap(block, axis, bit):
    count = lax.axis_size(axis)
    return lax.ppermute(block, axis, [(i, i ^ bit) for i in range(count)])


def shift(block, axis, distance):
    devices = range(lax.axis_size(axis))
    route = [(i - distance, i) for i in devices if i - distance in devices]
    return lax.ppermute(block, axis, route)


def sum_over_head(term):
    if lax.axis_size("head") != 4:
        return lax.psum(term, "head")
    odd = lax.axis_index("head") % 2
    half = term.shape[0] // 2
    keep = lax.dynamic_slice_in_dim(term, odd * half, half, 0)
    send = lax.dynamic_slice_in_dim(term, (1 - odd) * half, half, 0)
    part = keep + swap(send, "head", 1)
    part = part + swap(part, "head", 2)
    other = swap(part, "head", 1)
    return jnp.where(
        odd == 0,
        jnp.concatenate([part, other], axis=0),
        jnp.concatenate([other, part], axis=0),
    )


def relative_order(bits):
    if not bits:
        return [0]
    rest = relative_order(bits[1:])
    return [index ^ bits[0] for index in rest] + rest


def seq_bits(late):
    bits = []
    while 1 << len(bits) < lax.axis_size("seq"):
        bits.append(1 << len(bits))
    return bits[1:] + bits[:1] if late else bits


def arranged(rows, late=False):
    here = lax.axis_index("seq")
    size = rows.shape[1] // lax.axis_size("seq")
    return jnp.concatenate(
        [
            lax.dynamic_slice_in_dim(rows, (here ^ index) * size, size, 1)
            for index in relative_order(seq_bits(late))
        ],
        axis=1,
    )


def token_sum(rows, others, rows_first=True, late=False):
    half = rows.shape[1] // 2
    dim = 0 if rows_first else 1

    def product(piece):
        left, right = (piece, others) if rows_first else (others, piece)
        return lax.dot_general(
            left, right, (((0,), (0,)), ((), ())), preferred_element_type=F32
        )

    bits = seq_bits(late)
    given = product(rows[:, :half])
    kept = product(rows[:, half:])
    for place, bit in enumerate(bits):
        kept = kept + swap(given, "seq", bit)
        if place + 1 < len(bits):
            size = kept.shape[dim] // 2
            given = lax.slice_in_dim(kept, 0, size, axis=dim)
            kept = lax.slice_in_dim(kept, size, 2 * size, axis=dim)
    return kept


def chain(transfer, offset, distance):
    hops = max(lax.axis_size("seq") // 2, 1)
    state = shift(offset, "seq", distance)
    for _ in range(hops - 1):
        moved = jnp.einsum("hij,hjk->hik", transfer, state, precision=lax.Precision.HIGH) + offset
        state = shift(moved, "seq", distance)
    return state


def row_norm(values):
    return lax.rsqrt(jnp.mean(values * values, axis=-1, keepdims=True) + 1e-05)


def matmul(left, right, left_dim=1, right_dim=0):
    return lax.dot_general(
        left, right, (((left_dim,), (right_dim,)), ((), ())), preferred_element_type=F32
    )


def norm_pull(grad, values, scale, gain):
    scaled = gain * grad
    along = jnp.mean(values * scaled, axis=-1, keepdims=True)
    return scale * scaled - values * (scale * scale * scale * along)


def shards(
    hidden,
    doc_starts,
    norm_gain,
    w_query,
    w_key,
    w_value,
    w_strength,
    strength_bias,
    conv_query,
    conv_key,
    conv_value,
    head_gain,
    w_output,
    ffn_gain,
    w_gate,
    w_up,
    w_down,
    out_grad,
):
    length = hidden.shape[0]
    size = head_gain.shape[0]
    heads = strength_bias.shape[0]
    width = heads * size
    seq_rank = lax.axis_index("seq")
    seq_count = lax.axis_size("seq")
    base = (seq_rank * length).astype(jnp.int32).reshape(1)
    taps = tuple(part.astype(F32) for part in (conv_query, conv_key, conv_value))
    gain = head_gain.reshape(1, size)

    scale_one = row_norm(hidden)
    normed = (hidden * scale_one * norm_gain).astype(BF16)
    lins = tuple(matmul(normed, part) for part in (w_query, w_key, w_value))
    tails = jnp.concatenate([part[-EDGE:] for part in lins], axis=1)
    edge = shift(tails, "seq", 1)
    rates = jax.nn.sigmoid(matmul(normed, w_strength) + strength_bias)
    inverse, effective, local, memories, last = delta_forward(
        doc_starts, base, lins, edge, taps, rates, heads, size
    )
    transfer, offset = last[:, :, :size], last[:, :, size:]
    entering = chain(transfer, offset, 1)
    mixed_rows, headed = delta_output(effective, local, entering, gain)

    middle = hidden + sum_over_head(matmul(headed, w_output))
    scale_two = row_norm(middle)
    normed_two = (middle * scale_two * ffn_gain).astype(BF16)
    gate_rows = matmul(normed_two, w_gate)
    upward = matmul(normed_two, w_up)
    sigma = jax.nn.sigmoid(gate_rows)
    silu_gate = gate_rows * sigma
    active = (silu_gate * upward).astype(BF16)
    ffn_cot = out_grad.astype(BF16)
    active_grad = matmul(ffn_cot, w_down, 1, 1)
    gate_cot = (active_grad * upward * sigma * (1.0 + gate_rows * (1.0 - sigma))).astype(BF16)
    up_cot = (active_grad * silu_gate).astype(BF16)
    two_part = matmul(gate_cot, w_gate, 1, 1) + matmul(up_cot, w_up, 1, 1)
    normed_two_grad = sum_over_head(two_part)
    middle_grad = out_grad + norm_pull(normed_two_grad, middle, scale_two, ffn_gain)
    ffn_gain_part = jnp.sum(normed_two_grad * middle * scale_two, axis=0)
    branch_cot = middle_grad.astype(BF16)
    headed_grad = matmul(branch_cot, w_output, 1, 1)

    normed_two_ordered = arranged(normed_two)
    w_gate_grad = token_sum(normed_two_ordered, gate_cot)
    w_up_grad = token_sum(normed_two_ordered, up_cot)
    w_down_grad = token_sum(arranged(ffn_cot), active, False)
    block_output = middle + sum_over_head(matmul(active, w_down))

    mixed_grad, head_gain_part, local_grad = norm_back(
        headed_grad, mixed_rows, effective, gain, heads, size
    )
    leaving = chain(jnp.transpose(transfer, (0, 2, 1)), local_grad, -1)
    back = delta_backward(
        doc_starts, base, lins, edge, taps, rates, inverse, memories, entering, leaving, mixed_grad
    )
    returned = shift(back[3], "seq", -1)
    cots = tuple(
        jnp.concatenate(
            [part[:-EDGE], part[-EDGE:] + returned[:, index * width : (index + 1) * width]], axis=0
        ).astype(BF16)
        for index, part in enumerate(back[:3])
    )
    logit_grad = back[4]
    strength_cot = logit_grad.astype(BF16)
    first_part = matmul(cots[0], w_query, 1, 1)
    first_part = first_part + matmul(cots[1], w_key, 1, 1)
    first_part = first_part + matmul(cots[2], w_value, 1, 1)
    first_part = first_part + matmul(strength_cot, w_strength, 1, 1)
    normed_grad = sum_over_head(first_part)
    hidden_grad = middle_grad + norm_pull(normed_grad, hidden, scale_one, norm_gain)
    norm_gain_part = jnp.sum(first_part * hidden * scale_one, axis=0)

    w_output_grad = token_sum(arranged(branch_cot), headed, False)
    normed_ordered = arranged(normed)
    lin_grads = tuple(token_sum(normed_ordered, part) for part in cots)
    strength_term = matmul(strength_cot, normed, 0, 0)

    small = jnp.concatenate(
        [strength_term.reshape(-1), ffn_gain_part]
        + [part.reshape(-1) for part in back[5:8]]
        + [jnp.sum(logit_grad, axis=0)]
    )
    small = lax.psum(small, "seq")
    features = norm_gain.shape[0]
    block = features // seq_count
    cut = [heads * features, features] + [4 * width] * 3 + [heads]
    parts, at = [], 0
    for extent in cut:
        parts.append(small[at : at + extent])
        at += extent
    shared = lax.psum(
        jnp.concatenate([norm_gain_part, head_gain_part.reshape(-1)]), ("seq", "head")
    )

    def own(vector, axis=0):
        return lax.dynamic_slice_in_dim(vector, seq_rank * block, block, axis)

    return (
        block_output,
        hidden_grad,
        own(shared[:features]),
        lin_grads[0],
        lin_grads[1],
        lin_grads[2],
        own(parts[0].reshape(heads, features), 1).T,
        parts[5],
        parts[2].reshape(4, width),
        parts[3].reshape(4, width),
        parts[4].reshape(4, width),
        shared[features:],
        w_output_grad,
        own(parts[1]),
        w_gate_grad,
        w_up_grad,
        w_down_grad,
    )


def solution(mesh):
    return jax.shard_map(
        shards,
        mesh=mesh,
        in_specs=(
            P("seq", None),
            P(),
            P(),
            P(None, "head"),
            P(None, "head"),
            P(None, "head"),
            P(None, "head"),
            P("head"),
            P(None, "head"),
            P(None, "head"),
            P(None, "head"),
            P(),
            P("head", None),
            P(),
            P(None, "head"),
            P(None, "head"),
            P("head", None),
            P("seq", None),
        ),
        out_specs=(
            P("seq", None),
            P("seq", None),
            P("seq"),
            P("seq", "head"),
            P("seq", "head"),
            P("seq", "head"),
            P("seq", "head"),
            P("head"),
            P(None, "head"),
            P(None, "head"),
            P(None, "head"),
            P(),
            P("head", "seq"),
            P("seq"),
            P("seq", "head"),
            P("seq", "head"),
            P("head", "seq"),
        ),
        check_vma=False,
    )
```

```python
import jax
import jax.numpy as jnp
from jax import lax
from jax.experimental import pallas as pl
from jax.experimental.pallas import tpu as pltpu
from jax.sharding import PartitionSpec as P

BLOCK = 128
SUB = 32
EDGE = 8
F32 = jnp.float32
BF16 = jnp.bfloat16


def mm(left, right, left_dim=1, right_dim=0, passes=3):
    dims = (((left_dim,), (right_dim,)), ((), ()))
    if passes == 1:
        return lax.dot_general(
            left.astype(BF16), right.astype(BF16), dims, preferred_element_type=F32
        )
    precision = lax.Precision.HIGH if passes == 3 else lax.Precision.HIGHEST
    return lax.dot_general(left, right, dims, precision=precision, preferred_element_type=F32)


def doc_of(places, starts, count):
    total = jnp.full(places.shape, -1, jnp.int32) if places.shape else jnp.int32(-1)
    for index in range(count):
        total = total + jnp.where(starts[index] <= places, 1, 0).astype(jnp.int32)
    return total


def sigmoid(value):
    return 1.0 / (1.0 + jnp.exp(-value))


def block_masks(first, starts, count):
    rows = lax.broadcasted_iota(jnp.int32, (BLOCK, BLOCK), 0)
    columns = lax.broadcasted_iota(jnp.int32, (BLOCK, BLOCK), 1)
    row_docs = doc_of(first + rows, starts, count)
    column_docs = doc_of(first + columns, starts, count)
    same = row_docs == column_docs
    prior_doc = doc_of(first - 1, starts, count)
    last_doc = doc_of(first + BLOCK - 1, starts, count)
    carried = (row_docs == prior_doc).astype(F32)
    final = (row_docs == last_doc).astype(F32)
    through = jnp.where(prior_doc == last_doc, 1.0, 0.0).astype(F32)
    reach = [None]
    for back in range(1, 4):
        reach.append((row_docs == doc_of(first - back + rows, starts, count)).astype(F32))
    return rows, columns, same, carried, final, through, reach


def short_conv(joined, taps, reach):
    total = taps[3:4] * joined[EDGE:]
    for back in range(1, 4):
        total = total + taps[3 - back : 4 - back] * (
            joined[EDGE - back : EDGE - back + BLOCK] * reach[back]
        )
    return total


def block_inverses(stricts, rows, columns, passes=3):
    near_mask = rows // SUB == columns // SUB
    eye = jnp.where(rows == columns, 1.0, 0.0)
    nears = [jnp.where(near_mask, strict, 0.0) for strict in stricts]
    fars = [strict - near for strict, near in zip(stricts, nears)]
    inverses = [eye - near for near in nears]
    powers = [mm(near, near, passes=passes) for near in nears]
    covered = 2
    while covered * 2 < SUB:
        both = [
            mm(jnp.concatenate([power, inverse], axis=0), power, passes=passes)
            for power, inverse in zip(powers, inverses)
        ]
        powers = [part[:BLOCK] for part in both]
        inverses = [inverse + part[BLOCK:] for inverse, part in zip(inverses, both)]
        covered *= 2
    inverses = [
        inverse + mm(inverse, power, passes=passes) for inverse, power in zip(inverses, powers)
    ]
    chains = [mm(inverse, far, passes=passes) for inverse, far in zip(inverses, fars)]
    both = [
        mm(link, jnp.concatenate([inverse, link], axis=1), passes=passes)
        for link, inverse in zip(chains, inverses)
    ]
    partials = [inverse - part[:, :BLOCK] for inverse, part in zip(inverses, both)]
    return [
        partial + mm(part[:, BLOCK:], partial, passes=passes)
        for partial, part in zip(partials, both)
    ]


def forward_kernel(
    starts,
    base,
    lin_query,
    lin_key,
    lin_value,
    edge,
    taps_query,
    taps_key,
    taps_value,
    rates,
    inverse_out,
    effective_out,
    local_out,
    memory_out,
    final_out,
    before,
    memory,
):
    heads, size = memory.shape[0], memory.shape[1]
    width = heads * size
    step = pl.program_id(0)
    count = starts.shape[0]

    @pl.when(step == 0)
    def _():
        before[...] = edge[...]
        line = lax.broadcasted_iota(jnp.int32, (size, 2 * size), 0)
        lane = lax.broadcasted_iota(jnp.int32, (size, 2 * size), 1)
        start = jnp.where(line == lane, 1.0, 0.0).astype(F32)
        for head in range(heads):
            memory[head] = start

    first = base[0] + step * BLOCK
    rows, columns, same, carried, final, through, reach = block_masks(first, starts, count)
    below = jnp.logical_and(same, columns < rows)
    upto = jnp.logical_and(same, columns <= rows)
    queries, keys, values, stricts, scores, rate_list = [], [], [], [], [], []
    for head in range(heads):
        span = slice(head * size, (head + 1) * size)
        pieces = []
        for number, (lin, taps) in enumerate(
            ((lin_query, taps_query), (lin_key, taps_key), (lin_value, taps_value))
        ):
            place = slice(number * width + head * size, number * width + (head + 1) * size)
            joined = jnp.concatenate([before[:, place], lin[:, span]], axis=0)
            conv = short_conv(joined, taps[:, span], reach)
            pieces.append(conv * sigmoid(conv))
        query = pieces[0] * lax.rsqrt(jnp.sum(pieces[0] * pieces[0], axis=1, keepdims=True) + 1e-6)
        key = pieces[1] * lax.rsqrt(jnp.sum(pieces[1] * pieces[1], axis=1, keepdims=True) + 1e-6)
        queries.append(query)
        keys.append(key)
        values.append(pieces[2])
        rate_list.append(jnp.broadcast_to(rates[:, head : head + 1], (BLOCK, size)))
    for number, lin in enumerate((lin_query, lin_key, lin_value)):
        before[:, number * width : (number + 1) * width] = lin[BLOCK - EDGE :, :]
    for head in range(heads):
        products = mm(jnp.concatenate([queries[head], keys[head]], axis=0), keys[head], 1, 1)
        scores.append(jnp.where(upto, products[:BLOCK], 0.0))
        stricts.append(jnp.where(below, products[BLOCK:] * rate_list[head], 0.0))
    inverses = block_inverses(stricts, rows, columns)
    for head in range(heads):
        inverse_out[0, head] = inverses[head]
    writes = [
        mm(
            inverses[head],
            jnp.concatenate(
                [rate_list[head] * carried * keys[head], rate_list[head] * values[head]], axis=1
            )
        )
        for head in range(heads)
    ]
    helds = [memory[head] for head in range(heads)]
    for head in range(heads):
        memory_out[0, head] = helds[head]
    reads = [
        mm(
            jnp.concatenate([writes[head][:, :size], carried * queries[head]], axis=0),
            helds[head]
        )
        for head in range(heads)
    ]
    residues = [
        jnp.concatenate(
            [-reads[head][:BLOCK, :size], writes[head][:, size:] - reads[head][:BLOCK, size:]],
            axis=1,
        )
        for head in range(heads)
    ]
    updates = [
        through * helds[head] + mm(final * keys[head], residues[head], 0, 0)
        for head in range(heads)
    ]
    for head in range(heads):
        memory[head] = updates[head]
        final_out[head] = updates[head]
    for head in range(heads):
        span = slice(head * size, (head + 1) * size)
        result = reads[head][BLOCK:] + mm(scores[head], residues[head])
        effective_out[:, span] = result[:, :size]
        local_out[:, span] = result[:, size:]


def output_kernel(effective, local, entering, gain, mixed_out, headed_out, rounded_out):
    heads, size = entering.shape[0], entering.shape[1]
    for head in range(heads):
        span = slice(head * size, (head + 1) * size)
        mixed = local[:, span] + mm(effective[:, span], entering[head])
        mixed_out[:, span] = mixed
        scale = lax.rsqrt(jnp.mean(mixed * mixed, axis=1, keepdims=True) + 1e-5)
        headed = mixed * scale * gain[...]
        headed_out[:, span] = headed
        rounded_out[:, span] = headed.astype(rounded_out.dtype)


def norm_back_kernel(headed_grad, mixed_rows, effective, gain, grad_out, gain_out, local_out):
    heads, size = local_out.shape[0], local_out.shape[1]
    step = pl.program_id(0)

    @pl.when(step == 0)
    def _():
        gain_out[...] = jnp.zeros_like(gain_out)
        local_out[...] = jnp.zeros_like(local_out)

    for head in range(heads):
        span = slice(head * size, (head + 1) * size)
        mixed = mixed_rows[:, span]
        scale = lax.rsqrt(jnp.mean(mixed * mixed, axis=1, keepdims=True) + 1e-5)
        given = headed_grad[:, span]
        gain_out[...] += jnp.sum(given * mixed * scale, axis=0, keepdims=True)
        scaled = gain[...] * given
        along = jnp.mean(mixed * scaled, axis=1, keepdims=True)
        grad = scale * scaled - mixed * (scale * scale * scale * along)
        grad_out[:, span] = grad
        local_out[head] += mm(effective[:, span], grad, 0, 0)


def backward_kernel(
    starts,
    base,
    lin_query,
    lin_key,
    lin_value,
    prior_query,
    prior_key,
    prior_value,
    edge,
    taps_query,
    taps_key,
    taps_value,
    rates,
    inverse_in,
    memory_in,
    entering,
    leaving,
    mixed_grad,
    query_out,
    key_out,
    value_out,
    edge_out,
    logit_out,
    taps_query_out,
    taps_key_out,
    taps_value_out,
    after,
    memory_grad,
):
    heads, size = entering.shape[0], entering.shape[1]
    width = heads * size
    step = pl.program_id(0)
    blocks = pl.num_programs(0)
    here = blocks - 1 - step
    count = starts.shape[0]
    every = range(heads)
    spans = [slice(head * size, (head + 1) * size) for head in every]

    @pl.when(step == 0)
    def _():
        after[...] = jnp.zeros_like(after)
        memory_grad[...] = leaving[...]
        taps_query_out[...] = jnp.zeros_like(taps_query_out)
        taps_key_out[...] = jnp.zeros_like(taps_key_out)
        taps_value_out[...] = jnp.zeros_like(taps_value_out)

    first = base[0] + here * BLOCK
    rows, columns, same, carried, final, through, reach = block_masks(first, starts, count)
    below = jnp.logical_and(same, columns < rows)
    upto = jnp.logical_and(same, columns <= rows)

    def convolved(number, lin, prior, taps, head):
        place = slice(number * width + head * size, number * width + (head + 1) * size)
        border = jnp.where(here == 0, edge[:, place], prior[:, spans[head]])
        joined = jnp.concatenate([border, lin[:, spans[head]]], axis=0)
        conv = short_conv(joined, taps[:, spans[head]], reach)
        return joined, conv, sigmoid(conv)

    def unit_scale(piece):
        return lax.rsqrt(jnp.sum(piece * piece, axis=1, keepdims=True) + 1e-6)

    query_parts = [convolved(0, lin_query, prior_query, taps_query, head) for head in every]
    key_parts = [convolved(1, lin_key, prior_key, taps_key, head) for head in every]
    value_parts = [convolved(2, lin_value, prior_value, taps_value, head) for head in every]
    query_scales = [unit_scale(conv * gate) for _, conv, gate in query_parts]
    key_scales = [unit_scale(conv * gate) for _, conv, gate in key_parts]
    queries = [conv * gate * scale for (_, conv, gate), scale in zip(query_parts, query_scales)]
    keys = [conv * gate * scale for (_, conv, gate), scale in zip(key_parts, key_scales)]
    values = [conv * gate for _, conv, gate in value_parts]
    rate_columns = [rates[:, head : head + 1] for head in every]
    rate_wide = [jnp.broadcast_to(column, (BLOCK, size)) for column in rate_columns]
    products = [
        mm(jnp.concatenate([queries[head], keys[head]], axis=0), keys[head], 1, 1)
        for head in every
    ]
    scores = [jnp.where(upto, part[:BLOCK], 0.0) for part in products]
    grams = [part[BLOCK:] for part in products]
    inverses = [inverse_in[0, head] for head in every]
    memories = [
        mm(memory_in[0, head][:, :size], entering[head]) + memory_in[0, head][:, size:]
        for head in every
    ]
    lefts = [carried * key for key in keys]
    wanted = [values[head] - mm(lefts[head], memories[head]) for head in every]
    residues = [mm(inverses[head], rate_wide[head] * wanted[head]) for head in every]
    given = [mixed_grad[:, span] for span in spans]
    score_sides = [mm(scores[head], given[head], 0, 0) for head in every]
    state_grads = [memory_grad[head] for head in every]
    last_keys = [final * key for key in keys]
    residue_grads = [
        score_sides[head] + mm(last_keys[head], state_grads[head]) for head in every
    ]
    solved_grads = [mm(inverses[head], residue_grads[head], 0, 0) for head in every]
    wanted_grads = [rate_wide[head] * solved_grads[head] for head in every]
    updates = [
        through * state_grads[head]
        + mm(
            jnp.concatenate([carried * queries[head], -lefts[head]], axis=0),
            jnp.concatenate([given[head], wanted_grads[head]], axis=0),
            0,
            0,
        )
        for head in every
    ]
    for head in every:
        memory_grad[head] = updates[head]
    outers = [
        mm(jnp.concatenate([given[head], solved_grads[head]], axis=0), residues[head], 1, 1)
        for head in every
    ]
    state_sides = [
        mm(jnp.concatenate([given[head], wanted_grads[head]], axis=0), memories[head], 1, 1)
        for head in every
    ]
    final_sides = [final * mm(residues[head], state_grads[head], 1, 1) for head in every]
    score_grads = [jnp.where(upto, part[:BLOCK], 0.0) for part in outers]
    strict_grads = [jnp.where(below, -part[BLOCK:], 0.0) for part in outers]
    gram_grads = [rate_wide[head] * strict_grads[head] for head in every]
    pairs = [
        jnp.concatenate([score_grads[head], gram_grads[head]], axis=0) for head in every
    ]
    key_sides = [mm(pairs[head], keys[head]) for head in every]
    turned_sides = [
        mm(pairs[head], jnp.concatenate([queries[head], keys[head]], axis=0), 0, 0)
        for head in every
    ]
    rate_grads = [
        jnp.sum(
            solved_grads[head] * wanted[head] + strict_grads[head] * grams[head],
            axis=1,
            keepdims=True,
        )
        for head in every
    ]
    lanes = lax.broadcasted_iota(jnp.int32, (BLOCK, rates.shape[1]), 1)
    logit_grad = jnp.zeros((BLOCK, rates.shape[1]), F32)
    for head in every:
        column = rate_columns[head]
        logit_grad = jnp.where(
            lanes == head, rate_grads[head] * column * (1.0 - column), logit_grad
        )
    logit_out[...] = logit_grad
    query_grads = [
        carried * state_sides[head][:BLOCK] + key_sides[head][:BLOCK] for head in every
    ]
    key_grads = [
        key_sides[head][BLOCK:]
        - carried * state_sides[head][BLOCK:]
        + turned_sides[head]
        + final_sides[head]
        for head in every
    ]
    query_grads = [
        scale * (grad - query * jnp.sum(query * grad, axis=1, keepdims=True))
        for scale, grad, query in zip(query_scales, query_grads, queries)
    ]
    key_grads = [
        scale * (grad - key * jnp.sum(key * grad, axis=1, keepdims=True))
        for scale, grad, key in zip(key_scales, key_grads, keys)
    ]
    spare = jnp.zeros((EDGE, size), F32)
    for number, (grads, parts, taps, lin_out, taps_out) in enumerate(
        (
            (query_grads, query_parts, taps_query, query_out, taps_query_out),
            (key_grads, key_parts, taps_key, key_out, taps_key_out),
            (wanted_grads, value_parts, taps_value, value_out, taps_value_out),
        )
    ):
        for head in every:
            span = spans[head]
            place = slice(number * width + head * size, number * width + (head + 1) * size)
            joined, conv, gate = parts[head]
            conv_grad = grads[head] * gate * (1.0 + conv * (1.0 - gate))
            lin_grad = taps[3:4, span] * conv_grad
            tail = spare
            taps_grad = [jnp.sum(conv_grad * joined[EDGE:], axis=0, keepdims=True)]
            for back in range(1, 4):
                part = conv_grad * reach[back]
                tap = taps[3 - back : 4 - back, span]
                lin_grad = lin_grad + tap * jnp.concatenate([part, spare], axis=0)[
                    back : back + BLOCK
                ]
                tail = tail + tap * jnp.concatenate([spare, part[:EDGE]], axis=0)[
                    back : back + EDGE
                ]
                taps_grad.append(
                    jnp.sum(part * joined[EDGE - back : EDGE - back + BLOCK], axis=0, keepdims=True)
                )
            taps_out[:, span] += jnp.concatenate(taps_grad[::-1], axis=0)
            lin_out[: BLOCK - EDGE, span] = lin_grad[: BLOCK - EDGE]
            lin_out[BLOCK - EDGE :, span] = lin_grad[BLOCK - EDGE :] + after[:, place]
            after[:, place] = tail
            edge_out[:, place] = tail


def on_chip(kernel, name, **settings):
    return pl.pallas_call(
        kernel,
        name=name,
        cost_estimate=pl.CostEstimate(flops=1, bytes_accessed=1, transcendentals=0),
        compiler_params=pltpu.CompilerParams(
            dimension_semantics=("arbitrary",), vmem_limit_bytes=48 * 1024 * 1024
        ),
        **settings,
    )


def whole(shape):
    return pl.BlockSpec(shape, lambda i: (0,) * len(shape))


def scalars():
    return pl.BlockSpec(memory_space=pltpu.SMEM)


def delta_forward(starts, base, lins, edge, taps, rates, heads, size):
    length, width = lins[0].shape
    blocks = length // BLOCK
    row_block = pl.BlockSpec((BLOCK, width), lambda i: (i, 0))
    return on_chip(
        forward_kernel,
        "delta_forward",
        grid=(blocks,),
        in_specs=[scalars(), scalars()]
        + [row_block] * 3
        + [whole((EDGE, 3 * width))]
        + [whole((4, width))] * 3
        + [pl.BlockSpec((BLOCK, heads), lambda i: (i, 0))],
        out_specs=[
            pl.BlockSpec((1, heads, BLOCK, BLOCK), lambda i: (i, 0, 0, 0)),
            row_block,
            row_block,
            pl.BlockSpec((1, heads, size, 2 * size), lambda i: (i, 0, 0, 0)),
            whole((heads, size, 2 * size)),
        ],
        out_shape=[
            jax.ShapeDtypeStruct((blocks, heads, BLOCK, BLOCK), F32),
            jax.ShapeDtypeStruct((length, width), F32),
            jax.ShapeDtypeStruct((length, width), F32),
            jax.ShapeDtypeStruct((blocks, heads, size, 2 * size), F32),
            jax.ShapeDtypeStruct((heads, size, 2 * size), F32),
        ],
        scratch_shapes=[
            pltpu.VMEM((EDGE, 3 * width), F32),
            pltpu.VMEM((heads, size, 2 * size), F32),
        ],
    )(starts, base, *lins, edge, *taps, rates)


def delta_output(effective, local, entering, gain):
    length, width = local.shape
    heads, size = entering.shape[0], entering.shape[1]
    rows = min(length, 256)
    row_block = pl.BlockSpec((rows, width), lambda i: (i, 0))
    return on_chip(
        output_kernel,
        "delta_output",
        grid=(length // rows,),
        in_specs=[row_block, row_block, whole((heads, size, size)), whole((1, size))],
        out_specs=[row_block, row_block, row_block],
        out_shape=[
            jax.ShapeDtypeStruct((length, width), F32),
            jax.ShapeDtypeStruct((length, width), F32),
            jax.ShapeDtypeStruct((length, width), BF16),
        ],
    )(effective, local, entering, gain)


def norm_back(headed_grad, mixed_rows, effective, gain, heads, size):
    length, width = headed_grad.shape
    rows = min(length, 256)
    row_block = pl.BlockSpec((rows, width), lambda i: (i, 0))
    return on_chip(
        norm_back_kernel,
        "norm_back",
        grid=(length // rows,),
        in_specs=[row_block, row_block, row_block, whole((1, size))],
        out_specs=[row_block, whole((1, size)), whole((heads, size, size))],
        out_shape=[
            jax.ShapeDtypeStruct((length, width), F32),
            jax.ShapeDtypeStruct((1, size), F32),
            jax.ShapeDtypeStruct((heads, size, size), F32),
        ],
    )(headed_grad, mixed_rows, effective, gain)


def norm_pull_kernel(odd, part, other, values, gain, given, grad_out, rounded_out, gain_out):
    step = pl.program_id(0)
    second = step * 2 // pl.num_programs(0)

    @pl.when(step == 0)
    def _():
        gain_out[...] = jnp.zeros_like(gain_out)

    grad = jnp.where(second == odd[0], part[...], other[...])
    value = values[...]
    scale = lax.rsqrt(jnp.mean(value * value, axis=1, keepdims=True) + 1e-5)
    gain_out[...] += jnp.sum(grad * value * scale, axis=0, keepdims=True)
    scaled = gain[...] * grad
    along = jnp.mean(value * scaled, axis=1, keepdims=True)
    result = given[...] + (scale * scaled - value * (scale * scale * scale * along))
    grad_out[...] = result
    rounded_out[...] = result.astype(rounded_out.dtype)


def norm_pulled(halves, values, gain, given):
    length, width = values.shape
    rows = length // 8
    odd = (lax.axis_index("head") % 2).astype(jnp.int32).reshape(1)
    row_block = pl.BlockSpec((rows, width), lambda i: (i, 0))
    half_block = pl.BlockSpec((rows, width), lambda i: (i % 4, 0))
    return on_chip(
        norm_pull_kernel,
        "norm_pull",
        grid=(8,),
        in_specs=[scalars(), half_block, half_block, row_block, whole((1, width)), row_block],
        out_specs=[row_block, row_block, whole((1, width))],
        out_shape=[
            jax.ShapeDtypeStruct((length, width), F32),
            jax.ShapeDtypeStruct((length, width), BF16),
            jax.ShapeDtypeStruct((1, width), F32),
        ],
    )(odd, *halves, values, gain.reshape(1, width), given)


def beside_kernel(first, second, out):
    width = first.shape[1]
    out[:, :width] = first[...].astype(out.dtype)
    out[:, width:] = second[...].astype(out.dtype)


def above_kernel(first, second, out):
    rows = first.shape[0]
    out[:rows] = first[...].astype(out.dtype)
    out[rows:] = second[...].astype(out.dtype)


def rounded_beside(first, second):
    length, width = first.shape
    rows = min(length, 256)
    block = pl.BlockSpec((rows, width), lambda i: (i, 0))
    return on_chip(
        beside_kernel,
        "rounded_beside",
        grid=(length // rows,),
        in_specs=[block, block],
        out_specs=pl.BlockSpec((rows, 2 * width), lambda i: (i, 0)),
        out_shape=jax.ShapeDtypeStruct((length, 2 * width), BF16),
    )(first, second)


def rounded_above(first, second):
    rows, width = first.shape
    columns = min(width, 256)
    block = pl.BlockSpec((rows, columns), lambda i: (0, i))
    return on_chip(
        above_kernel,
        "rounded_above",
        grid=(width // columns,),
        in_specs=[block, block],
        out_specs=pl.BlockSpec((2 * rows, columns), lambda i: (0, i)),
        out_shape=jax.ShapeDtypeStruct((2 * rows, width), BF16),
    )(first, second)


def delta_backward(
    starts, base, lins, edge, taps, rates, inverse, memories, entering, leaving, mixed_grad
):
    length, width = lins[0].shape
    heads, size = entering.shape[0], entering.shape[1]
    blocks = length // BLOCK
    ratio = BLOCK // EDGE
    row_block = pl.BlockSpec((BLOCK, width), lambda i: (blocks - 1 - i, 0))
    prior = pl.BlockSpec(
        (EDGE, width), lambda i: (jnp.maximum((blocks - 1 - i) * ratio - 1, 0), 0)
    )
    rate_block = pl.BlockSpec((BLOCK, heads), lambda i: (blocks - 1 - i, 0))
    return on_chip(
        backward_kernel,
        "delta_backward",
        grid=(blocks,),
        in_specs=[scalars(), scalars()]
        + [row_block] * 3
        + [prior] * 3
        + [whole((EDGE, 3 * width))]
        + [whole((4, width))] * 3
        + [
            rate_block,
            pl.BlockSpec((1, heads, BLOCK, BLOCK), lambda i: (blocks - 1 - i, 0, 0, 0)),
            pl.BlockSpec((1, heads, size, 2 * size), lambda i: (blocks - 1 - i, 0, 0, 0)),
            whole((heads, size, size)),
            whole((heads, size, size)),
            row_block,
        ],
        out_specs=[row_block] * 3
        + [whole((EDGE, 3 * width)), rate_block]
        + [whole((4, width))] * 3,
        out_shape=[jax.ShapeDtypeStruct((length, width), F32)] * 3
        + [
            jax.ShapeDtypeStruct((EDGE, 3 * width), F32),
            jax.ShapeDtypeStruct((length, heads), F32),
        ]
        + [jax.ShapeDtypeStruct((4, width), F32)] * 3,
        scratch_shapes=[
            pltpu.VMEM((EDGE, 3 * width), F32),
            pltpu.VMEM((heads, size, size), F32),
        ],
    )(starts, base, *lins, *lins, edge, *taps, rates, inverse, memories, entering, leaving, mixed_grad)


def swap(block, axis, bit):
    count = lax.axis_size(axis)
    return lax.ppermute(block, axis, [(i, i ^ bit) for i in range(count)])


def shift(block, axis, distance):
    devices = range(lax.axis_size(axis))
    route = [(i - distance, i) for i in devices if i - distance in devices]
    return lax.ppermute(block, axis, route)


def begun_over_head(term):
    odd = lax.axis_index("head") % 2
    half = term.shape[0] // 2
    keep = lax.dynamic_slice_in_dim(term, odd * half, half, 0)
    send = lax.dynamic_slice_in_dim(term, (1 - odd) * half, half, 0)
    return keep + swap(send, "head", 1)


def ended_over_head(part, *gates):
    part = part + after(swap(part, "head", 2), *gates)
    return part, swap(part, "head", 1)


def whole_rows(part, other):
    return jnp.where(
        lax.axis_index("head") % 2 == 0,
        jnp.concatenate([part, other], axis=0),
        jnp.concatenate([other, part], axis=0),
    )


def after(value, *others):
    return lax.optimization_barrier((value,) + others)[0] if others else value


def summed_everywhere(vector, axis):
    count = lax.axis_size(axis)
    bit = 1
    while bit < count:
        vector = vector + swap(vector, axis, bit)
        bit *= 2
    return vector


def relative_order(bits):
    if not bits:
        return [0]
    rest = relative_order(bits[1:])
    return [index ^ bits[0] for index in rest] + rest


def seq_bits():
    bits = []
    while 1 << len(bits) < lax.axis_size("seq"):
        bits.append(1 << len(bits))
    return bits


def arrange_kernel(places, rows, out):
    out[...] = rows[...]


def arranged(rows, places):
    length, size = rows.shape[0], rows.shape[1] // lax.axis_size("seq")
    if size % 128:
        return jnp.concatenate(
            [lax.dynamic_slice_in_dim(rows, place * size, size, 1) for place in places], axis=1
        )
    return pl.pallas_call(
        arrange_kernel,
        name="arrange",
        cost_estimate=pl.CostEstimate(flops=1, bytes_accessed=1, transcendentals=0),
        grid_spec=pltpu.PrefetchScalarGridSpec(
            num_scalar_prefetch=1,
            grid=(len(places),),
            in_specs=[pl.BlockSpec((length, size), lambda i, places: (0, places[i]))],
            out_specs=pl.BlockSpec((length, size), lambda i, places: (0, i)),
        ),
        out_shape=jax.ShapeDtypeStruct(rows.shape, rows.dtype),
        compiler_params=pltpu.CompilerParams(dimension_semantics=("arbitrary",)),
    )(jnp.stack(places).astype(jnp.int32), rows)


def relative_places():
    here = lax.axis_index("seq")
    return [here ^ index for index in relative_order(seq_bits())]


def product(rows, others, rows_first):
    return matmul(rows, others, 0, 0) if rows_first else matmul(others, rows, 0, 0)


def received(given, kept, axis, place):
    bits = seq_bits()
    kept = kept + swap(given, "seq", bits[place])
    if place + 1 == len(bits):
        return None, kept
    size = kept.shape[axis] // 2
    return lax.slice_in_dim(kept, 0, size, axis=axis), lax.slice_in_dim(
        kept, size, 2 * size, axis=axis
    )


def finished(given, kept, axis, place):
    while place < len(seq_bits()):
        given, kept = received(given, kept, axis, place)
        place += 1
    return kept


def chain(transfer, offset, distance, turned=False, between=()):
    hops = max(lax.axis_size("seq") // 2, 1)
    groups = 2
    count = offset.shape[0] // groups
    picks = [slice(index * count, (index + 1) * count) for index in range(groups)]
    form = "hji,hjk->hik" if turned else "hij,hjk->hik"
    states = [shift(offset[pick], "seq", distance) for pick in picks]
    for hop in range(hops - 1):
        if hop < len(between):
            states[0] = after(states[0], between[hop])
        moved = [
            jnp.einsum(form, transfer[pick], state, precision=lax.Precision.HIGH) + offset[pick]
            for pick, state in zip(picks, states)
        ]
        states = [shift(part, "seq", distance) for part in moved]
    return jnp.concatenate(states, axis=0)


def row_norm(values):
    return lax.rsqrt(jnp.mean(values * values, axis=-1, keepdims=True) + 1e-05)


def matmul(left, right, left_dim=1, right_dim=0):
    return lax.dot_general(
        left, right, (((left_dim,), (right_dim,)), ((), ())), preferred_element_type=F32
    )


def shards(
    hidden,
    doc_starts,
    norm_gain,
    w_query,
    w_key,
    w_value,
    w_strength,
    strength_bias,
    conv_query,
    conv_key,
    conv_value,
    head_gain,
    w_output,
    ffn_gain,
    w_gate,
    w_up,
    w_down,
    out_grad,
):
    length = hidden.shape[0]
    size = head_gain.shape[0]
    heads = strength_bias.shape[0]
    width = heads * size
    seq_rank = lax.axis_index("seq")
    seq_count = lax.axis_size("seq")
    base = (seq_rank * length).astype(jnp.int32).reshape(1)
    taps = tuple(part.astype(F32) for part in (conv_query, conv_key, conv_value))
    gain = head_gain.reshape(1, size)

    scale_one = row_norm(hidden)
    normed = (hidden * scale_one * norm_gain).astype(BF16)
    w_wide = w_output.astype(F32)
    w_across = swap(w_wide, "head", 2)
    lins = tuple(matmul(normed, part) for part in (w_query, w_key, w_value))
    tails = jnp.concatenate([part[-EDGE:] for part in lins], axis=1)
    edge = shift(tails, "seq", 1)
    rates = jax.nn.sigmoid(matmul(normed, w_strength) + strength_bias)
    inverse, effective, local, memories, last = delta_forward(
        doc_starts, base, lins, edge, taps, rates, heads, size
    )
    transfer, offset = last[:, :, :size], last[:, :, size:]
    entering = chain(transfer, offset, 1)
    mixed_rows, headed_wide, headed = delta_output(effective, local, entering, gain)
    h_across = swap(headed_wide, "head", 2)
    h_core = swap(headed_wide, "head", 1)
    w_late, w_across = after((w_wide, w_across), headed)
    w_near = rounded_above(w_late, swap(w_late, "head", 1))
    w_distant = rounded_above(w_across, swap(w_across, "head", 1))
    middle = hidden + matmul(rounded_beside(headed_wide, h_core), w_near)
    ffn_cot = after(out_grad, headed).astype(BF16)
    cot_ordered = arranged(ffn_cot, relative_places())
    h_across = after(h_across, middle, w_distant, cot_ordered)
    h_far = swap(h_across, "head", 1)
    middle = middle + matmul(rounded_beside(h_across, h_far), w_distant)
    scale_two = row_norm(middle)
    normed_two = (middle * scale_two * ffn_gain).astype(BF16)
    gate_rows = matmul(normed_two, w_gate)
    upward = matmul(normed_two, w_up)
    sigma = jax.nn.sigmoid(gate_rows)
    silu_gate = gate_rows * sigma
    active = (silu_gate * upward).astype(BF16)
    half = ffn_cot.shape[1] // 2
    split = active.shape[1] // 128 * 3 // 4 * 128
    lead, rest = active[:, :split], active[:, split:]
    lead_given = product(cot_ordered[:, :half], lead, False)
    ffn_cot = after(ffn_cot, lead_given)
    active_grad = matmul(ffn_cot, w_down, 1, 1)
    gate_cot = (active_grad * upward * sigma * (1.0 + gate_rows * (1.0 - sigma))).astype(BF16)
    up_cot = (active_grad * silu_gate).astype(BF16)
    gate_term = matmul(normed_two, gate_cot, 0, 0)
    w_gate_grad = lax.psum_scatter(gate_term, "seq", scatter_dimension=0, tiled=True)
    gate_late, up_late = after(gate_cot, gate_term), after(up_cot, gate_term)
    two_part = matmul(gate_late, w_gate, 1, 1) + matmul(up_late, w_up, 1, 1)
    two_begun = begun_over_head(two_part)
    ffn_begun = begun_over_head(matmul(after(active, two_begun), w_down))
    up_term = matmul(normed_two, after(up_cot, two_begun), 0, 0)
    w_up_grad = lax.psum_scatter(up_term, "seq", scatter_dimension=0, tiled=True)
    cot_ordered = after(cot_ordered, two_begun)
    lead_kept = product(cot_ordered[:, half:], lead, False)
    rest_given = product(cot_ordered[:, :half], rest, False)
    rest_kept = product(cot_ordered[:, half:], rest, False)
    middle_grad, branch_cot, ffn_gain_part = norm_pulled(
        ended_over_head(
            two_begun, ffn_begun, up_term, lead_kept, rest_given, rest_kept
        ),
        middle,
        ffn_gain,
        out_grad,
    )
    headed_grad = matmul(branch_cot, w_output, 1, 1)
    branch_ordered = arranged(after(branch_cot, headed_grad), relative_places())
    mix_given = jnp.concatenate(
        [rest_given, product(branch_ordered[:, :half], headed, False)], axis=0
    )
    mixed_grad, head_gain_part, local_grad = norm_back(
        headed_grad, mixed_rows, effective, gain, heads, size
    )
    leaving = chain(transfer, local_grad, -1, True)
    lead_given, lead_kept = received(lead_given, lead_kept, 1, 0)
    lead_given, mix_given = after((lead_given, mix_given), leaving)
    leaving = after(leaving, lead_given, mix_given)
    back = delta_backward(
        doc_starts, base, lins, edge, taps, rates, inverse, memories, entering, leaving, mixed_grad
    )
    ffn_halves = ended_over_head(ffn_begun)
    lead_given, lead_kept = received(lead_given, lead_kept, 1, 1)
    returned, logit_grad = after(
        (shift(back[3], "seq", -1), back[4]), lead_given, ffn_halves[0]
    )
    cots = tuple(
        jnp.concatenate(
            [part[:-EDGE], part[-EDGE:] + returned[:, index * width : (index + 1) * width]], axis=0
        ).astype(BF16)
        for index, part in enumerate(back[:3])
    )
    strength_cot = logit_grad.astype(BF16)
    cot = after(jnp.concatenate(cots, axis=1), w_gate_grad, lead_given)
    lin_term = product(normed, cot, True)
    lin_grad = lax.psum_scatter(lin_term, "seq", scatter_dimension=0, tiled=True)
    lin_grads = tuple(lin_grad[:, index * width : (index + 1) * width] for index in range(3))
    mix_kept = jnp.concatenate(
        [rest_kept, product(branch_ordered[:, half:], headed, False)], axis=0
    )
    late_cots, strength_cot = after((cots, strength_cot), lin_term)
    first_part = matmul(late_cots[0], w_query, 1, 1)
    first_part = first_part + matmul(late_cots[1], w_key, 1, 1)
    first_part = first_part + matmul(late_cots[2], w_value, 1, 1)
    first_part = first_part + matmul(strength_cot, w_strength, 1, 1)
    norm_gain_part = jnp.sum(first_part * hidden * scale_one, axis=0)
    shared = summed_everywhere(
        jnp.concatenate([norm_gain_part, head_gain_part.reshape(-1)]), "head"
    )
    first_begun = after(begun_over_head(first_part), shared)
    mix_given, mix_kept = received(mix_given, after(mix_kept, first_begun), 1, 0)
    lead_kept = finished(lead_given, lead_kept, 1, 2)
    first_halves = ended_over_head(first_begun, mix_given, lead_kept, w_up_grad)
    mix_given, mix_kept = received(mix_given, mix_kept, 1, 1)
    hidden_grad = norm_pulled(first_halves, hidden, norm_gain, middle_grad)[0]
    block_output = middle + whole_rows(*ffn_halves)
    mix_kept = finished(mix_given, mix_kept, 1, 2)
    rest_rows = rest.shape[1]
    w_down_grad = jnp.concatenate([lead_kept, mix_kept[:rest_rows]], axis=0)
    w_output_grad = mix_kept[rest_rows:]
    strength_term = matmul(strength_cot, normed, 0, 0)

    small = jnp.concatenate(
        [
            shared,
            strength_term.reshape(-1),
            ffn_gain_part.reshape(-1),
        ]
        + [part.reshape(-1) for part in back[5:8]]
        + [jnp.sum(logit_grad, axis=0)]
    )
    small = summed_everywhere(small, "seq")
    features = norm_gain.shape[0]
    block = features // seq_count
    cut = [features, size, heads * features, features] + [4 * width] * 3 + [heads]
    parts, at = [], 0
    for extent in cut:
        parts.append(small[at : at + extent])
        at += extent

    def own(vector, axis=0):
        return lax.dynamic_slice_in_dim(vector, seq_rank * block, block, axis)

    return (
        block_output,
        hidden_grad,
        own(parts[0]),
        lin_grads[0],
        lin_grads[1],
        lin_grads[2],
        own(parts[2].reshape(heads, features), 1).T,
        parts[7],
        parts[4].reshape(4, width),
        parts[5].reshape(4, width),
        parts[6].reshape(4, width),
        parts[1],
        w_output_grad,
        own(parts[3]),
        w_gate_grad,
        w_up_grad,
        w_down_grad,
    )


def solution(mesh):
    return jax.shard_map(
        shards,
        mesh=mesh,
        in_specs=(
            P("seq", None),
            P(),
            P(),
            P(None, "head"),
            P(None, "head"),
            P(None, "head"),
            P(None, "head"),
            P("head"),
            P(None, "head"),
            P(None, "head"),
            P(None, "head"),
            P(),
            P("head", None),
            P(),
            P(None, "head"),
            P(None, "head"),
            P("head", None),
            P("seq", None),
        ),
        out_specs=(
            P("seq", None),
            P("seq", None),
            P("seq"),
            P("seq", "head"),
            P("seq", "head"),
            P("seq", "head"),
            P("seq", "head"),
            P("head"),
            P(None, "head"),
            P(None, "head"),
            P(None, "head"),
            P(),
            P("head", "seq"),
            P("seq"),
            P("seq", "head"),
            P("seq", "head"),
            P("head", "seq"),
        ),
        check_vma=False,
    )
```

```python
import jax
import jax.numpy as jnp
from jax import lax
from jax.experimental import pallas as pl
from jax.experimental.pallas import tpu as pltpu
from jax.sharding import PartitionSpec as P

BLOCK = 128
SUB = 32
EDGE = 8
F32 = jnp.float32
BF16 = jnp.bfloat16


def mm(left, right, left_dim=1, right_dim=0, passes=3):
    dims = (((left_dim,), (right_dim,)), ((), ()))
    if passes == 1:
        return lax.dot_general(
            left.astype(BF16), right.astype(BF16), dims, preferred_element_type=F32
        )
    precision = lax.Precision.HIGH if passes == 3 else lax.Precision.HIGHEST
    return lax.dot_general(left, right, dims, precision=precision, preferred_element_type=F32)


def doc_of(places, starts, count):
    total = jnp.full(places.shape, -1, jnp.int32) if places.shape else jnp.int32(-1)
    for index in range(count):
        total = total + jnp.where(starts[index] <= places, 1, 0).astype(jnp.int32)
    return total


def sigmoid(value):
    return 1.0 / (1.0 + jnp.exp(-value))


def block_masks(first, starts, count):
    rows = lax.broadcasted_iota(jnp.int32, (BLOCK, BLOCK), 0)
    columns = lax.broadcasted_iota(jnp.int32, (BLOCK, BLOCK), 1)
    row_docs = doc_of(first + rows, starts, count)
    column_docs = doc_of(first + columns, starts, count)
    same = row_docs == column_docs
    prior_doc = doc_of(first - 1, starts, count)
    last_doc = doc_of(first + BLOCK - 1, starts, count)
    carried = (row_docs == prior_doc).astype(F32)
    final = (row_docs == last_doc).astype(F32)
    through = jnp.where(prior_doc == last_doc, 1.0, 0.0).astype(F32)
    reach = [None]
    for back in range(1, 4):
        reach.append((row_docs == doc_of(first - back + rows, starts, count)).astype(F32))
    return rows, columns, same, carried, final, through, reach


def short_conv(joined, taps, reach):
    total = taps[3:4] * joined[EDGE:]
    for back in range(1, 4):
        total = total + taps[3 - back : 4 - back] * (
            joined[EDGE - back : EDGE - back + BLOCK] * reach[back]
        )
    return total


def block_inverses(stricts, rows, columns, passes=3):
    near_mask = rows // SUB == columns // SUB
    eye = jnp.where(rows == columns, 1.0, 0.0)
    nears = [jnp.where(near_mask, strict, 0.0) for strict in stricts]
    fars = [strict - near for strict, near in zip(stricts, nears)]
    inverses = [eye - near for near in nears]
    powers = [mm(near, near, passes=passes) for near in nears]
    covered = 2
    while covered * 2 < SUB:
        both = [
            mm(jnp.concatenate([power, inverse], axis=0), power, passes=passes)
            for power, inverse in zip(powers, inverses)
        ]
        powers = [part[:BLOCK] for part in both]
        inverses = [inverse + part[BLOCK:] for inverse, part in zip(inverses, both)]
        covered *= 2
    inverses = [
        inverse + mm(inverse, power, passes=passes) for inverse, power in zip(inverses, powers)
    ]
    chains = [mm(inverse, far, passes=passes) for inverse, far in zip(inverses, fars)]
    both = [
        mm(link, jnp.concatenate([inverse, link], axis=1), passes=passes)
        for link, inverse in zip(chains, inverses)
    ]
    partials = [inverse - part[:, :BLOCK] for inverse, part in zip(inverses, both)]
    return [
        partial + mm(part[:, BLOCK:], partial, passes=passes)
        for partial, part in zip(partials, both)
    ]


def forward_kernel(
    starts,
    base,
    lin_query,
    lin_key,
    lin_value,
    edge,
    taps_query,
    taps_key,
    taps_value,
    rates,
    inverse_out,
    effective_out,
    local_out,
    memory_out,
    final_out,
    before,
    memory,
):
    heads, size = memory.shape[0], memory.shape[1]
    width = heads * size
    step = pl.program_id(0)
    count = starts.shape[0]

    @pl.when(step == 0)
    def _():
        before[...] = edge[...]
        line = lax.broadcasted_iota(jnp.int32, (size, 2 * size), 0)
        lane = lax.broadcasted_iota(jnp.int32, (size, 2 * size), 1)
        start = jnp.where(line == lane, 1.0, 0.0).astype(F32)
        for head in range(heads):
            memory[head] = start

    first = base[0] + step * BLOCK
    rows, columns, same, carried, final, through, reach = block_masks(first, starts, count)
    below = jnp.logical_and(same, columns < rows)
    upto = jnp.logical_and(same, columns <= rows)
    queries, keys, values, stricts, scores, rate_list = [], [], [], [], [], []
    for head in range(heads):
        span = slice(head * size, (head + 1) * size)
        pieces = []
        for number, (lin, taps) in enumerate(
            ((lin_query, taps_query), (lin_key, taps_key), (lin_value, taps_value))
        ):
            place = slice(number * width + head * size, number * width + (head + 1) * size)
            joined = jnp.concatenate([before[:, place], lin[:, span]], axis=0)
            conv = short_conv(joined, taps[:, span], reach)
            pieces.append(conv * sigmoid(conv))
        query = pieces[0] * lax.rsqrt(jnp.sum(pieces[0] * pieces[0], axis=1, keepdims=True) + 1e-6)
        key = pieces[1] * lax.rsqrt(jnp.sum(pieces[1] * pieces[1], axis=1, keepdims=True) + 1e-6)
        queries.append(query)
        keys.append(key)
        values.append(pieces[2])
        rate_list.append(jnp.broadcast_to(rates[:, head : head + 1], (BLOCK, size)))
    for number, lin in enumerate((lin_query, lin_key, lin_value)):
        before[:, number * width : (number + 1) * width] = lin[BLOCK - EDGE :, :]
    for head in range(heads):
        products = mm(jnp.concatenate([queries[head], keys[head]], axis=0), keys[head], 1, 1)
        scores.append(jnp.where(upto, products[:BLOCK], 0.0))
        stricts.append(jnp.where(below, products[BLOCK:] * rate_list[head], 0.0))
    inverses = block_inverses(stricts, rows, columns)
    for head in range(heads):
        inverse_out[0, head] = inverses[head]
    writes = [
        mm(
            inverses[head],
            jnp.concatenate(
                [rate_list[head] * carried * keys[head], rate_list[head] * values[head]], axis=1
            )
        )
        for head in range(heads)
    ]
    helds = [memory[head] for head in range(heads)]
    for head in range(heads):
        memory_out[0, head] = helds[head]
    reads = [
        mm(
            jnp.concatenate([writes[head][:, :size], carried * queries[head]], axis=0),
            helds[head]
        )
        for head in range(heads)
    ]
    residues = [
        jnp.concatenate(
            [-reads[head][:BLOCK, :size], writes[head][:, size:] - reads[head][:BLOCK, size:]],
            axis=1,
        )
        for head in range(heads)
    ]
    updates = [
        through * helds[head] + mm(final * keys[head], residues[head], 0, 0)
        for head in range(heads)
    ]
    for head in range(heads):
        memory[head] = updates[head]
        final_out[head] = updates[head]
    for head in range(heads):
        span = slice(head * size, (head + 1) * size)
        result = reads[head][BLOCK:] + mm(scores[head], residues[head])
        effective_out[:, span] = result[:, :size]
        local_out[:, span] = result[:, size:]


def output_kernel(effective, local, entering, gain, mixed_out, headed_out, rounded_out):
    heads, size = entering.shape[0], entering.shape[1]
    for head in range(heads):
        span = slice(head * size, (head + 1) * size)
        mixed = local[:, span] + mm(effective[:, span], entering[head])
        mixed_out[:, span] = mixed
        scale = lax.rsqrt(jnp.mean(mixed * mixed, axis=1, keepdims=True) + 1e-5)
        headed = mixed * scale * gain[...]
        headed_out[:, span] = headed
        rounded_out[:, span] = headed.astype(rounded_out.dtype)


def norm_back_kernel(headed_grad, mixed_rows, effective, gain, grad_out, gain_out, local_out):
    heads, size = local_out.shape[0], local_out.shape[1]
    step = pl.program_id(0)

    @pl.when(step == 0)
    def _():
        gain_out[...] = jnp.zeros_like(gain_out)
        local_out[...] = jnp.zeros_like(local_out)

    for head in range(heads):
        span = slice(head * size, (head + 1) * size)
        mixed = mixed_rows[:, span]
        scale = lax.rsqrt(jnp.mean(mixed * mixed, axis=1, keepdims=True) + 1e-5)
        given = headed_grad[:, span]
        gain_out[...] += jnp.sum(given * mixed * scale, axis=0, keepdims=True)
        scaled = gain[...] * given
        along = jnp.mean(mixed * scaled, axis=1, keepdims=True)
        grad = scale * scaled - mixed * (scale * scale * scale * along)
        grad_out[:, span] = grad
        local_out[head] += mm(effective[:, span], grad, 0, 0)


def backward_kernel(
    starts,
    base,
    lin_query,
    lin_key,
    lin_value,
    prior_query,
    prior_key,
    prior_value,
    edge,
    taps_query,
    taps_key,
    taps_value,
    rates,
    inverse_in,
    memory_in,
    entering,
    leaving,
    mixed_grad,
    query_out,
    key_out,
    value_out,
    edge_out,
    logit_out,
    taps_query_out,
    taps_key_out,
    taps_value_out,
    after,
    memory_grad,
):
    heads, size = entering.shape[0], entering.shape[1]
    width = heads * size
    step = pl.program_id(0)
    blocks = pl.num_programs(0)
    here = blocks - 1 - step
    count = starts.shape[0]
    every = range(heads)
    spans = [slice(head * size, (head + 1) * size) for head in every]

    @pl.when(step == 0)
    def _():
        after[...] = jnp.zeros_like(after)
        memory_grad[...] = leaving[...]
        taps_query_out[...] = jnp.zeros_like(taps_query_out)
        taps_key_out[...] = jnp.zeros_like(taps_key_out)
        taps_value_out[...] = jnp.zeros_like(taps_value_out)

    first = base[0] + here * BLOCK
    rows, columns, same, carried, final, through, reach = block_masks(first, starts, count)
    below = jnp.logical_and(same, columns < rows)
    upto = jnp.logical_and(same, columns <= rows)

    def convolved(number, lin, prior, taps, head):
        place = slice(number * width + head * size, number * width + (head + 1) * size)
        border = jnp.where(here == 0, edge[:, place], prior[:, spans[head]])
        joined = jnp.concatenate([border, lin[:, spans[head]]], axis=0)
        conv = short_conv(joined, taps[:, spans[head]], reach)
        return joined, conv, sigmoid(conv)

    def unit_scale(piece):
        return lax.rsqrt(jnp.sum(piece * piece, axis=1, keepdims=True) + 1e-6)

    query_parts = [convolved(0, lin_query, prior_query, taps_query, head) for head in every]
    key_parts = [convolved(1, lin_key, prior_key, taps_key, head) for head in every]
    value_parts = [convolved(2, lin_value, prior_value, taps_value, head) for head in every]
    query_scales = [unit_scale(conv * gate) for _, conv, gate in query_parts]
    key_scales = [unit_scale(conv * gate) for _, conv, gate in key_parts]
    queries = [conv * gate * scale for (_, conv, gate), scale in zip(query_parts, query_scales)]
    keys = [conv * gate * scale for (_, conv, gate), scale in zip(key_parts, key_scales)]
    values = [conv * gate for _, conv, gate in value_parts]
    rate_columns = [rates[:, head : head + 1] for head in every]
    rate_wide = [jnp.broadcast_to(column, (BLOCK, size)) for column in rate_columns]
    products = [
        mm(jnp.concatenate([queries[head], keys[head]], axis=0), keys[head], 1, 1)
        for head in every
    ]
    scores = [jnp.where(upto, part[:BLOCK], 0.0) for part in products]
    grams = [part[BLOCK:] for part in products]
    inverses = [inverse_in[0, head] for head in every]
    memories = [
        mm(memory_in[0, head][:, :size], entering[head]) + memory_in[0, head][:, size:]
        for head in every
    ]
    lefts = [carried * key for key in keys]
    wanted = [values[head] - mm(lefts[head], memories[head]) for head in every]
    residues = [mm(inverses[head], rate_wide[head] * wanted[head]) for head in every]
    given = [mixed_grad[:, span] for span in spans]
    score_sides = [mm(scores[head], given[head], 0, 0) for head in every]
    state_grads = [memory_grad[head] for head in every]
    last_keys = [final * key for key in keys]
    residue_grads = [
        score_sides[head] + mm(last_keys[head], state_grads[head]) for head in every
    ]
    solved_grads = [mm(inverses[head], residue_grads[head], 0, 0) for head in every]
    wanted_grads = [rate_wide[head] * solved_grads[head] for head in every]
    updates = [
        through * state_grads[head]
        + mm(
            jnp.concatenate([carried * queries[head], -lefts[head]], axis=0),
            jnp.concatenate([given[head], wanted_grads[head]], axis=0),
            0,
            0,
        )
        for head in every
    ]
    for head in every:
        memory_grad[head] = updates[head]
    outers = [
        mm(jnp.concatenate([given[head], solved_grads[head]], axis=0), residues[head], 1, 1)
        for head in every
    ]
    state_sides = [
        mm(jnp.concatenate([given[head], wanted_grads[head]], axis=0), memories[head], 1, 1)
        for head in every
    ]
    final_sides = [final * mm(residues[head], state_grads[head], 1, 1) for head in every]
    score_grads = [jnp.where(upto, part[:BLOCK], 0.0) for part in outers]
    strict_grads = [jnp.where(below, -part[BLOCK:], 0.0) for part in outers]
    gram_grads = [rate_wide[head] * strict_grads[head] for head in every]
    pairs = [
        jnp.concatenate([score_grads[head], gram_grads[head]], axis=0) for head in every
    ]
    key_sides = [mm(pairs[head], keys[head]) for head in every]
    turned_sides = [
        mm(pairs[head], jnp.concatenate([queries[head], keys[head]], axis=0), 0, 0)
        for head in every
    ]
    rate_grads = [
        jnp.sum(
            solved_grads[head] * wanted[head] + strict_grads[head] * grams[head],
            axis=1,
            keepdims=True,
        )
        for head in every
    ]
    lanes = lax.broadcasted_iota(jnp.int32, (BLOCK, rates.shape[1]), 1)
    logit_grad = jnp.zeros((BLOCK, rates.shape[1]), F32)
    for head in every:
        column = rate_columns[head]
        logit_grad = jnp.where(
            lanes == head, rate_grads[head] * column * (1.0 - column), logit_grad
        )
    logit_out[...] = logit_grad
    query_grads = [
        carried * state_sides[head][:BLOCK] + key_sides[head][:BLOCK] for head in every
    ]
    key_grads = [
        key_sides[head][BLOCK:]
        - carried * state_sides[head][BLOCK:]
        + turned_sides[head]
        + final_sides[head]
        for head in every
    ]
    query_grads = [
        scale * (grad - query * jnp.sum(query * grad, axis=1, keepdims=True))
        for scale, grad, query in zip(query_scales, query_grads, queries)
    ]
    key_grads = [
        scale * (grad - key * jnp.sum(key * grad, axis=1, keepdims=True))
        for scale, grad, key in zip(key_scales, key_grads, keys)
    ]
    spare = jnp.zeros((EDGE, size), F32)
    for number, (grads, parts, taps, lin_out, taps_out) in enumerate(
        (
            (query_grads, query_parts, taps_query, query_out, taps_query_out),
            (key_grads, key_parts, taps_key, key_out, taps_key_out),
            (wanted_grads, value_parts, taps_value, value_out, taps_value_out),
        )
    ):
        for head in every:
            span = spans[head]
            place = slice(number * width + head * size, number * width + (head + 1) * size)
            joined, conv, gate = parts[head]
            conv_grad = grads[head] * gate * (1.0 + conv * (1.0 - gate))
            lin_grad = taps[3:4, span] * conv_grad
            tail = spare
            taps_grad = [jnp.sum(conv_grad * joined[EDGE:], axis=0, keepdims=True)]
            for back in range(1, 4):
                part = conv_grad * reach[back]
                tap = taps[3 - back : 4 - back, span]
                lin_grad = lin_grad + tap * jnp.concatenate([part, spare], axis=0)[
                    back : back + BLOCK
                ]
                tail = tail + tap * jnp.concatenate([spare, part[:EDGE]], axis=0)[
                    back : back + EDGE
                ]
                taps_grad.append(
                    jnp.sum(part * joined[EDGE - back : EDGE - back + BLOCK], axis=0, keepdims=True)
                )
            taps_out[:, span] += jnp.concatenate(taps_grad[::-1], axis=0)
            lin_out[: BLOCK - EDGE, span] = lin_grad[: BLOCK - EDGE]
            lin_out[BLOCK - EDGE :, span] = lin_grad[BLOCK - EDGE :] + after[:, place]
            after[:, place] = tail
            edge_out[:, place] = tail


def on_chip(kernel, name, **settings):
    return pl.pallas_call(
        kernel,
        name=name,
        cost_estimate=pl.CostEstimate(flops=1, bytes_accessed=1, transcendentals=0),
        compiler_params=pltpu.CompilerParams(
            dimension_semantics=("arbitrary",), vmem_limit_bytes=48 * 1024 * 1024
        ),
        **settings,
    )


def whole(shape):
    return pl.BlockSpec(shape, lambda i: (0,) * len(shape))


def scalars():
    return pl.BlockSpec(memory_space=pltpu.SMEM)


def delta_forward(starts, base, lins, edge, taps, rates, heads, size):
    length, width = lins[0].shape
    blocks = length // BLOCK
    row_block = pl.BlockSpec((BLOCK, width), lambda i: (i, 0))
    return on_chip(
        forward_kernel,
        "delta_forward",
        grid=(blocks,),
        in_specs=[scalars(), scalars()]
        + [row_block] * 3
        + [whole((EDGE, 3 * width))]
        + [whole((4, width))] * 3
        + [pl.BlockSpec((BLOCK, heads), lambda i: (i, 0))],
        out_specs=[
            pl.BlockSpec((1, heads, BLOCK, BLOCK), lambda i: (i, 0, 0, 0)),
            row_block,
            row_block,
            pl.BlockSpec((1, heads, size, 2 * size), lambda i: (i, 0, 0, 0)),
            whole((heads, size, 2 * size)),
        ],
        out_shape=[
            jax.ShapeDtypeStruct((blocks, heads, BLOCK, BLOCK), F32),
            jax.ShapeDtypeStruct((length, width), F32),
            jax.ShapeDtypeStruct((length, width), F32),
            jax.ShapeDtypeStruct((blocks, heads, size, 2 * size), F32),
            jax.ShapeDtypeStruct((heads, size, 2 * size), F32),
        ],
        scratch_shapes=[
            pltpu.VMEM((EDGE, 3 * width), F32),
            pltpu.VMEM((heads, size, 2 * size), F32),
        ],
    )(starts, base, *lins, edge, *taps, rates)


def delta_output(effective, local, entering, gain):
    length, width = local.shape
    heads, size = entering.shape[0], entering.shape[1]
    rows = min(length, 256)
    row_block = pl.BlockSpec((rows, width), lambda i: (i, 0))
    return on_chip(
        output_kernel,
        "delta_output",
        grid=(length // rows,),
        in_specs=[row_block, row_block, whole((heads, size, size)), whole((1, size))],
        out_specs=[row_block, row_block, row_block],
        out_shape=[
            jax.ShapeDtypeStruct((length, width), F32),
            jax.ShapeDtypeStruct((length, width), F32),
            jax.ShapeDtypeStruct((length, width), BF16),
        ],
    )(effective, local, entering, gain)


def norm_back(headed_grad, mixed_rows, effective, gain, heads, size):
    length, width = headed_grad.shape
    rows = min(length, 256)
    row_block = pl.BlockSpec((rows, width), lambda i: (i, 0))
    return on_chip(
        norm_back_kernel,
        "norm_back",
        grid=(length // rows,),
        in_specs=[row_block, row_block, row_block, whole((1, size))],
        out_specs=[row_block, whole((1, size)), whole((heads, size, size))],
        out_shape=[
            jax.ShapeDtypeStruct((length, width), F32),
            jax.ShapeDtypeStruct((1, size), F32),
            jax.ShapeDtypeStruct((heads, size, size), F32),
        ],
    )(headed_grad, mixed_rows, effective, gain)


def norm_pull_kernel(odd, part, other, values, gain, given, grad_out, rounded_out, gain_out):
    step = pl.program_id(0)
    second = step * 2 // pl.num_programs(0)

    @pl.when(step == 0)
    def _():
        gain_out[...] = jnp.zeros_like(gain_out)

    grad = jnp.where(second == odd[0], part[...], other[...])
    value = values[...]
    scale = lax.rsqrt(jnp.mean(value * value, axis=1, keepdims=True) + 1e-5)
    gain_out[...] += jnp.sum(grad * value * scale, axis=0, keepdims=True)
    scaled = gain[...] * grad
    along = jnp.mean(value * scaled, axis=1, keepdims=True)
    result = given[...] + (scale * scaled - value * (scale * scale * scale * along))
    grad_out[...] = result
    rounded_out[...] = result.astype(rounded_out.dtype)


def norm_pulled(halves, values, gain, given):
    length, width = values.shape
    rows = length // 8
    odd = (lax.axis_index("head") % 2).astype(jnp.int32).reshape(1)
    row_block = pl.BlockSpec((rows, width), lambda i: (i, 0))
    half_block = pl.BlockSpec((rows, width), lambda i: (i % 4, 0))
    return on_chip(
        norm_pull_kernel,
        "norm_pull",
        grid=(8,),
        in_specs=[scalars(), half_block, half_block, row_block, whole((1, width)), row_block],
        out_specs=[row_block, row_block, whole((1, width))],
        out_shape=[
            jax.ShapeDtypeStruct((length, width), F32),
            jax.ShapeDtypeStruct((length, width), BF16),
            jax.ShapeDtypeStruct((1, width), F32),
        ],
    )(odd, *halves, values, gain.reshape(1, width), given)


def beside_kernel(first, second, out):
    width = first.shape[1]
    out[:, :width] = first[...].astype(out.dtype)
    out[:, width:] = second[...].astype(out.dtype)


def above_kernel(first, second, out):
    rows = first.shape[0]
    out[:rows] = first[...].astype(out.dtype)
    out[rows:] = second[...].astype(out.dtype)


def rounded_beside(first, second):
    length, width = first.shape
    rows = min(length, 256)
    block = pl.BlockSpec((rows, width), lambda i: (i, 0))
    return on_chip(
        beside_kernel,
        "rounded_beside",
        grid=(length // rows,),
        in_specs=[block, block],
        out_specs=pl.BlockSpec((rows, 2 * width), lambda i: (i, 0)),
        out_shape=jax.ShapeDtypeStruct((length, 2 * width), BF16),
    )(first, second)


def rounded_above(first, second):
    rows, width = first.shape
    columns = min(width, 256)
    block = pl.BlockSpec((rows, columns), lambda i: (0, i))
    return on_chip(
        above_kernel,
        "rounded_above",
        grid=(width // columns,),
        in_specs=[block, block],
        out_specs=pl.BlockSpec((2 * rows, columns), lambda i: (0, i)),
        out_shape=jax.ShapeDtypeStruct((2 * rows, width), BF16),
    )(first, second)


def delta_backward(
    starts, base, lins, edge, taps, rates, inverse, memories, entering, leaving, mixed_grad
):
    length, width = lins[0].shape
    heads, size = entering.shape[0], entering.shape[1]
    blocks = length // BLOCK
    ratio = BLOCK // EDGE
    row_block = pl.BlockSpec((BLOCK, width), lambda i: (blocks - 1 - i, 0))
    prior = pl.BlockSpec(
        (EDGE, width), lambda i: (jnp.maximum((blocks - 1 - i) * ratio - 1, 0), 0)
    )
    rate_block = pl.BlockSpec((BLOCK, heads), lambda i: (blocks - 1 - i, 0))
    return on_chip(
        backward_kernel,
        "delta_backward",
        grid=(blocks,),
        in_specs=[scalars(), scalars()]
        + [row_block] * 3
        + [prior] * 3
        + [whole((EDGE, 3 * width))]
        + [whole((4, width))] * 3
        + [
            rate_block,
            pl.BlockSpec((1, heads, BLOCK, BLOCK), lambda i: (blocks - 1 - i, 0, 0, 0)),
            pl.BlockSpec((1, heads, size, 2 * size), lambda i: (blocks - 1 - i, 0, 0, 0)),
            whole((heads, size, size)),
            whole((heads, size, size)),
            row_block,
        ],
        out_specs=[row_block] * 3
        + [whole((EDGE, 3 * width)), rate_block]
        + [whole((4, width))] * 3,
        out_shape=[jax.ShapeDtypeStruct((length, width), F32)] * 3
        + [
            jax.ShapeDtypeStruct((EDGE, 3 * width), F32),
            jax.ShapeDtypeStruct((length, heads), F32),
        ]
        + [jax.ShapeDtypeStruct((4, width), F32)] * 3,
        scratch_shapes=[
            pltpu.VMEM((EDGE, 3 * width), F32),
            pltpu.VMEM((heads, size, size), F32),
        ],
    )(starts, base, *lins, *lins, edge, *taps, rates, inverse, memories, entering, leaving, mixed_grad)


def swap(block, axis, bit):
    count = lax.axis_size(axis)
    return lax.ppermute(block, axis, [(i, i ^ bit) for i in range(count)])


def shift(block, axis, distance):
    devices = range(lax.axis_size(axis))
    route = [(i - distance, i) for i in devices if i - distance in devices]
    return lax.ppermute(block, axis, route)


def begun_over_head(term):
    odd = lax.axis_index("head") % 2
    half = term.shape[0] // 2
    keep = lax.dynamic_slice_in_dim(term, odd * half, half, 0)
    send = lax.dynamic_slice_in_dim(term, (1 - odd) * half, half, 0)
    return keep + swap(send, "head", 1)


def ended_over_head(part, *gates):
    part = part + after(swap(part, "head", 2), *gates)
    return part, swap(part, "head", 1)


def whole_rows(part, other):
    return jnp.where(
        lax.axis_index("head") % 2 == 0,
        jnp.concatenate([part, other], axis=0),
        jnp.concatenate([other, part], axis=0),
    )


def after(value, *others):
    return lax.optimization_barrier((value,) + others)[0] if others else value


def summed_everywhere(vector, axis):
    count = lax.axis_size(axis)
    bit = 1
    while bit < count:
        vector = vector + swap(vector, axis, bit)
        bit *= 2
    return vector


def relative_order(bits):
    if not bits:
        return [0]
    rest = relative_order(bits[1:])
    return [index ^ bits[0] for index in rest] + rest


def seq_bits():
    bits = []
    while 1 << len(bits) < lax.axis_size("seq"):
        bits.append(1 << len(bits))
    return bits


def arrange_kernel(places, rows, out):
    out[...] = rows[...]


def arranged(rows, places):
    length, size = rows.shape[0], rows.shape[1] // lax.axis_size("seq")
    if size % 128:
        return jnp.concatenate(
            [lax.dynamic_slice_in_dim(rows, place * size, size, 1) for place in places], axis=1
        )
    return pl.pallas_call(
        arrange_kernel,
        name="arrange",
        cost_estimate=pl.CostEstimate(flops=1, bytes_accessed=1, transcendentals=0),
        grid_spec=pltpu.PrefetchScalarGridSpec(
            num_scalar_prefetch=1,
            grid=(len(places),),
            in_specs=[pl.BlockSpec((length, size), lambda i, places: (0, places[i]))],
            out_specs=pl.BlockSpec((length, size), lambda i, places: (0, i)),
        ),
        out_shape=jax.ShapeDtypeStruct(rows.shape, rows.dtype),
        compiler_params=pltpu.CompilerParams(dimension_semantics=("arbitrary",)),
    )(jnp.stack(places).astype(jnp.int32), rows)


def relative_places():
    here = lax.axis_index("seq")
    return [here ^ index for index in relative_order(seq_bits())]


def product(rows, others, rows_first):
    return matmul(rows, others, 0, 0) if rows_first else matmul(others, rows, 0, 0)


def received(given, kept, axis, place):
    bits = seq_bits()
    kept = kept + swap(given, "seq", bits[place])
    if place + 1 == len(bits):
        return None, kept
    size = kept.shape[axis] // 2
    return lax.slice_in_dim(kept, 0, size, axis=axis), lax.slice_in_dim(
        kept, size, 2 * size, axis=axis
    )


def finished(given, kept, axis, place):
    while place < len(seq_bits()):
        given, kept = received(given, kept, axis, place)
        place += 1
    return kept


def chain(transfer, offset, distance, turned=False, between=()):
    hops = max(lax.axis_size("seq") // 2, 1)
    groups = 2
    count = offset.shape[0] // groups
    picks = [slice(index * count, (index + 1) * count) for index in range(groups)]
    form = "hji,hjk->hik" if turned else "hij,hjk->hik"
    states = [shift(offset[pick], "seq", distance) for pick in picks]
    for hop in range(hops - 1):
        if hop < len(between):
            states[0] = after(states[0], between[hop])
        moved = [
            jnp.einsum(form, transfer[pick], state, precision=lax.Precision.HIGH) + offset[pick]
            for pick, state in zip(picks, states)
        ]
        states = [shift(part, "seq", distance) for part in moved]
    return jnp.concatenate(states, axis=0)


def row_norm(values):
    return lax.rsqrt(jnp.mean(values * values, axis=-1, keepdims=True) + 1e-05)


def matmul(left, right, left_dim=1, right_dim=0):
    return lax.dot_general(
        left, right, (((left_dim,), (right_dim,)), ((), ())), preferred_element_type=F32
    )


def shards(
    hidden,
    doc_starts,
    norm_gain,
    w_query,
    w_key,
    w_value,
    w_strength,
    strength_bias,
    conv_query,
    conv_key,
    conv_value,
    head_gain,
    w_output,
    ffn_gain,
    w_gate,
    w_up,
    w_down,
    out_grad,
):
    length = hidden.shape[0]
    size = head_gain.shape[0]
    heads = strength_bias.shape[0]
    width = heads * size
    seq_rank = lax.axis_index("seq")
    seq_count = lax.axis_size("seq")
    base = (seq_rank * length).astype(jnp.int32).reshape(1)
    taps = tuple(part.astype(F32) for part in (conv_query, conv_key, conv_value))
    gain = head_gain.reshape(1, size)

    scale_one = row_norm(hidden)
    normed = (hidden * scale_one * norm_gain).astype(BF16)
    w_wide = w_output.astype(F32)
    w_across = swap(w_wide, "head", 2)
    lins = tuple(matmul(normed, part) for part in (w_query, w_key, w_value))
    tails = jnp.concatenate([part[-EDGE:] for part in lins], axis=1)
    edge = shift(tails, "seq", 1)
    rates = jax.nn.sigmoid(matmul(normed, w_strength) + strength_bias)
    inverse, effective, local, memories, last = delta_forward(
        doc_starts, base, lins, edge, taps, rates, heads, size
    )
    transfer, offset = last[:, :, :size], last[:, :, size:]
    entering = chain(transfer, offset, 1)
    mixed_rows, headed_wide, headed = delta_output(effective, local, entering, gain)
    h_across = swap(headed_wide, "head", 2)
    h_core = swap(headed_wide, "head", 1)
    w_late, w_across = after((w_wide, w_across), headed)
    w_near = rounded_above(w_late, swap(w_late, "head", 1))
    w_distant = rounded_above(w_across, swap(w_across, "head", 1))
    middle = hidden + matmul(rounded_beside(headed_wide, h_core), w_near)
    ffn_cot = after(out_grad, headed).astype(BF16)
    cot_ordered = arranged(ffn_cot, relative_places())
    h_across = after(h_across, middle, w_distant, cot_ordered)
    h_far = swap(h_across, "head", 1)
    middle = middle + matmul(rounded_beside(h_across, h_far), w_distant)
    scale_two = row_norm(middle)
    normed_two = (middle * scale_two * ffn_gain).astype(BF16)
    gate_rows = matmul(normed_two, w_gate)
    upward = matmul(normed_two, w_up)
    sigma = jax.nn.sigmoid(gate_rows)
    silu_gate = gate_rows * sigma
    active = (silu_gate * upward).astype(BF16)
    half = ffn_cot.shape[1] // 2
    split = active.shape[1] // 128 * 3 // 4 * 128
    lead, rest = active[:, :split], active[:, split:]
    lead_given = product(cot_ordered[:, :half], lead, False)
    ffn_cot = after(ffn_cot, lead_given)
    active_grad = matmul(ffn_cot, w_down, 1, 1)
    gate_cot = (active_grad * upward * sigma * (1.0 + gate_rows * (1.0 - sigma))).astype(BF16)
    up_cot = (active_grad * silu_gate).astype(BF16)
    both_term = matmul(normed_two, jnp.concatenate([gate_cot, up_cot], axis=1), 0, 0)
    both_grad = lax.psum_scatter(both_term, "seq", scatter_dimension=0, tiled=True)
    gate_late, up_late = after((gate_cot, up_cot), both_term)
    two_part = matmul(gate_late, w_gate, 1, 1) + matmul(up_late, w_up, 1, 1)
    two_begun = begun_over_head(two_part)
    ffn_begun = begun_over_head(matmul(after(active, two_begun), w_down))
    cot_ordered = after(cot_ordered, two_begun)
    lead_kept = product(cot_ordered[:, half:], lead, False)
    rest_given = product(cot_ordered[:, :half], rest, False)
    rest_kept = product(cot_ordered[:, half:], rest, False)
    middle_grad, branch_cot, ffn_gain_part = norm_pulled(
        ended_over_head(
            two_begun, ffn_begun, lead_kept, rest_given, rest_kept
        ),
        middle,
        ffn_gain,
        out_grad,
    )
    headed_grad = matmul(branch_cot, w_output, 1, 1)
    mixed_grad, head_gain_part, local_grad = norm_back(
        headed_grad, mixed_rows, effective, gain, heads, size
    )
    leaving = chain(transfer, local_grad, -1, True)
    lead_given, lead_kept = received(lead_given, lead_kept, 1, 0)
    lead_given = after(lead_given, leaving)
    leaving = after(leaving, lead_given)
    back = delta_backward(
        doc_starts, base, lins, edge, taps, rates, inverse, memories, entering, leaving, mixed_grad
    )
    ffn_halves = ended_over_head(ffn_begun)
    lead_given, lead_kept = received(lead_given, lead_kept, 1, 1)
    returned, logit_grad = after(
        (shift(back[3], "seq", -1), back[4]), lead_given, ffn_halves[0]
    )
    branch_ordered = arranged(after(branch_cot, back[3]), relative_places())
    mix_given = jnp.concatenate(
        [rest_given, product(branch_ordered[:, :half], headed, False)], axis=0
    )
    mix_given = after(mix_given, returned)
    cots = tuple(
        jnp.concatenate(
            [part[:-EDGE], part[-EDGE:] + returned[:, index * width : (index + 1) * width]], axis=0
        ).astype(BF16)
        for index, part in enumerate(back[:3])
    )
    strength_cot = logit_grad.astype(BF16)
    cot = after(jnp.concatenate(cots, axis=1), lead_given)
    lin_term = product(normed, cot, True)
    lin_grad = lax.psum_scatter(lin_term, "seq", scatter_dimension=0, tiled=True)
    mix_kept = jnp.concatenate(
        [rest_kept, product(branch_ordered[:, half:], headed, False)], axis=0
    )
    mix_given, mix_kept = received(mix_given, after(mix_kept, lin_term), 1, 0)
    late_cots, strength_cot = after((cots, strength_cot), lin_term, mix_given)
    first_part = matmul(late_cots[0], w_query, 1, 1)
    first_part = first_part + matmul(late_cots[1], w_key, 1, 1)
    first_part = first_part + matmul(late_cots[2], w_value, 1, 1)
    first_part = first_part + matmul(strength_cot, w_strength, 1, 1)
    norm_gain_part = jnp.sum(first_part * hidden * scale_one, axis=0)
    shared = summed_everywhere(
        jnp.concatenate([norm_gain_part, head_gain_part.reshape(-1)]), "head"
    )
    first_begun = after(begun_over_head(first_part), shared)
    lead_kept = finished(lead_given, lead_kept, 1, 2)
    mix_given, mix_kept = received(mix_given, after(mix_kept, first_begun), 1, 1)
    first_halves = ended_over_head(first_begun, mix_given, lead_kept, both_grad)
    hidden_grad = norm_pulled(first_halves, hidden, norm_gain, middle_grad)[0]
    block_output = middle + whole_rows(*ffn_halves)
    mix_kept = finished(mix_given, after(mix_kept, hidden_grad, block_output), 1, 2)
    hidden_units = gate_cot.shape[1]
    w_gate_grad, w_up_grad = both_grad[:, :hidden_units], both_grad[:, hidden_units:]
    lin_grad = after(lin_grad, hidden_grad, block_output, w_gate_grad, w_up_grad, mix_kept)
    lin_grads = tuple(lin_grad[:, index * width : (index + 1) * width] for index in range(3))
    rest_rows = rest.shape[1]
    w_down_grad = jnp.concatenate([lead_kept, mix_kept[:rest_rows]], axis=0)
    w_output_grad = mix_kept[rest_rows:]
    strength_term = matmul(strength_cot, normed, 0, 0)

    small = jnp.concatenate(
        [
            shared,
            strength_term.reshape(-1),
            ffn_gain_part.reshape(-1),
        ]
        + [part.reshape(-1) for part in back[5:8]]
        + [jnp.sum(logit_grad, axis=0)]
    )
    small = summed_everywhere(small, "seq")
    features = norm_gain.shape[0]
    block = features // seq_count
    cut = [features, size, heads * features, features] + [4 * width] * 3 + [heads]
    parts, at = [], 0
    for extent in cut:
        parts.append(small[at : at + extent])
        at += extent

    def own(vector, axis=0):
        return lax.dynamic_slice_in_dim(vector, seq_rank * block, block, axis)

    return (
        block_output,
        hidden_grad,
        own(parts[0]),
        lin_grads[0],
        lin_grads[1],
        lin_grads[2],
        own(parts[2].reshape(heads, features), 1).T,
        parts[7],
        parts[4].reshape(4, width),
        parts[5].reshape(4, width),
        parts[6].reshape(4, width),
        parts[1],
        w_output_grad,
        own(parts[3]),
        w_gate_grad,
        w_up_grad,
        w_down_grad,
    )


def solution(mesh):
    return jax.shard_map(
        shards,
        mesh=mesh,
        in_specs=(
            P("seq", None),
            P(),
            P(),
            P(None, "head"),
            P(None, "head"),
            P(None, "head"),
            P(None, "head"),
            P("head"),
            P(None, "head"),
            P(None, "head"),
            P(None, "head"),
            P(),
            P("head", None),
            P(),
            P(None, "head"),
            P(None, "head"),
            P("head", None),
            P("seq", None),
        ),
        out_specs=(
            P("seq", None),
            P("seq", None),
            P("seq"),
            P("seq", "head"),
            P("seq", "head"),
            P("seq", "head"),
            P("seq", "head"),
            P("head"),
            P(None, "head"),
            P(None, "head"),
            P(None, "head"),
            P(),
            P("head", "seq"),
            P("seq"),
            P("seq", "head"),
            P("seq", "head"),
            P("head", "seq"),
        ),
        check_vma=False,
    )
```

```python
import jax
import jax.numpy as jnp
from jax import lax
from jax.experimental import pallas as pl
from jax.experimental.pallas import tpu as pltpu
from jax.sharding import PartitionSpec as P

BLOCK = 128
SUB = 32
EDGE = 8
F32 = jnp.float32
BF16 = jnp.bfloat16


def mm(left, right, left_dim=1, right_dim=0, passes=3):
    dims = (((left_dim,), (right_dim,)), ((), ()))
    if passes == 1:
        return lax.dot_general(
            left.astype(BF16), right.astype(BF16), dims, preferred_element_type=F32
        )
    precision = lax.Precision.HIGH if passes == 3 else lax.Precision.HIGHEST
    return lax.dot_general(left, right, dims, precision=precision, preferred_element_type=F32)


def doc_of(places, starts, count):
    total = jnp.full(places.shape, -1, jnp.int32) if places.shape else jnp.int32(-1)
    for index in range(count):
        total = total + jnp.where(starts[index] <= places, 1, 0).astype(jnp.int32)
    return total


def sigmoid(value):
    return 1.0 / (1.0 + jnp.exp(-value))


def block_masks(first, starts, count):
    rows = lax.broadcasted_iota(jnp.int32, (BLOCK, BLOCK), 0)
    columns = lax.broadcasted_iota(jnp.int32, (BLOCK, BLOCK), 1)
    row_docs = doc_of(first + rows, starts, count)
    column_docs = doc_of(first + columns, starts, count)
    same = row_docs == column_docs
    prior_doc = doc_of(first - 1, starts, count)
    last_doc = doc_of(first + BLOCK - 1, starts, count)
    carried = (row_docs == prior_doc).astype(F32)
    final = (row_docs == last_doc).astype(F32)
    through = jnp.where(prior_doc == last_doc, 1.0, 0.0).astype(F32)
    reach = [None]
    for back in range(1, 4):
        reach.append((row_docs == doc_of(first - back + rows, starts, count)).astype(F32))
    return rows, columns, same, carried, final, through, reach


def short_conv(joined, taps, reach):
    total = taps[3:4] * joined[EDGE:]
    for back in range(1, 4):
        total = total + taps[3 - back : 4 - back] * (
            joined[EDGE - back : EDGE - back + BLOCK] * reach[back]
        )
    return total


def block_inverses(stricts, rows, columns, passes=3):
    near_mask = rows // SUB == columns // SUB
    eye = jnp.where(rows == columns, 1.0, 0.0)
    nears = [jnp.where(near_mask, strict, 0.0) for strict in stricts]
    fars = [strict - near for strict, near in zip(stricts, nears)]
    inverses = [eye - near for near in nears]
    powers = [mm(near, near, passes=passes) for near in nears]
    covered = 2
    while covered * 2 < SUB:
        both = [
            mm(jnp.concatenate([power, inverse], axis=0), power, passes=passes)
            for power, inverse in zip(powers, inverses)
        ]
        powers = [part[:BLOCK] for part in both]
        inverses = [inverse + part[BLOCK:] for inverse, part in zip(inverses, both)]
        covered *= 2
    inverses = [
        inverse + mm(inverse, power, passes=passes) for inverse, power in zip(inverses, powers)
    ]
    chains = [mm(inverse, far, passes=passes) for inverse, far in zip(inverses, fars)]
    both = [
        mm(link, jnp.concatenate([inverse, link], axis=1), passes=passes)
        for link, inverse in zip(chains, inverses)
    ]
    partials = [inverse - part[:, :BLOCK] for inverse, part in zip(inverses, both)]
    return [
        partial + mm(part[:, BLOCK:], partial, passes=passes)
        for partial, part in zip(partials, both)
    ]


def forward_kernel(
    starts,
    base,
    lin_query,
    lin_key,
    lin_value,
    edge,
    taps_query,
    taps_key,
    taps_value,
    rates,
    inverse_out,
    effective_out,
    local_out,
    memory_out,
    final_out,
    before,
    memory,
):
    heads, size = memory.shape[0], memory.shape[1]
    width = heads * size
    step = pl.program_id(0)
    count = starts.shape[0]

    @pl.when(step == 0)
    def _():
        before[...] = edge[...]
        line = lax.broadcasted_iota(jnp.int32, (size, 2 * size), 0)
        lane = lax.broadcasted_iota(jnp.int32, (size, 2 * size), 1)
        start = jnp.where(line == lane, 1.0, 0.0).astype(F32)
        for head in range(heads):
            memory[head] = start

    first = base[0] + step * BLOCK
    rows, columns, same, carried, final, through, reach = block_masks(first, starts, count)
    below = jnp.logical_and(same, columns < rows)
    upto = jnp.logical_and(same, columns <= rows)
    queries, keys, values, stricts, scores, rate_list = [], [], [], [], [], []
    for head in range(heads):
        span = slice(head * size, (head + 1) * size)
        pieces = []
        for number, (lin, taps) in enumerate(
            ((lin_query, taps_query), (lin_key, taps_key), (lin_value, taps_value))
        ):
            place = slice(number * width + head * size, number * width + (head + 1) * size)
            joined = jnp.concatenate([before[:, place], lin[:, span]], axis=0)
            conv = short_conv(joined, taps[:, span], reach)
            pieces.append(conv * sigmoid(conv))
        query = pieces[0] * lax.rsqrt(jnp.sum(pieces[0] * pieces[0], axis=1, keepdims=True) + 1e-6)
        key = pieces[1] * lax.rsqrt(jnp.sum(pieces[1] * pieces[1], axis=1, keepdims=True) + 1e-6)
        queries.append(query)
        keys.append(key)
        values.append(pieces[2])
        rate_list.append(jnp.broadcast_to(rates[:, head : head + 1], (BLOCK, size)))
    for number, lin in enumerate((lin_query, lin_key, lin_value)):
        before[:, number * width : (number + 1) * width] = lin[BLOCK - EDGE :, :]
    for head in range(heads):
        products = mm(jnp.concatenate([queries[head], keys[head]], axis=0), keys[head], 1, 1)
        scores.append(jnp.where(upto, products[:BLOCK], 0.0))
        stricts.append(jnp.where(below, products[BLOCK:] * rate_list[head], 0.0))
    inverses = block_inverses(stricts, rows, columns)
    for head in range(heads):
        inverse_out[0, head] = inverses[head]
    writes = [
        mm(
            inverses[head],
            jnp.concatenate(
                [rate_list[head] * carried * keys[head], rate_list[head] * values[head]], axis=1
            )
        )
        for head in range(heads)
    ]
    helds = [memory[head] for head in range(heads)]
    for head in range(heads):
        memory_out[0, head] = helds[head]
    reads = [
        mm(
            jnp.concatenate([writes[head][:, :size], carried * queries[head]], axis=0),
            helds[head]
        )
        for head in range(heads)
    ]
    residues = [
        jnp.concatenate(
            [-reads[head][:BLOCK, :size], writes[head][:, size:] - reads[head][:BLOCK, size:]],
            axis=1,
        )
        for head in range(heads)
    ]
    updates = [
        through * helds[head] + mm(final * keys[head], residues[head], 0, 0)
        for head in range(heads)
    ]
    for head in range(heads):
        memory[head] = updates[head]
        final_out[head] = updates[head]
    for head in range(heads):
        span = slice(head * size, (head + 1) * size)
        result = reads[head][BLOCK:] + mm(scores[head], residues[head])
        effective_out[:, span] = result[:, :size]
        local_out[:, span] = result[:, size:]


def output_kernel(effective, local, entering, gain, mixed_out, headed_out, rounded_out):
    heads, size = entering.shape[0], entering.shape[1]
    for head in range(heads):
        span = slice(head * size, (head + 1) * size)
        mixed = local[:, span] + mm(effective[:, span], entering[head])
        mixed_out[:, span] = mixed
        scale = lax.rsqrt(jnp.mean(mixed * mixed, axis=1, keepdims=True) + 1e-5)
        headed = mixed * scale * gain[...]
        headed_out[:, span] = headed
        rounded_out[:, span] = headed.astype(rounded_out.dtype)


def norm_back_kernel(headed_grad, mixed_rows, effective, gain, grad_out, gain_out, local_out):
    heads, size = local_out.shape[0], local_out.shape[1]
    step = pl.program_id(0)

    @pl.when(step == 0)
    def _():
        gain_out[...] = jnp.zeros_like(gain_out)
        local_out[...] = jnp.zeros_like(local_out)

    for head in range(heads):
        span = slice(head * size, (head + 1) * size)
        mixed = mixed_rows[:, span]
        scale = lax.rsqrt(jnp.mean(mixed * mixed, axis=1, keepdims=True) + 1e-5)
        given = headed_grad[:, span]
        gain_out[...] += jnp.sum(given * mixed * scale, axis=0, keepdims=True)
        scaled = gain[...] * given
        along = jnp.mean(mixed * scaled, axis=1, keepdims=True)
        grad = scale * scaled - mixed * (scale * scale * scale * along)
        grad_out[:, span] = grad
        local_out[head] += mm(effective[:, span], grad, 0, 0)


def backward_kernel(
    starts,
    base,
    lin_query,
    lin_key,
    lin_value,
    prior_query,
    prior_key,
    prior_value,
    edge,
    taps_query,
    taps_key,
    taps_value,
    rates,
    inverse_in,
    memory_in,
    entering,
    leaving,
    mixed_grad,
    query_out,
    key_out,
    value_out,
    edge_out,
    logit_out,
    taps_query_out,
    taps_key_out,
    taps_value_out,
    after,
    memory_grad,
):
    heads, size = entering.shape[0], entering.shape[1]
    width = heads * size
    step = pl.program_id(0)
    blocks = pl.num_programs(0)
    here = blocks - 1 - step
    count = starts.shape[0]
    every = range(heads)
    spans = [slice(head * size, (head + 1) * size) for head in every]

    @pl.when(step == 0)
    def _():
        after[...] = jnp.zeros_like(after)
        memory_grad[...] = leaving[...]
        taps_query_out[...] = jnp.zeros_like(taps_query_out)
        taps_key_out[...] = jnp.zeros_like(taps_key_out)
        taps_value_out[...] = jnp.zeros_like(taps_value_out)

    first = base[0] + here * BLOCK
    rows, columns, same, carried, final, through, reach = block_masks(first, starts, count)
    below = jnp.logical_and(same, columns < rows)
    upto = jnp.logical_and(same, columns <= rows)

    def convolved(number, lin, prior, taps, head):
        place = slice(number * width + head * size, number * width + (head + 1) * size)
        border = jnp.where(here == 0, edge[:, place], prior[:, spans[head]])
        joined = jnp.concatenate([border, lin[:, spans[head]]], axis=0)
        conv = short_conv(joined, taps[:, spans[head]], reach)
        return joined, conv, sigmoid(conv)

    def unit_scale(piece):
        return lax.rsqrt(jnp.sum(piece * piece, axis=1, keepdims=True) + 1e-6)

    query_parts = [convolved(0, lin_query, prior_query, taps_query, head) for head in every]
    key_parts = [convolved(1, lin_key, prior_key, taps_key, head) for head in every]
    value_parts = [convolved(2, lin_value, prior_value, taps_value, head) for head in every]
    query_scales = [unit_scale(conv * gate) for _, conv, gate in query_parts]
    key_scales = [unit_scale(conv * gate) for _, conv, gate in key_parts]
    queries = [conv * gate * scale for (_, conv, gate), scale in zip(query_parts, query_scales)]
    keys = [conv * gate * scale for (_, conv, gate), scale in zip(key_parts, key_scales)]
    values = [conv * gate for _, conv, gate in value_parts]
    rate_columns = [rates[:, head : head + 1] for head in every]
    rate_wide = [jnp.broadcast_to(column, (BLOCK, size)) for column in rate_columns]
    products = [
        mm(jnp.concatenate([queries[head], keys[head]], axis=0), keys[head], 1, 1)
        for head in every
    ]
    scores = [jnp.where(upto, part[:BLOCK], 0.0) for part in products]
    grams = [part[BLOCK:] for part in products]
    inverses = [inverse_in[0, head] for head in every]
    memories = [
        mm(memory_in[0, head][:, :size], entering[head]) + memory_in[0, head][:, size:]
        for head in every
    ]
    lefts = [carried * key for key in keys]
    wanted = [values[head] - mm(lefts[head], memories[head]) for head in every]
    residues = [mm(inverses[head], rate_wide[head] * wanted[head]) for head in every]
    given = [mixed_grad[:, span] for span in spans]
    score_sides = [mm(scores[head], given[head], 0, 0) for head in every]
    state_grads = [memory_grad[head] for head in every]
    last_keys = [final * key for key in keys]
    residue_grads = [
        score_sides[head] + mm(last_keys[head], state_grads[head]) for head in every
    ]
    solved_grads = [mm(inverses[head], residue_grads[head], 0, 0) for head in every]
    wanted_grads = [rate_wide[head] * solved_grads[head] for head in every]
    updates = [
        through * state_grads[head]
        + mm(
            jnp.concatenate([carried * queries[head], -lefts[head]], axis=0),
            jnp.concatenate([given[head], wanted_grads[head]], axis=0),
            0,
            0,
        )
        for head in every
    ]
    for head in every:
        memory_grad[head] = updates[head]
    outers = [
        mm(jnp.concatenate([given[head], solved_grads[head]], axis=0), residues[head], 1, 1)
        for head in every
    ]
    state_sides = [
        mm(jnp.concatenate([given[head], wanted_grads[head]], axis=0), memories[head], 1, 1)
        for head in every
    ]
    final_sides = [final * mm(residues[head], state_grads[head], 1, 1) for head in every]
    score_grads = [jnp.where(upto, part[:BLOCK], 0.0) for part in outers]
    strict_grads = [jnp.where(below, -part[BLOCK:], 0.0) for part in outers]
    gram_grads = [rate_wide[head] * strict_grads[head] for head in every]
    pairs = [
        jnp.concatenate([score_grads[head], gram_grads[head]], axis=0) for head in every
    ]
    key_sides = [mm(pairs[head], keys[head]) for head in every]
    turned_sides = [
        mm(pairs[head], jnp.concatenate([queries[head], keys[head]], axis=0), 0, 0)
        for head in every
    ]
    rate_grads = [
        jnp.sum(
            solved_grads[head] * wanted[head] + strict_grads[head] * grams[head],
            axis=1,
            keepdims=True,
        )
        for head in every
    ]
    lanes = lax.broadcasted_iota(jnp.int32, (BLOCK, rates.shape[1]), 1)
    logit_grad = jnp.zeros((BLOCK, rates.shape[1]), F32)
    for head in every:
        column = rate_columns[head]
        logit_grad = jnp.where(
            lanes == head, rate_grads[head] * column * (1.0 - column), logit_grad
        )
    logit_out[...] = logit_grad
    query_grads = [
        carried * state_sides[head][:BLOCK] + key_sides[head][:BLOCK] for head in every
    ]
    key_grads = [
        key_sides[head][BLOCK:]
        - carried * state_sides[head][BLOCK:]
        + turned_sides[head]
        + final_sides[head]
        for head in every
    ]
    query_grads = [
        scale * (grad - query * jnp.sum(query * grad, axis=1, keepdims=True))
        for scale, grad, query in zip(query_scales, query_grads, queries)
    ]
    key_grads = [
        scale * (grad - key * jnp.sum(key * grad, axis=1, keepdims=True))
        for scale, grad, key in zip(key_scales, key_grads, keys)
    ]
    spare = jnp.zeros((EDGE, size), F32)
    for number, (grads, parts, taps, lin_out, taps_out) in enumerate(
        (
            (query_grads, query_parts, taps_query, query_out, taps_query_out),
            (key_grads, key_parts, taps_key, key_out, taps_key_out),
            (wanted_grads, value_parts, taps_value, value_out, taps_value_out),
        )
    ):
        for head in every:
            span = spans[head]
            place = slice(number * width + head * size, number * width + (head + 1) * size)
            joined, conv, gate = parts[head]
            conv_grad = grads[head] * gate * (1.0 + conv * (1.0 - gate))
            lin_grad = taps[3:4, span] * conv_grad
            tail = spare
            taps_grad = [jnp.sum(conv_grad * joined[EDGE:], axis=0, keepdims=True)]
            for back in range(1, 4):
                part = conv_grad * reach[back]
                tap = taps[3 - back : 4 - back, span]
                lin_grad = lin_grad + tap * jnp.concatenate([part, spare], axis=0)[
                    back : back + BLOCK
                ]
                tail = tail + tap * jnp.concatenate([spare, part[:EDGE]], axis=0)[
                    back : back + EDGE
                ]
                taps_grad.append(
                    jnp.sum(part * joined[EDGE - back : EDGE - back + BLOCK], axis=0, keepdims=True)
                )
            taps_out[:, span] += jnp.concatenate(taps_grad[::-1], axis=0)
            lin_out[: BLOCK - EDGE, span] = lin_grad[: BLOCK - EDGE]
            lin_out[BLOCK - EDGE :, span] = lin_grad[BLOCK - EDGE :] + after[:, place]
            after[:, place] = tail
            edge_out[:, place] = tail


def on_chip(kernel, name, **settings):
    return pl.pallas_call(
        kernel,
        name=name,
        cost_estimate=pl.CostEstimate(flops=1, bytes_accessed=1, transcendentals=0),
        compiler_params=pltpu.CompilerParams(
            dimension_semantics=("arbitrary",), vmem_limit_bytes=48 * 1024 * 1024
        ),
        **settings,
    )


def whole(shape):
    return pl.BlockSpec(shape, lambda i: (0,) * len(shape))


def scalars():
    return pl.BlockSpec(memory_space=pltpu.SMEM)


def delta_forward(starts, base, lins, edge, taps, rates, heads, size):
    length, width = lins[0].shape
    blocks = length // BLOCK
    row_block = pl.BlockSpec((BLOCK, width), lambda i: (i, 0))
    return on_chip(
        forward_kernel,
        "delta_forward",
        grid=(blocks,),
        in_specs=[scalars(), scalars()]
        + [row_block] * 3
        + [whole((EDGE, 3 * width))]
        + [whole((4, width))] * 3
        + [pl.BlockSpec((BLOCK, heads), lambda i: (i, 0))],
        out_specs=[
            pl.BlockSpec((1, heads, BLOCK, BLOCK), lambda i: (i, 0, 0, 0)),
            row_block,
            row_block,
            pl.BlockSpec((1, heads, size, 2 * size), lambda i: (i, 0, 0, 0)),
            whole((heads, size, 2 * size)),
        ],
        out_shape=[
            jax.ShapeDtypeStruct((blocks, heads, BLOCK, BLOCK), F32),
            jax.ShapeDtypeStruct((length, width), F32),
            jax.ShapeDtypeStruct((length, width), F32),
            jax.ShapeDtypeStruct((blocks, heads, size, 2 * size), F32),
            jax.ShapeDtypeStruct((heads, size, 2 * size), F32),
        ],
        scratch_shapes=[
            pltpu.VMEM((EDGE, 3 * width), F32),
            pltpu.VMEM((heads, size, 2 * size), F32),
        ],
    )(starts, base, *lins, edge, *taps, rates)


def delta_output(effective, local, entering, gain):
    length, width = local.shape
    heads, size = entering.shape[0], entering.shape[1]
    rows = min(length, 256)
    row_block = pl.BlockSpec((rows, width), lambda i: (i, 0))
    return on_chip(
        output_kernel,
        "delta_output",
        grid=(length // rows,),
        in_specs=[row_block, row_block, whole((heads, size, size)), whole((1, size))],
        out_specs=[row_block, row_block, row_block],
        out_shape=[
            jax.ShapeDtypeStruct((length, width), F32),
            jax.ShapeDtypeStruct((length, width), F32),
            jax.ShapeDtypeStruct((length, width), BF16),
        ],
    )(effective, local, entering, gain)


def norm_back(headed_grad, mixed_rows, effective, gain, heads, size):
    length, width = headed_grad.shape
    rows = min(length, 256)
    row_block = pl.BlockSpec((rows, width), lambda i: (i, 0))
    return on_chip(
        norm_back_kernel,
        "norm_back",
        grid=(length // rows,),
        in_specs=[row_block, row_block, row_block, whole((1, size))],
        out_specs=[row_block, whole((1, size)), whole((heads, size, size))],
        out_shape=[
            jax.ShapeDtypeStruct((length, width), F32),
            jax.ShapeDtypeStruct((1, size), F32),
            jax.ShapeDtypeStruct((heads, size, size), F32),
        ],
    )(headed_grad, mixed_rows, effective, gain)


def norm_pull_kernel(odd, part, other, values, gain, given, grad_out, rounded_out, gain_out):
    step = pl.program_id(0)
    second = step * 2 // pl.num_programs(0)

    @pl.when(step == 0)
    def _():
        gain_out[...] = jnp.zeros_like(gain_out)

    grad = jnp.where(second == odd[0], part[...], other[...])
    value = values[...]
    scale = lax.rsqrt(jnp.mean(value * value, axis=1, keepdims=True) + 1e-5)
    gain_out[...] += jnp.sum(grad * value * scale, axis=0, keepdims=True)
    scaled = gain[...] * grad
    along = jnp.mean(value * scaled, axis=1, keepdims=True)
    result = given[...] + (scale * scaled - value * (scale * scale * scale * along))
    grad_out[...] = result
    rounded_out[...] = result.astype(rounded_out.dtype)


def norm_pulled(halves, values, gain, given):
    length, width = values.shape
    rows = length // 8
    odd = (lax.axis_index("head") % 2).astype(jnp.int32).reshape(1)
    row_block = pl.BlockSpec((rows, width), lambda i: (i, 0))
    half_block = pl.BlockSpec((rows, width), lambda i: (i % 4, 0))
    return on_chip(
        norm_pull_kernel,
        "norm_pull",
        grid=(8,),
        in_specs=[scalars(), half_block, half_block, row_block, whole((1, width)), row_block],
        out_specs=[row_block, row_block, whole((1, width))],
        out_shape=[
            jax.ShapeDtypeStruct((length, width), F32),
            jax.ShapeDtypeStruct((length, width), BF16),
            jax.ShapeDtypeStruct((1, width), F32),
        ],
    )(odd, *halves, values, gain.reshape(1, width), given)


def beside_kernel(first, second, out):
    width = first.shape[1]
    out[:, :width] = first[...].astype(out.dtype)
    out[:, width:] = second[...].astype(out.dtype)


def above_kernel(first, second, out):
    rows = first.shape[0]
    out[:rows] = first[...].astype(out.dtype)
    out[rows:] = second[...].astype(out.dtype)


def rounded_beside(first, second):
    length, width = first.shape
    rows = min(length, 256)
    block = pl.BlockSpec((rows, width), lambda i: (i, 0))
    return on_chip(
        beside_kernel,
        "rounded_beside",
        grid=(length // rows,),
        in_specs=[block, block],
        out_specs=pl.BlockSpec((rows, 2 * width), lambda i: (i, 0)),
        out_shape=jax.ShapeDtypeStruct((length, 2 * width), BF16),
    )(first, second)


def rounded_above(first, second):
    rows, width = first.shape
    columns = min(width, 256)
    block = pl.BlockSpec((rows, columns), lambda i: (0, i))
    return on_chip(
        above_kernel,
        "rounded_above",
        grid=(width // columns,),
        in_specs=[block, block],
        out_specs=pl.BlockSpec((2 * rows, columns), lambda i: (0, i)),
        out_shape=jax.ShapeDtypeStruct((2 * rows, width), BF16),
    )(first, second)


def delta_backward(
    starts, base, lins, edge, taps, rates, inverse, memories, entering, leaving, mixed_grad
):
    length, width = lins[0].shape
    heads, size = entering.shape[0], entering.shape[1]
    blocks = length // BLOCK
    ratio = BLOCK // EDGE
    row_block = pl.BlockSpec((BLOCK, width), lambda i: (blocks - 1 - i, 0))
    prior = pl.BlockSpec(
        (EDGE, width), lambda i: (jnp.maximum((blocks - 1 - i) * ratio - 1, 0), 0)
    )
    rate_block = pl.BlockSpec((BLOCK, heads), lambda i: (blocks - 1 - i, 0))
    return on_chip(
        backward_kernel,
        "delta_backward",
        grid=(blocks,),
        in_specs=[scalars(), scalars()]
        + [row_block] * 3
        + [prior] * 3
        + [whole((EDGE, 3 * width))]
        + [whole((4, width))] * 3
        + [
            rate_block,
            pl.BlockSpec((1, heads, BLOCK, BLOCK), lambda i: (blocks - 1 - i, 0, 0, 0)),
            pl.BlockSpec((1, heads, size, 2 * size), lambda i: (blocks - 1 - i, 0, 0, 0)),
            whole((heads, size, size)),
            whole((heads, size, size)),
            row_block,
        ],
        out_specs=[row_block] * 3
        + [whole((EDGE, 3 * width)), rate_block]
        + [whole((4, width))] * 3,
        out_shape=[jax.ShapeDtypeStruct((length, width), F32)] * 3
        + [
            jax.ShapeDtypeStruct((EDGE, 3 * width), F32),
            jax.ShapeDtypeStruct((length, heads), F32),
        ]
        + [jax.ShapeDtypeStruct((4, width), F32)] * 3,
        scratch_shapes=[
            pltpu.VMEM((EDGE, 3 * width), F32),
            pltpu.VMEM((heads, size, size), F32),
        ],
    )(starts, base, *lins, *lins, edge, *taps, rates, inverse, memories, entering, leaving, mixed_grad)


def swap(block, axis, bit):
    count = lax.axis_size(axis)
    return lax.ppermute(block, axis, [(i, i ^ bit) for i in range(count)])


def shift(block, axis, distance):
    devices = range(lax.axis_size(axis))
    route = [(i - distance, i) for i in devices if i - distance in devices]
    return lax.ppermute(block, axis, route)


def begun_over_head(term):
    odd = lax.axis_index("head") % 2
    half = term.shape[0] // 2
    keep = lax.dynamic_slice_in_dim(term, odd * half, half, 0)
    send = lax.dynamic_slice_in_dim(term, (1 - odd) * half, half, 0)
    return keep + swap(send, "head", 1)


def ended_over_head(part, *gates):
    part = part + after(swap(part, "head", 2), *gates)
    return part, swap(part, "head", 1)


def whole_rows(part, other):
    return jnp.where(
        lax.axis_index("head") % 2 == 0,
        jnp.concatenate([part, other], axis=0),
        jnp.concatenate([other, part], axis=0),
    )


def after(value, *others):
    return lax.optimization_barrier((value,) + others)[0] if others else value


def summed_everywhere(vector, axis):
    count = lax.axis_size(axis)
    bit = 1
    while bit < count:
        vector = vector + swap(vector, axis, bit)
        bit *= 2
    return vector


def relative_order(bits):
    if not bits:
        return [0]
    rest = relative_order(bits[1:])
    return [index ^ bits[0] for index in rest] + rest


def seq_bits():
    bits = []
    while 1 << len(bits) < lax.axis_size("seq"):
        bits.append(1 << len(bits))
    return bits


def arrange_kernel(places, rows, out):
    out[...] = rows[...]


def arranged(rows, places):
    length, size = rows.shape[0], rows.shape[1] // lax.axis_size("seq")
    if size % 128:
        return jnp.concatenate(
            [lax.dynamic_slice_in_dim(rows, place * size, size, 1) for place in places], axis=1
        )
    return pl.pallas_call(
        arrange_kernel,
        name="arrange",
        cost_estimate=pl.CostEstimate(flops=1, bytes_accessed=1, transcendentals=0),
        grid_spec=pltpu.PrefetchScalarGridSpec(
            num_scalar_prefetch=1,
            grid=(len(places),),
            in_specs=[pl.BlockSpec((length, size), lambda i, places: (0, places[i]))],
            out_specs=pl.BlockSpec((length, size), lambda i, places: (0, i)),
        ),
        out_shape=jax.ShapeDtypeStruct(rows.shape, rows.dtype),
        compiler_params=pltpu.CompilerParams(dimension_semantics=("arbitrary",)),
    )(jnp.stack(places).astype(jnp.int32), rows)


def relative_places():
    here = lax.axis_index("seq")
    return [here ^ index for index in relative_order(seq_bits())]


def product(rows, others, rows_first):
    return matmul(rows, others, 0, 0) if rows_first else matmul(others, rows, 0, 0)


def received(given, kept, axis, place):
    bits = seq_bits()
    kept = kept + swap(given, "seq", bits[place])
    if place + 1 == len(bits):
        return None, kept
    size = kept.shape[axis] // 2
    return lax.slice_in_dim(kept, 0, size, axis=axis), lax.slice_in_dim(
        kept, size, 2 * size, axis=axis
    )


def finished(given, kept, axis, place):
    while place < len(seq_bits()):
        given, kept = received(given, kept, axis, place)
        place += 1
    return kept


def chain(transfer, offset, distance, turned=False, between=()):
    hops = max(lax.axis_size("seq") // 2, 1)
    groups = 2
    count = offset.shape[0] // groups
    picks = [slice(index * count, (index + 1) * count) for index in range(groups)]
    form = "hji,hjk->hik" if turned else "hij,hjk->hik"
    states = [shift(offset[pick], "seq", distance) for pick in picks]
    for hop in range(hops - 1):
        if hop < len(between):
            states[0] = after(states[0], between[hop])
        moved = [
            jnp.einsum(form, transfer[pick], state, precision=lax.Precision.HIGH) + offset[pick]
            for pick, state in zip(picks, states)
        ]
        states = [shift(part, "seq", distance) for part in moved]
    return jnp.concatenate(states, axis=0)


def row_norm(values):
    return lax.rsqrt(jnp.mean(values * values, axis=-1, keepdims=True) + 1e-05)


def matmul(left, right, left_dim=1, right_dim=0):
    return lax.dot_general(
        left, right, (((left_dim,), (right_dim,)), ((), ())), preferred_element_type=F32
    )


def shards(
    hidden,
    doc_starts,
    norm_gain,
    w_query,
    w_key,
    w_value,
    w_strength,
    strength_bias,
    conv_query,
    conv_key,
    conv_value,
    head_gain,
    w_output,
    ffn_gain,
    w_gate,
    w_up,
    w_down,
    out_grad,
):
    length = hidden.shape[0]
    size = head_gain.shape[0]
    heads = strength_bias.shape[0]
    width = heads * size
    seq_rank = lax.axis_index("seq")
    seq_count = lax.axis_size("seq")
    base = (seq_rank * length).astype(jnp.int32).reshape(1)
    taps = tuple(part.astype(F32) for part in (conv_query, conv_key, conv_value))
    gain = head_gain.reshape(1, size)

    scale_one = row_norm(hidden)
    normed = (hidden * scale_one * norm_gain).astype(BF16)
    w_wide = w_output.astype(F32)
    w_across = swap(w_wide, "head", 2)
    lins = tuple(matmul(normed, part) for part in (w_query, w_key, w_value))
    tails = jnp.concatenate([part[-EDGE:] for part in lins], axis=1)
    edge = shift(tails, "seq", 1)
    rates = jax.nn.sigmoid(matmul(normed, w_strength) + strength_bias)
    inverse, effective, local, memories, last = delta_forward(
        doc_starts, base, lins, edge, taps, rates, heads, size
    )
    transfer, offset = last[:, :, :size], last[:, :, size:]
    entering = chain(transfer, offset, 1)
    mixed_rows, headed_wide, headed = delta_output(effective, local, entering, gain)
    h_across = swap(headed_wide, "head", 2)
    h_core = swap(headed_wide, "head", 1)
    w_late, w_across = after((w_wide, w_across), headed)
    w_near = rounded_above(w_late, swap(w_late, "head", 1))
    w_distant = rounded_above(w_across, swap(w_across, "head", 1))
    middle = hidden + matmul(rounded_beside(headed_wide, h_core), w_near)
    ffn_cot = after(out_grad, headed).astype(BF16)
    cot_ordered = arranged(ffn_cot, relative_places())
    h_across = after(h_across, middle, w_distant, cot_ordered)
    h_far = swap(h_across, "head", 1)
    middle = middle + matmul(rounded_beside(h_across, h_far), w_distant)
    scale_two = row_norm(middle)
    normed_two = (middle * scale_two * ffn_gain).astype(BF16)
    gate_rows = matmul(normed_two, w_gate)
    upward = matmul(normed_two, w_up)
    sigma = jax.nn.sigmoid(gate_rows)
    silu_gate = gate_rows * sigma
    active = (silu_gate * upward).astype(BF16)
    half = ffn_cot.shape[1] // 2
    split = active.shape[1] // 128 * 3 // 4 * 128
    lead, rest = active[:, :split], active[:, split:]
    lead_given = product(cot_ordered[:, :half], lead, False)
    ffn_cot = after(ffn_cot, lead_given)
    active_grad = matmul(ffn_cot, w_down, 1, 1)
    gate_cot = (active_grad * upward * sigma * (1.0 + gate_rows * (1.0 - sigma))).astype(BF16)
    up_cot = (active_grad * silu_gate).astype(BF16)
    both_term = matmul(normed_two, jnp.concatenate([gate_cot, up_cot], axis=1), 0, 0)
    both_grad = lax.psum_scatter(both_term, "seq", scatter_dimension=0, tiled=True)
    gate_late, up_late = after((gate_cot, up_cot), both_term)
    two_part = matmul(gate_late, w_gate, 1, 1) + matmul(up_late, w_up, 1, 1)
    two_begun = begun_over_head(two_part)
    ffn_begun = begun_over_head(matmul(after(active, two_begun), w_down))
    cot_ordered = after(cot_ordered, two_begun)
    lead_kept = product(cot_ordered[:, half:], lead, False)
    rest_given = product(cot_ordered[:, :half], rest, False)
    rest_kept = product(cot_ordered[:, half:], rest, False)
    middle_grad, branch_cot, ffn_gain_part = norm_pulled(
        ended_over_head(
            two_begun, ffn_begun, lead_kept, rest_given, rest_kept
        ),
        middle,
        ffn_gain,
        out_grad,
    )
    headed_grad = matmul(branch_cot, w_output, 1, 1)
    mixed_grad, head_gain_part, local_grad = norm_back(
        headed_grad, mixed_rows, effective, gain, heads, size
    )
    leaving = chain(transfer, local_grad, -1, True)
    lead_given, lead_kept = received(lead_given, lead_kept, 1, 0)
    lead_given = after(lead_given, leaving)
    leaving = after(leaving, lead_given)
    back = delta_backward(
        doc_starts, base, lins, edge, taps, rates, inverse, memories, entering, leaving, mixed_grad
    )
    ffn_halves = ended_over_head(ffn_begun)
    lead_given, lead_kept = received(lead_given, lead_kept, 1, 1)
    returned, logit_grad = after(
        (shift(back[3], "seq", -1), back[4]), lead_given, ffn_halves[0]
    )
    branch_ordered = arranged(after(branch_cot, back[3]), relative_places())
    mix_given = jnp.concatenate(
        [rest_given, product(branch_ordered[:, :half], headed, False)], axis=0
    )
    mix_given = after(mix_given, returned)
    cots = tuple(
        jnp.concatenate(
            [part[:-EDGE], part[-EDGE:] + returned[:, index * width : (index + 1) * width]], axis=0
        ).astype(BF16)
        for index, part in enumerate(back[:3])
    )
    strength_cot = logit_grad.astype(BF16)
    cot = after(jnp.concatenate(cots, axis=1), lead_given)
    lin_term = product(normed, cot, True)
    lin_grad = lax.psum_scatter(lin_term, "seq", scatter_dimension=0, tiled=True)
    mix_kept = jnp.concatenate(
        [rest_kept, product(branch_ordered[:, half:], headed, False)], axis=0
    )
    mix_given, mix_kept = received(mix_given, after(mix_kept, lin_term), 1, 0)
    lead_kept = finished(lead_given, after(lead_kept, lin_term), 1, 2)
    late_cots, strength_cot = after((cots, strength_cot), lin_term, mix_given, lead_kept)
    first_part = matmul(late_cots[0], w_query, 1, 1)
    first_part = first_part + matmul(late_cots[1], w_key, 1, 1)
    first_part = first_part + matmul(late_cots[2], w_value, 1, 1)
    first_part = first_part + matmul(strength_cot, w_strength, 1, 1)
    norm_gain_part = jnp.sum(first_part * hidden * scale_one, axis=0)
    shared = summed_everywhere(
        jnp.concatenate([norm_gain_part, head_gain_part.reshape(-1)]), "head"
    )
    first_begun = after(begun_over_head(first_part), shared)
    mix_given, mix_kept = received(mix_given, after(mix_kept, first_begun), 1, 1)
    first_halves = ended_over_head(first_begun, mix_given, both_grad)
    mix_kept = finished(mix_given, after(mix_kept, first_halves[0]), 1, 2)
    first_halves = after(first_halves, mix_kept)
    hidden_grad = norm_pulled(first_halves, hidden, norm_gain, middle_grad)[0]
    block_output = middle + whole_rows(*ffn_halves)
    hidden_units = gate_cot.shape[1]
    w_gate_grad, w_up_grad = both_grad[:, :hidden_units], both_grad[:, hidden_units:]
    lin_grad = after(lin_grad, hidden_grad, block_output, w_gate_grad, w_up_grad, mix_kept)
    lin_grads = tuple(lin_grad[:, index * width : (index + 1) * width] for index in range(3))
    rest_rows = rest.shape[1]
    w_down_grad = jnp.concatenate([lead_kept, mix_kept[:rest_rows]], axis=0)
    w_output_grad = mix_kept[rest_rows:]
    strength_term = matmul(strength_cot, normed, 0, 0)

    small = jnp.concatenate(
        [
            shared,
            strength_term.reshape(-1),
            ffn_gain_part.reshape(-1),
        ]
        + [part.reshape(-1) for part in back[5:8]]
        + [jnp.sum(logit_grad, axis=0)]
    )
    small = summed_everywhere(small, "seq")
    features = norm_gain.shape[0]
    block = features // seq_count
    cut = [features, size, heads * features, features] + [4 * width] * 3 + [heads]
    parts, at = [], 0
    for extent in cut:
        parts.append(small[at : at + extent])
        at += extent

    def own(vector, axis=0):
        return lax.dynamic_slice_in_dim(vector, seq_rank * block, block, axis)

    return (
        block_output,
        hidden_grad,
        own(parts[0]),
        lin_grads[0],
        lin_grads[1],
        lin_grads[2],
        own(parts[2].reshape(heads, features), 1).T,
        parts[7],
        parts[4].reshape(4, width),
        parts[5].reshape(4, width),
        parts[6].reshape(4, width),
        parts[1],
        w_output_grad,
        own(parts[3]),
        w_gate_grad,
        w_up_grad,
        w_down_grad,
    )


def solution(mesh):
    return jax.shard_map(
        shards,
        mesh=mesh,
        in_specs=(
            P("seq", None),
            P(),
            P(),
            P(None, "head"),
            P(None, "head"),
            P(None, "head"),
            P(None, "head"),
            P("head"),
            P(None, "head"),
            P(None, "head"),
            P(None, "head"),
            P(),
            P("head", None),
            P(),
            P(None, "head"),
            P(None, "head"),
            P("head", None),
            P("seq", None),
        ),
        out_specs=(
            P("seq", None),
            P("seq", None),
            P("seq"),
            P("seq", "head"),
            P("seq", "head"),
            P("seq", "head"),
            P("seq", "head"),
            P("head"),
            P(None, "head"),
            P(None, "head"),
            P(None, "head"),
            P(),
            P("head", "seq"),
            P("seq"),
            P("seq", "head"),
            P("seq", "head"),
            P("head", "seq"),
        ),
        check_vma=False,
    )
```

```python
import jax
import jax.numpy as jnp
from jax import lax
from jax.experimental import pallas as pl
from jax.experimental.pallas import tpu as pltpu
from jax.sharding import PartitionSpec as P

BLOCK = 128
SUB = 32
EDGE = 8
F32 = jnp.float32
BF16 = jnp.bfloat16


def mm(left, right, left_dim=1, right_dim=0, passes=3):
    dims = (((left_dim,), (right_dim,)), ((), ()))
    if passes == 1:
        return lax.dot_general(
            left.astype(BF16), right.astype(BF16), dims, preferred_element_type=F32
        )
    precision = lax.Precision.HIGH if passes == 3 else lax.Precision.HIGHEST
    return lax.dot_general(left, right, dims, precision=precision, preferred_element_type=F32)


def doc_of(places, starts, count):
    total = jnp.full(places.shape, -1, jnp.int32) if places.shape else jnp.int32(-1)
    for index in range(count):
        total = total + jnp.where(starts[index] <= places, 1, 0).astype(jnp.int32)
    return total


def sigmoid(value):
    return 1.0 / (1.0 + jnp.exp(-value))


def block_masks(first, starts, count):
    rows = lax.broadcasted_iota(jnp.int32, (BLOCK, BLOCK), 0)
    columns = lax.broadcasted_iota(jnp.int32, (BLOCK, BLOCK), 1)
    row_docs = doc_of(first + rows, starts, count)
    column_docs = doc_of(first + columns, starts, count)
    same = row_docs == column_docs
    prior_doc = doc_of(first - 1, starts, count)
    last_doc = doc_of(first + BLOCK - 1, starts, count)
    carried = (row_docs == prior_doc).astype(F32)
    final = (row_docs == last_doc).astype(F32)
    through = jnp.where(prior_doc == last_doc, 1.0, 0.0).astype(F32)
    reach = [None]
    for back in range(1, 4):
        reach.append((row_docs == doc_of(first - back + rows, starts, count)).astype(F32))
    return rows, columns, same, carried, final, through, reach


def short_conv(joined, taps, reach):
    total = taps[3:4] * joined[EDGE:]
    for back in range(1, 4):
        total = total + taps[3 - back : 4 - back] * (
            joined[EDGE - back : EDGE - back + BLOCK] * reach[back]
        )
    return total


def block_inverses(stricts, rows, columns, passes=3):
    near_mask = rows // SUB == columns // SUB
    eye = jnp.where(rows == columns, 1.0, 0.0)
    nears = [jnp.where(near_mask, strict, 0.0) for strict in stricts]
    fars = [strict - near for strict, near in zip(stricts, nears)]
    inverses = [eye - near for near in nears]
    powers = [mm(near, near, passes=passes) for near in nears]
    covered = 2
    while covered * 2 < SUB:
        both = [
            mm(jnp.concatenate([power, inverse], axis=0), power, passes=passes)
            for power, inverse in zip(powers, inverses)
        ]
        powers = [part[:BLOCK] for part in both]
        inverses = [inverse + part[BLOCK:] for inverse, part in zip(inverses, both)]
        covered *= 2
    inverses = [
        inverse + mm(inverse, power, passes=passes) for inverse, power in zip(inverses, powers)
    ]
    chains = [mm(inverse, far, passes=passes) for inverse, far in zip(inverses, fars)]
    both = [
        mm(link, jnp.concatenate([inverse, link], axis=1), passes=passes)
        for link, inverse in zip(chains, inverses)
    ]
    partials = [inverse - part[:, :BLOCK] for inverse, part in zip(inverses, both)]
    return [
        partial + mm(part[:, BLOCK:], partial, passes=passes)
        for partial, part in zip(partials, both)
    ]


def forward_kernel(
    starts,
    base,
    lin_query,
    lin_key,
    lin_value,
    edge,
    taps_query,
    taps_key,
    taps_value,
    rates,
    inverse_out,
    effective_out,
    local_out,
    memory_out,
    final_out,
    before,
    memory,
):
    heads, size = memory.shape[0], memory.shape[1]
    width = heads * size
    step = pl.program_id(0)
    count = starts.shape[0]

    @pl.when(step == 0)
    def _():
        before[...] = edge[...]
        line = lax.broadcasted_iota(jnp.int32, (size, 2 * size), 0)
        lane = lax.broadcasted_iota(jnp.int32, (size, 2 * size), 1)
        start = jnp.where(line == lane, 1.0, 0.0).astype(F32)
        for head in range(heads):
            memory[head] = start

    first = base[0] + step * BLOCK
    rows, columns, same, carried, final, through, reach = block_masks(first, starts, count)
    below = jnp.logical_and(same, columns < rows)
    upto = jnp.logical_and(same, columns <= rows)
    queries, keys, values, stricts, scores, rate_list = [], [], [], [], [], []
    for head in range(heads):
        span = slice(head * size, (head + 1) * size)
        pieces = []
        for number, (lin, taps) in enumerate(
            ((lin_query, taps_query), (lin_key, taps_key), (lin_value, taps_value))
        ):
            place = slice(number * width + head * size, number * width + (head + 1) * size)
            joined = jnp.concatenate([before[:, place], lin[:, span]], axis=0)
            conv = short_conv(joined, taps[:, span], reach)
            pieces.append(conv * sigmoid(conv))
        query = pieces[0] * lax.rsqrt(jnp.sum(pieces[0] * pieces[0], axis=1, keepdims=True) + 1e-6)
        key = pieces[1] * lax.rsqrt(jnp.sum(pieces[1] * pieces[1], axis=1, keepdims=True) + 1e-6)
        queries.append(query)
        keys.append(key)
        values.append(pieces[2])
        rate_list.append(jnp.broadcast_to(rates[:, head : head + 1], (BLOCK, size)))
    for number, lin in enumerate((lin_query, lin_key, lin_value)):
        before[:, number * width : (number + 1) * width] = lin[BLOCK - EDGE :, :]
    for head in range(heads):
        products = mm(jnp.concatenate([queries[head], keys[head]], axis=0), keys[head], 1, 1)
        scores.append(jnp.where(upto, products[:BLOCK], 0.0))
        stricts.append(jnp.where(below, products[BLOCK:] * rate_list[head], 0.0))
    inverses = block_inverses(stricts, rows, columns)
    for head in range(heads):
        inverse_out[0, head] = inverses[head]
    writes = [
        mm(
            inverses[head],
            jnp.concatenate(
                [rate_list[head] * carried * keys[head], rate_list[head] * values[head]], axis=1
            )
        )
        for head in range(heads)
    ]
    helds = [memory[head] for head in range(heads)]
    for head in range(heads):
        memory_out[0, head] = helds[head]
    reads = [
        mm(
            jnp.concatenate([writes[head][:, :size], carried * queries[head]], axis=0),
            helds[head]
        )
        for head in range(heads)
    ]
    residues = [
        jnp.concatenate(
            [-reads[head][:BLOCK, :size], writes[head][:, size:] - reads[head][:BLOCK, size:]],
            axis=1,
        )
        for head in range(heads)
    ]
    updates = [
        through * helds[head] + mm(final * keys[head], residues[head], 0, 0)
        for head in range(heads)
    ]
    for head in range(heads):
        memory[head] = updates[head]
        final_out[head] = updates[head]
    for head in range(heads):
        span = slice(head * size, (head + 1) * size)
        result = reads[head][BLOCK:] + mm(scores[head], residues[head])
        effective_out[:, span] = result[:, :size]
        local_out[:, span] = result[:, size:]


def output_kernel(effective, local, entering, gain, mixed_out, headed_out, rounded_out):
    heads, size = entering.shape[0], entering.shape[1]
    for head in range(heads):
        span = slice(head * size, (head + 1) * size)
        mixed = local[:, span] + mm(effective[:, span], entering[head])
        mixed_out[:, span] = mixed
        scale = lax.rsqrt(jnp.mean(mixed * mixed, axis=1, keepdims=True) + 1e-5)
        headed = mixed * scale * gain[...]
        headed_out[:, span] = headed
        rounded_out[:, span] = headed.astype(rounded_out.dtype)


def norm_back_kernel(headed_grad, mixed_rows, effective, gain, grad_out, gain_out, local_out):
    heads, size = local_out.shape[0], local_out.shape[1]
    step = pl.program_id(0)

    @pl.when(step == 0)
    def _():
        gain_out[...] = jnp.zeros_like(gain_out)
        local_out[...] = jnp.zeros_like(local_out)

    for head in range(heads):
        span = slice(head * size, (head + 1) * size)
        mixed = mixed_rows[:, span]
        scale = lax.rsqrt(jnp.mean(mixed * mixed, axis=1, keepdims=True) + 1e-5)
        given = headed_grad[:, span]
        gain_out[...] += jnp.sum(given * mixed * scale, axis=0, keepdims=True)
        scaled = gain[...] * given
        along = jnp.mean(mixed * scaled, axis=1, keepdims=True)
        grad = scale * scaled - mixed * (scale * scale * scale * along)
        grad_out[:, span] = grad
        local_out[head] += mm(effective[:, span], grad, 0, 0)


def backward_kernel(
    starts,
    base,
    lin_query,
    lin_key,
    lin_value,
    prior_query,
    prior_key,
    prior_value,
    edge,
    taps_query,
    taps_key,
    taps_value,
    rates,
    inverse_in,
    memory_in,
    entering,
    leaving,
    mixed_grad,
    query_out,
    key_out,
    value_out,
    edge_out,
    logit_out,
    taps_query_out,
    taps_key_out,
    taps_value_out,
    after,
    memory_grad,
):
    heads, size = entering.shape[0], entering.shape[1]
    width = heads * size
    step = pl.program_id(0)
    blocks = pl.num_programs(0)
    here = blocks - 1 - step
    count = starts.shape[0]
    every = range(heads)
    spans = [slice(head * size, (head + 1) * size) for head in every]

    @pl.when(step == 0)
    def _():
        after[...] = jnp.zeros_like(after)
        memory_grad[...] = leaving[...]
        taps_query_out[...] = jnp.zeros_like(taps_query_out)
        taps_key_out[...] = jnp.zeros_like(taps_key_out)
        taps_value_out[...] = jnp.zeros_like(taps_value_out)

    first = base[0] + here * BLOCK
    rows, columns, same, carried, final, through, reach = block_masks(first, starts, count)
    below = jnp.logical_and(same, columns < rows)
    upto = jnp.logical_and(same, columns <= rows)

    def convolved(number, lin, prior, taps, head):
        place = slice(number * width + head * size, number * width + (head + 1) * size)
        border = jnp.where(here == 0, edge[:, place], prior[:, spans[head]])
        joined = jnp.concatenate([border, lin[:, spans[head]]], axis=0)
        conv = short_conv(joined, taps[:, spans[head]], reach)
        return joined, conv, sigmoid(conv)

    def unit_scale(piece):
        return lax.rsqrt(jnp.sum(piece * piece, axis=1, keepdims=True) + 1e-6)

    query_parts = [convolved(0, lin_query, prior_query, taps_query, head) for head in every]
    key_parts = [convolved(1, lin_key, prior_key, taps_key, head) for head in every]
    value_parts = [convolved(2, lin_value, prior_value, taps_value, head) for head in every]
    query_scales = [unit_scale(conv * gate) for _, conv, gate in query_parts]
    key_scales = [unit_scale(conv * gate) for _, conv, gate in key_parts]
    queries = [conv * gate * scale for (_, conv, gate), scale in zip(query_parts, query_scales)]
    keys = [conv * gate * scale for (_, conv, gate), scale in zip(key_parts, key_scales)]
    values = [conv * gate for _, conv, gate in value_parts]
    rate_columns = [rates[:, head : head + 1] for head in every]
    rate_wide = [jnp.broadcast_to(column, (BLOCK, size)) for column in rate_columns]
    products = [
        mm(jnp.concatenate([queries[head], keys[head]], axis=0), keys[head], 1, 1)
        for head in every
    ]
    scores = [jnp.where(upto, part[:BLOCK], 0.0) for part in products]
    grams = [part[BLOCK:] for part in products]
    inverses = [inverse_in[0, head] for head in every]
    memories = [
        mm(memory_in[0, head][:, :size], entering[head]) + memory_in[0, head][:, size:]
        for head in every
    ]
    lefts = [carried * key for key in keys]
    wanted = [values[head] - mm(lefts[head], memories[head]) for head in every]
    residues = [mm(inverses[head], rate_wide[head] * wanted[head]) for head in every]
    given = [mixed_grad[:, span] for span in spans]
    score_sides = [mm(scores[head], given[head], 0, 0) for head in every]
    state_grads = [memory_grad[head] for head in every]
    last_keys = [final * key for key in keys]
    residue_grads = [
        score_sides[head] + mm(last_keys[head], state_grads[head]) for head in every
    ]
    solved_grads = [mm(inverses[head], residue_grads[head], 0, 0) for head in every]
    wanted_grads = [rate_wide[head] * solved_grads[head] for head in every]
    updates = [
        through * state_grads[head]
        + mm(
            jnp.concatenate([carried * queries[head], -lefts[head]], axis=0),
            jnp.concatenate([given[head], wanted_grads[head]], axis=0),
            0,
            0,
        )
        for head in every
    ]
    for head in every:
        memory_grad[head] = updates[head]
    outers = [
        mm(jnp.concatenate([given[head], solved_grads[head]], axis=0), residues[head], 1, 1)
        for head in every
    ]
    state_sides = [
        mm(jnp.concatenate([given[head], wanted_grads[head]], axis=0), memories[head], 1, 1)
        for head in every
    ]
    final_sides = [final * mm(residues[head], state_grads[head], 1, 1) for head in every]
    score_grads = [jnp.where(upto, part[:BLOCK], 0.0) for part in outers]
    strict_grads = [jnp.where(below, -part[BLOCK:], 0.0) for part in outers]
    gram_grads = [rate_wide[head] * strict_grads[head] for head in every]
    pairs = [
        jnp.concatenate([score_grads[head], gram_grads[head]], axis=0) for head in every
    ]
    key_sides = [mm(pairs[head], keys[head]) for head in every]
    turned_sides = [
        mm(pairs[head], jnp.concatenate([queries[head], keys[head]], axis=0), 0, 0)
        for head in every
    ]
    rate_grads = [
        jnp.sum(
            solved_grads[head] * wanted[head] + strict_grads[head] * grams[head],
            axis=1,
            keepdims=True,
        )
        for head in every
    ]
    lanes = lax.broadcasted_iota(jnp.int32, (BLOCK, rates.shape[1]), 1)
    logit_grad = jnp.zeros((BLOCK, rates.shape[1]), F32)
    for head in every:
        column = rate_columns[head]
        logit_grad = jnp.where(
            lanes == head, rate_grads[head] * column * (1.0 - column), logit_grad
        )
    logit_out[...] = logit_grad
    query_grads = [
        carried * state_sides[head][:BLOCK] + key_sides[head][:BLOCK] for head in every
    ]
    key_grads = [
        key_sides[head][BLOCK:]
        - carried * state_sides[head][BLOCK:]
        + turned_sides[head]
        + final_sides[head]
        for head in every
    ]
    query_grads = [
        scale * (grad - query * jnp.sum(query * grad, axis=1, keepdims=True))
        for scale, grad, query in zip(query_scales, query_grads, queries)
    ]
    key_grads = [
        scale * (grad - key * jnp.sum(key * grad, axis=1, keepdims=True))
        for scale, grad, key in zip(key_scales, key_grads, keys)
    ]
    spare = jnp.zeros((EDGE, size), F32)
    for number, (grads, parts, taps, lin_out, taps_out) in enumerate(
        (
            (query_grads, query_parts, taps_query, query_out, taps_query_out),
            (key_grads, key_parts, taps_key, key_out, taps_key_out),
            (wanted_grads, value_parts, taps_value, value_out, taps_value_out),
        )
    ):
        for head in every:
            span = spans[head]
            place = slice(number * width + head * size, number * width + (head + 1) * size)
            joined, conv, gate = parts[head]
            conv_grad = grads[head] * gate * (1.0 + conv * (1.0 - gate))
            lin_grad = taps[3:4, span] * conv_grad
            tail = spare
            taps_grad = [jnp.sum(conv_grad * joined[EDGE:], axis=0, keepdims=True)]
            for back in range(1, 4):
                part = conv_grad * reach[back]
                tap = taps[3 - back : 4 - back, span]
                lin_grad = lin_grad + tap * jnp.concatenate([part, spare], axis=0)[
                    back : back + BLOCK
                ]
                tail = tail + tap * jnp.concatenate([spare, part[:EDGE]], axis=0)[
                    back : back + EDGE
                ]
                taps_grad.append(
                    jnp.sum(part * joined[EDGE - back : EDGE - back + BLOCK], axis=0, keepdims=True)
                )
            taps_out[:, span] += jnp.concatenate(taps_grad[::-1], axis=0)
            lin_out[: BLOCK - EDGE, span] = lin_grad[: BLOCK - EDGE]
            lin_out[BLOCK - EDGE :, span] = lin_grad[BLOCK - EDGE :] + after[:, place]
            after[:, place] = tail
            edge_out[:, place] = tail


def on_chip(kernel, name, **settings):
    return pl.pallas_call(
        kernel,
        name=name,
        cost_estimate=pl.CostEstimate(flops=1, bytes_accessed=1, transcendentals=0),
        compiler_params=pltpu.CompilerParams(
            dimension_semantics=("arbitrary",), vmem_limit_bytes=48 * 1024 * 1024
        ),
        **settings,
    )


def whole(shape):
    return pl.BlockSpec(shape, lambda i: (0,) * len(shape))


def scalars():
    return pl.BlockSpec(memory_space=pltpu.SMEM)


def delta_forward(starts, base, lins, edge, taps, rates, heads, size):
    length, width = lins[0].shape
    blocks = length // BLOCK
    row_block = pl.BlockSpec((BLOCK, width), lambda i: (i, 0))
    return on_chip(
        forward_kernel,
        "delta_forward",
        grid=(blocks,),
        in_specs=[scalars(), scalars()]
        + [row_block] * 3
        + [whole((EDGE, 3 * width))]
        + [whole((4, width))] * 3
        + [pl.BlockSpec((BLOCK, heads), lambda i: (i, 0))],
        out_specs=[
            pl.BlockSpec((1, heads, BLOCK, BLOCK), lambda i: (i, 0, 0, 0)),
            row_block,
            row_block,
            pl.BlockSpec((1, heads, size, 2 * size), lambda i: (i, 0, 0, 0)),
            whole((heads, size, 2 * size)),
        ],
        out_shape=[
            jax.ShapeDtypeStruct((blocks, heads, BLOCK, BLOCK), F32),
            jax.ShapeDtypeStruct((length, width), F32),
            jax.ShapeDtypeStruct((length, width), F32),
            jax.ShapeDtypeStruct((blocks, heads, size, 2 * size), F32),
            jax.ShapeDtypeStruct((heads, size, 2 * size), F32),
        ],
        scratch_shapes=[
            pltpu.VMEM((EDGE, 3 * width), F32),
            pltpu.VMEM((heads, size, 2 * size), F32),
        ],
    )(starts, base, *lins, edge, *taps, rates)


def delta_output(effective, local, entering, gain):
    length, width = local.shape
    heads, size = entering.shape[0], entering.shape[1]
    rows = min(length, 256)
    row_block = pl.BlockSpec((rows, width), lambda i: (i, 0))
    return on_chip(
        output_kernel,
        "delta_output",
        grid=(length // rows,),
        in_specs=[row_block, row_block, whole((heads, size, size)), whole((1, size))],
        out_specs=[row_block, row_block, row_block],
        out_shape=[
            jax.ShapeDtypeStruct((length, width), F32),
            jax.ShapeDtypeStruct((length, width), F32),
            jax.ShapeDtypeStruct((length, width), BF16),
        ],
    )(effective, local, entering, gain)


def norm_back(headed_grad, mixed_rows, effective, gain, heads, size):
    length, width = headed_grad.shape
    rows = min(length, 256)
    row_block = pl.BlockSpec((rows, width), lambda i: (i, 0))
    return on_chip(
        norm_back_kernel,
        "norm_back",
        grid=(length // rows,),
        in_specs=[row_block, row_block, row_block, whole((1, size))],
        out_specs=[row_block, whole((1, size)), whole((heads, size, size))],
        out_shape=[
            jax.ShapeDtypeStruct((length, width), F32),
            jax.ShapeDtypeStruct((1, size), F32),
            jax.ShapeDtypeStruct((heads, size, size), F32),
        ],
    )(headed_grad, mixed_rows, effective, gain)


def norm_pull_kernel(odd, part, other, values, gain, given, grad_out, rounded_out, gain_out):
    step = pl.program_id(0)
    second = step * 2 // pl.num_programs(0)

    @pl.when(step == 0)
    def _():
        gain_out[...] = jnp.zeros_like(gain_out)

    grad = jnp.where(second == odd[0], part[...], other[...])
    value = values[...]
    scale = lax.rsqrt(jnp.mean(value * value, axis=1, keepdims=True) + 1e-5)
    gain_out[...] += jnp.sum(grad * value * scale, axis=0, keepdims=True)
    scaled = gain[...] * grad
    along = jnp.mean(value * scaled, axis=1, keepdims=True)
    result = given[...] + (scale * scaled - value * (scale * scale * scale * along))
    grad_out[...] = result
    rounded_out[...] = result.astype(rounded_out.dtype)


def norm_pulled(halves, values, gain, given):
    length, width = values.shape
    rows = length // 8
    odd = (lax.axis_index("head") % 2).astype(jnp.int32).reshape(1)
    row_block = pl.BlockSpec((rows, width), lambda i: (i, 0))
    half_block = pl.BlockSpec((rows, width), lambda i: (i % 4, 0))
    return on_chip(
        norm_pull_kernel,
        "norm_pull",
        grid=(8,),
        in_specs=[scalars(), half_block, half_block, row_block, whole((1, width)), row_block],
        out_specs=[row_block, row_block, whole((1, width))],
        out_shape=[
            jax.ShapeDtypeStruct((length, width), F32),
            jax.ShapeDtypeStruct((length, width), BF16),
            jax.ShapeDtypeStruct((1, width), F32),
        ],
    )(odd, *halves, values, gain.reshape(1, width), given)


def beside_kernel(first, second, out):
    width = first.shape[1]
    out[:, :width] = first[...].astype(out.dtype)
    out[:, width:] = second[...].astype(out.dtype)


def above_kernel(first, second, out):
    rows = first.shape[0]
    out[:rows] = first[...].astype(out.dtype)
    out[rows:] = second[...].astype(out.dtype)


def rounded_beside(first, second):
    length, width = first.shape
    rows = min(length, 256)
    block = pl.BlockSpec((rows, width), lambda i: (i, 0))
    return on_chip(
        beside_kernel,
        "rounded_beside",
        grid=(length // rows,),
        in_specs=[block, block],
        out_specs=pl.BlockSpec((rows, 2 * width), lambda i: (i, 0)),
        out_shape=jax.ShapeDtypeStruct((length, 2 * width), BF16),
    )(first, second)


def rounded_above(first, second):
    rows, width = first.shape
    columns = min(width, 256)
    block = pl.BlockSpec((rows, columns), lambda i: (0, i))
    return on_chip(
        above_kernel,
        "rounded_above",
        grid=(width // columns,),
        in_specs=[block, block],
        out_specs=pl.BlockSpec((2 * rows, columns), lambda i: (0, i)),
        out_shape=jax.ShapeDtypeStruct((2 * rows, width), BF16),
    )(first, second)


def delta_backward(
    starts, base, lins, edge, taps, rates, inverse, memories, entering, leaving, mixed_grad
):
    length, width = lins[0].shape
    heads, size = entering.shape[0], entering.shape[1]
    blocks = length // BLOCK
    ratio = BLOCK // EDGE
    row_block = pl.BlockSpec((BLOCK, width), lambda i: (blocks - 1 - i, 0))
    prior = pl.BlockSpec(
        (EDGE, width), lambda i: (jnp.maximum((blocks - 1 - i) * ratio - 1, 0), 0)
    )
    rate_block = pl.BlockSpec((BLOCK, heads), lambda i: (blocks - 1 - i, 0))
    return on_chip(
        backward_kernel,
        "delta_backward",
        grid=(blocks,),
        in_specs=[scalars(), scalars()]
        + [row_block] * 3
        + [prior] * 3
        + [whole((EDGE, 3 * width))]
        + [whole((4, width))] * 3
        + [
            rate_block,
            pl.BlockSpec((1, heads, BLOCK, BLOCK), lambda i: (blocks - 1 - i, 0, 0, 0)),
            pl.BlockSpec((1, heads, size, 2 * size), lambda i: (blocks - 1 - i, 0, 0, 0)),
            whole((heads, size, size)),
            whole((heads, size, size)),
            row_block,
        ],
        out_specs=[row_block] * 3
        + [whole((EDGE, 3 * width)), rate_block]
        + [whole((4, width))] * 3,
        out_shape=[jax.ShapeDtypeStruct((length, width), F32)] * 3
        + [
            jax.ShapeDtypeStruct((EDGE, 3 * width), F32),
            jax.ShapeDtypeStruct((length, heads), F32),
        ]
        + [jax.ShapeDtypeStruct((4, width), F32)] * 3,
        scratch_shapes=[
            pltpu.VMEM((EDGE, 3 * width), F32),
            pltpu.VMEM((heads, size, size), F32),
        ],
    )(starts, base, *lins, *lins, edge, *taps, rates, inverse, memories, entering, leaving, mixed_grad)


def swap(block, axis, bit):
    count = lax.axis_size(axis)
    return lax.ppermute(block, axis, [(i, i ^ bit) for i in range(count)])


def shift(block, axis, distance):
    devices = range(lax.axis_size(axis))
    route = [(i - distance, i) for i in devices if i - distance in devices]
    return lax.ppermute(block, axis, route)


def begun_over_head(term):
    odd = lax.axis_index("head") % 2
    half = term.shape[0] // 2
    keep = lax.dynamic_slice_in_dim(term, odd * half, half, 0)
    send = lax.dynamic_slice_in_dim(term, (1 - odd) * half, half, 0)
    return keep + swap(send, "head", 1)


def ended_over_head(part, *gates):
    part = part + after(swap(part, "head", 2), *gates)
    return part, swap(part, "head", 1)


def whole_rows(part, other):
    return jnp.where(
        lax.axis_index("head") % 2 == 0,
        jnp.concatenate([part, other], axis=0),
        jnp.concatenate([other, part], axis=0),
    )


def after(value, *others):
    return lax.optimization_barrier((value,) + others)[0] if others else value


def summed_everywhere(vector, axis):
    count = lax.axis_size(axis)
    bit = 1
    while bit < count:
        vector = vector + swap(vector, axis, bit)
        bit *= 2
    return vector


def relative_order(bits):
    if not bits:
        return [0]
    rest = relative_order(bits[1:])
    return [index ^ bits[0] for index in rest] + rest


def seq_bits():
    bits = []
    while 1 << len(bits) < lax.axis_size("seq"):
        bits.append(1 << len(bits))
    return bits


def arrange_kernel(places, rows, out):
    out[...] = rows[...]


def arranged(rows, places):
    length, size = rows.shape[0], rows.shape[1] // lax.axis_size("seq")
    if size % 128:
        return jnp.concatenate(
            [lax.dynamic_slice_in_dim(rows, place * size, size, 1) for place in places], axis=1
        )
    return pl.pallas_call(
        arrange_kernel,
        name="arrange",
        cost_estimate=pl.CostEstimate(flops=1, bytes_accessed=1, transcendentals=0),
        grid_spec=pltpu.PrefetchScalarGridSpec(
            num_scalar_prefetch=1,
            grid=(len(places),),
            in_specs=[pl.BlockSpec((length, size), lambda i, places: (0, places[i]))],
            out_specs=pl.BlockSpec((length, size), lambda i, places: (0, i)),
        ),
        out_shape=jax.ShapeDtypeStruct(rows.shape, rows.dtype),
        compiler_params=pltpu.CompilerParams(dimension_semantics=("arbitrary",)),
    )(jnp.stack(places).astype(jnp.int32), rows)


def relative_places():
    here = lax.axis_index("seq")
    return [here ^ index for index in relative_order(seq_bits())]


def product(rows, others, rows_first):
    return matmul(rows, others, 0, 0) if rows_first else matmul(others, rows, 0, 0)


def received(given, kept, axis, place):
    bits = seq_bits()
    kept = kept + swap(given, "seq", bits[place])
    if place + 1 == len(bits):
        return None, kept
    size = kept.shape[axis] // 2
    return lax.slice_in_dim(kept, 0, size, axis=axis), lax.slice_in_dim(
        kept, size, 2 * size, axis=axis
    )


def finished(given, kept, axis, place):
    while place < len(seq_bits()):
        given, kept = received(given, kept, axis, place)
        place += 1
    return kept


def chain(transfer, offset, distance, turned=False, between=()):
    hops = max(lax.axis_size("seq") // 2, 1)
    groups = 2
    count = offset.shape[0] // groups
    picks = [slice(index * count, (index + 1) * count) for index in range(groups)]
    form = "hji,hjk->hik" if turned else "hij,hjk->hik"
    states = [shift(offset[pick], "seq", distance) for pick in picks]
    for hop in range(hops - 1):
        if hop < len(between):
            states[0] = after(states[0], between[hop])
        moved = [
            jnp.einsum(form, transfer[pick], state, precision=lax.Precision.HIGH) + offset[pick]
            for pick, state in zip(picks, states)
        ]
        states = [shift(part, "seq", distance) for part in moved]
    return jnp.concatenate(states, axis=0)


def row_norm(values):
    return lax.rsqrt(jnp.mean(values * values, axis=-1, keepdims=True) + 1e-05)


def matmul(left, right, left_dim=1, right_dim=0):
    return lax.dot_general(
        left, right, (((left_dim,), (right_dim,)), ((), ())), preferred_element_type=F32
    )


def shards(
    hidden,
    doc_starts,
    norm_gain,
    w_query,
    w_key,
    w_value,
    w_strength,
    strength_bias,
    conv_query,
    conv_key,
    conv_value,
    head_gain,
    w_output,
    ffn_gain,
    w_gate,
    w_up,
    w_down,
    out_grad,
):
    length = hidden.shape[0]
    size = head_gain.shape[0]
    heads = strength_bias.shape[0]
    width = heads * size
    seq_rank = lax.axis_index("seq")
    seq_count = lax.axis_size("seq")
    base = (seq_rank * length).astype(jnp.int32).reshape(1)
    taps = tuple(part.astype(F32) for part in (conv_query, conv_key, conv_value))
    gain = head_gain.reshape(1, size)

    scale_one = row_norm(hidden)
    normed = (hidden * scale_one * norm_gain).astype(BF16)
    w_wide = w_output.astype(F32)
    w_across = swap(w_wide, "head", 2)
    lins = tuple(matmul(normed, part) for part in (w_query, w_key, w_value))
    tails = jnp.concatenate([part[-EDGE:] for part in lins], axis=1)
    edge = shift(tails, "seq", 1)
    rates = jax.nn.sigmoid(matmul(normed, w_strength) + strength_bias)
    inverse, effective, local, memories, last = delta_forward(
        doc_starts, base, lins, edge, taps, rates, heads, size
    )
    transfer, offset = last[:, :, :size], last[:, :, size:]
    entering = chain(transfer, offset, 1)
    mixed_rows, headed_wide, headed = delta_output(effective, local, entering, gain)
    h_across = swap(headed_wide, "head", 2)
    h_core = swap(headed_wide, "head", 1)
    w_late, w_across = after((w_wide, w_across), headed)
    w_near = rounded_above(w_late, swap(w_late, "head", 1))
    w_distant = rounded_above(w_across, swap(w_across, "head", 1))
    middle = hidden + matmul(rounded_beside(headed_wide, h_core), w_near)
    ffn_cot = after(out_grad, headed).astype(BF16)
    cot_ordered = arranged(ffn_cot, relative_places())
    h_across = after(h_across, middle, w_distant, cot_ordered)
    h_far = swap(h_across, "head", 1)
    middle = middle + matmul(rounded_beside(h_across, h_far), w_distant)
    scale_two = row_norm(middle)
    normed_two = (middle * scale_two * ffn_gain).astype(BF16)
    gate_rows = matmul(normed_two, w_gate)
    upward = matmul(normed_two, w_up)
    sigma = jax.nn.sigmoid(gate_rows)
    silu_gate = gate_rows * sigma
    active = (silu_gate * upward).astype(BF16)
    half = ffn_cot.shape[1] // 2
    split = active.shape[1] // 128 * 3 // 4 * 128
    lead, rest = active[:, :split], active[:, split:]
    lead_given = product(cot_ordered[:, :half], lead, False)
    ffn_cot = after(ffn_cot, lead_given)
    active_grad = matmul(ffn_cot, w_down, 1, 1)
    gate_cot = (active_grad * upward * sigma * (1.0 + gate_rows * (1.0 - sigma))).astype(BF16)
    up_cot = (active_grad * silu_gate).astype(BF16)
    both_term = matmul(normed_two, jnp.concatenate([gate_cot, up_cot], axis=1), 0, 0)
    both_grad = lax.psum_scatter(both_term, "seq", scatter_dimension=0, tiled=True)
    gate_late, up_late = after((gate_cot, up_cot), both_term)
    two_part = matmul(gate_late, w_gate, 1, 1) + matmul(up_late, w_up, 1, 1)
    two_begun = begun_over_head(two_part)
    ffn_begun = begun_over_head(matmul(after(active, two_begun), w_down))
    cot_ordered = after(cot_ordered, two_begun)
    lead_kept = product(cot_ordered[:, half:], lead, False)
    rest_given = product(cot_ordered[:, :half], rest, False)
    rest_kept = product(cot_ordered[:, half:], rest, False)
    middle_grad, branch_cot, ffn_gain_part = norm_pulled(
        ended_over_head(
            two_begun, ffn_begun, lead_kept, rest_given, rest_kept
        ),
        middle,
        ffn_gain,
        out_grad,
    )
    headed_grad = matmul(branch_cot, w_output, 1, 1)
    mixed_grad, head_gain_part, local_grad = norm_back(
        headed_grad, mixed_rows, effective, gain, heads, size
    )
    leaving = chain(transfer, local_grad, -1, True)
    lead_given, lead_kept = received(lead_given, lead_kept, 1, 0)
    lead_given = after(lead_given, leaving)
    leaving = after(leaving, lead_given)
    back = delta_backward(
        doc_starts, base, lins, edge, taps, rates, inverse, memories, entering, leaving, mixed_grad
    )
    ffn_halves = ended_over_head(ffn_begun)
    lead_given, lead_kept = received(lead_given, lead_kept, 1, 1)
    returned, logit_grad = after(
        (shift(back[3], "seq", -1), back[4]), lead_given, ffn_halves[0]
    )
    branch_ordered = arranged(after(branch_cot, back[3]), relative_places())
    mix_given = jnp.concatenate(
        [rest_given, product(branch_ordered[:, :half], headed, False)], axis=0
    )
    mix_given = after(mix_given, returned)
    cots = tuple(
        jnp.concatenate(
            [part[:-EDGE], part[-EDGE:] + returned[:, index * width : (index + 1) * width]], axis=0
        ).astype(BF16)
        for index, part in enumerate(back[:3])
    )
    strength_cot = logit_grad.astype(BF16)
    cot = after(jnp.concatenate(cots, axis=1), lead_given)
    lin_term = product(normed, cot, True)
    lin_grad = lax.psum_scatter(lin_term, "seq", scatter_dimension=0, tiled=True)
    mix_kept = jnp.concatenate(
        [rest_kept, product(branch_ordered[:, half:], headed, False)], axis=0
    )
    mix_given, mix_kept = received(mix_given, after(mix_kept, lin_term), 1, 0)
    lead_kept = finished(lead_given, after(lead_kept, lin_term), 1, 2)
    late_cots, strength_cot = after((cots, strength_cot), lin_term, mix_given, lead_kept)
    first_part = matmul(late_cots[0], w_query, 1, 1)
    first_part = first_part + matmul(late_cots[1], w_key, 1, 1)
    first_part = first_part + matmul(late_cots[2], w_value, 1, 1)
    first_part = first_part + matmul(strength_cot, w_strength, 1, 1)
    norm_gain_part = jnp.sum(first_part * hidden * scale_one, axis=0)
    shared = summed_everywhere(
        jnp.concatenate([norm_gain_part, head_gain_part.reshape(-1)]), "head"
    )
    mix_given, mix_kept = received(mix_given, after(mix_kept, first_part), 1, 1)
    first_begun = after(begun_over_head(first_part), shared, mix_given)
    first_halves = ended_over_head(first_begun, both_grad)
    mix_kept = finished(mix_given, after(mix_kept, first_halves[0]), 1, 2)
    first_halves = after(first_halves, mix_kept)
    hidden_grad = norm_pulled(first_halves, hidden, norm_gain, middle_grad)[0]
    block_output = middle + whole_rows(*ffn_halves)
    hidden_units = gate_cot.shape[1]
    w_gate_grad, w_up_grad = both_grad[:, :hidden_units], both_grad[:, hidden_units:]
    lin_grad = after(lin_grad, hidden_grad, block_output, w_gate_grad, w_up_grad, mix_kept)
    lin_grads = tuple(lin_grad[:, index * width : (index + 1) * width] for index in range(3))
    rest_rows = rest.shape[1]
    w_down_grad = jnp.concatenate([lead_kept, mix_kept[:rest_rows]], axis=0)
    w_output_grad = mix_kept[rest_rows:]
    strength_term = matmul(strength_cot, normed, 0, 0)

    small = jnp.concatenate(
        [
            shared,
            strength_term.reshape(-1),
            ffn_gain_part.reshape(-1),
        ]
        + [part.reshape(-1) for part in back[5:8]]
        + [jnp.sum(logit_grad, axis=0)]
    )
    small = summed_everywhere(small, "seq")
    features = norm_gain.shape[0]
    block = features // seq_count
    cut = [features, size, heads * features, features] + [4 * width] * 3 + [heads]
    parts, at = [], 0
    for extent in cut:
        parts.append(small[at : at + extent])
        at += extent

    def own(vector, axis=0):
        return lax.dynamic_slice_in_dim(vector, seq_rank * block, block, axis)

    return (
        block_output,
        hidden_grad,
        own(parts[0]),
        lin_grads[0],
        lin_grads[1],
        lin_grads[2],
        own(parts[2].reshape(heads, features), 1).T,
        parts[7],
        parts[4].reshape(4, width),
        parts[5].reshape(4, width),
        parts[6].reshape(4, width),
        parts[1],
        w_output_grad,
        own(parts[3]),
        w_gate_grad,
        w_up_grad,
        w_down_grad,
    )


def solution(mesh):
    return jax.shard_map(
        shards,
        mesh=mesh,
        in_specs=(
            P("seq", None),
            P(),
            P(),
            P(None, "head"),
            P(None, "head"),
            P(None, "head"),
            P(None, "head"),
            P("head"),
            P(None, "head"),
            P(None, "head"),
            P(None, "head"),
            P(),
            P("head", None),
            P(),
            P(None, "head"),
            P(None, "head"),
            P("head", None),
            P("seq", None),
        ),
        out_specs=(
            P("seq", None),
            P("seq", None),
            P("seq"),
            P("seq", "head"),
            P("seq", "head"),
            P("seq", "head"),
            P("seq", "head"),
            P("head"),
            P(None, "head"),
            P(None, "head"),
            P(None, "head"),
            P(),
            P("head", "seq"),
            P("seq"),
            P("seq", "head"),
            P("seq", "head"),
            P("head", "seq"),
        ),
        check_vma=False,
    )
```

```python
import jax
import jax.numpy as jnp
from jax import lax
from jax.experimental import pallas as pl
from jax.experimental.pallas import tpu as pltpu
from jax.sharding import PartitionSpec as P

BLOCK = 128
SUB = 32
EDGE = 8
F32 = jnp.float32
BF16 = jnp.bfloat16


def mm(left, right, left_dim=1, right_dim=0, passes=3):
    dims = (((left_dim,), (right_dim,)), ((), ()))
    if passes == 1:
        return lax.dot_general(
            left.astype(BF16), right.astype(BF16), dims, preferred_element_type=F32
        )
    precision = lax.Precision.HIGH if passes == 3 else lax.Precision.HIGHEST
    return lax.dot_general(left, right, dims, precision=precision, preferred_element_type=F32)


def doc_of(places, starts, count):
    total = jnp.full(places.shape, -1, jnp.int32) if places.shape else jnp.int32(-1)
    for index in range(count):
        total = total + jnp.where(starts[index] <= places, 1, 0).astype(jnp.int32)
    return total


def sigmoid(value):
    return 1.0 / (1.0 + jnp.exp(-value))


def block_masks(first, starts, count):
    rows = lax.broadcasted_iota(jnp.int32, (BLOCK, BLOCK), 0)
    columns = lax.broadcasted_iota(jnp.int32, (BLOCK, BLOCK), 1)
    row_docs = doc_of(first + rows, starts, count)
    column_docs = doc_of(first + columns, starts, count)
    same = row_docs == column_docs
    prior_doc = doc_of(first - 1, starts, count)
    last_doc = doc_of(first + BLOCK - 1, starts, count)
    carried = (row_docs == prior_doc).astype(F32)
    final = (row_docs == last_doc).astype(F32)
    through = jnp.where(prior_doc == last_doc, 1.0, 0.0).astype(F32)
    reach = [None]
    for back in range(1, 4):
        reach.append((row_docs == doc_of(first - back + rows, starts, count)).astype(F32))
    return rows, columns, same, carried, final, through, reach


def short_conv(joined, taps, reach):
    total = taps[3:4] * joined[EDGE:]
    for back in range(1, 4):
        total = total + taps[3 - back : 4 - back] * (
            joined[EDGE - back : EDGE - back + BLOCK] * reach[back]
        )
    return total


def block_inverses(stricts, rows, columns, passes=3):
    near_mask = rows // SUB == columns // SUB
    eye = jnp.where(rows == columns, 1.0, 0.0)
    nears = [jnp.where(near_mask, strict, 0.0) for strict in stricts]
    fars = [strict - near for strict, near in zip(stricts, nears)]
    inverses = [eye - near for near in nears]
    powers = [mm(near, near, passes=passes) for near in nears]
    covered = 2
    while covered * 2 < SUB:
        both = [
            mm(jnp.concatenate([power, inverse], axis=0), power, passes=passes)
            for power, inverse in zip(powers, inverses)
        ]
        powers = [part[:BLOCK] for part in both]
        inverses = [inverse + part[BLOCK:] for inverse, part in zip(inverses, both)]
        covered *= 2
    inverses = [
        inverse + mm(inverse, power, passes=passes) for inverse, power in zip(inverses, powers)
    ]
    chains = [mm(inverse, far, passes=passes) for inverse, far in zip(inverses, fars)]
    both = [
        mm(link, jnp.concatenate([inverse, link], axis=1), passes=passes)
        for link, inverse in zip(chains, inverses)
    ]
    partials = [inverse - part[:, :BLOCK] for inverse, part in zip(inverses, both)]
    return [
        partial + mm(part[:, BLOCK:], partial, passes=passes)
        for partial, part in zip(partials, both)
    ]


def forward_kernel(
    starts,
    base,
    lin_query,
    lin_key,
    lin_value,
    edge,
    taps_query,
    taps_key,
    taps_value,
    rates,
    inverse_out,
    effective_out,
    local_out,
    memory_out,
    final_out,
    before,
    memory,
):
    heads, size = memory.shape[0], memory.shape[1]
    width = heads * size
    step = pl.program_id(0)
    count = starts.shape[0]

    @pl.when(step == 0)
    def _():
        before[...] = edge[...]
        line = lax.broadcasted_iota(jnp.int32, (size, 2 * size), 0)
        lane = lax.broadcasted_iota(jnp.int32, (size, 2 * size), 1)
        start = jnp.where(line == lane, 1.0, 0.0).astype(F32)
        for head in range(heads):
            memory[head] = start

    first = base[0] + step * BLOCK
    rows, columns, same, carried, final, through, reach = block_masks(first, starts, count)
    below = jnp.logical_and(same, columns < rows)
    upto = jnp.logical_and(same, columns <= rows)
    queries, keys, values, stricts, scores, rate_list = [], [], [], [], [], []
    for head in range(heads):
        span = slice(head * size, (head + 1) * size)
        pieces = []
        for number, (lin, taps) in enumerate(
            ((lin_query, taps_query), (lin_key, taps_key), (lin_value, taps_value))
        ):
            place = slice(number * width + head * size, number * width + (head + 1) * size)
            joined = jnp.concatenate([before[:, place], lin[:, span]], axis=0)
            conv = short_conv(joined, taps[:, span], reach)
            pieces.append(conv * sigmoid(conv))
        query = pieces[0] * lax.rsqrt(jnp.sum(pieces[0] * pieces[0], axis=1, keepdims=True) + 1e-6)
        key = pieces[1] * lax.rsqrt(jnp.sum(pieces[1] * pieces[1], axis=1, keepdims=True) + 1e-6)
        queries.append(query)
        keys.append(key)
        values.append(pieces[2])
        rate_list.append(jnp.broadcast_to(rates[:, head : head + 1], (BLOCK, size)))
    for number, lin in enumerate((lin_query, lin_key, lin_value)):
        before[:, number * width : (number + 1) * width] = lin[BLOCK - EDGE :, :]
    for head in range(heads):
        products = mm(jnp.concatenate([queries[head], keys[head]], axis=0), keys[head], 1, 1)
        scores.append(jnp.where(upto, products[:BLOCK], 0.0))
        stricts.append(jnp.where(below, products[BLOCK:] * rate_list[head], 0.0))
    inverses = block_inverses(stricts, rows, columns)
    for head in range(heads):
        inverse_out[0, head] = inverses[head]
    writes = [
        mm(
            inverses[head],
            jnp.concatenate(
                [rate_list[head] * carried * keys[head], rate_list[head] * values[head]], axis=1
            )
        )
        for head in range(heads)
    ]
    helds = [memory[head] for head in range(heads)]
    for head in range(heads):
        memory_out[0, head] = helds[head]
    reads = [
        mm(
            jnp.concatenate([writes[head][:, :size], carried * queries[head]], axis=0),
            helds[head]
        )
        for head in range(heads)
    ]
    residues = [
        jnp.concatenate(
            [-reads[head][:BLOCK, :size], writes[head][:, size:] - reads[head][:BLOCK, size:]],
            axis=1,
        )
        for head in range(heads)
    ]
    updates = [
        through * helds[head] + mm(final * keys[head], residues[head], 0, 0)
        for head in range(heads)
    ]
    for head in range(heads):
        memory[head] = updates[head]
        final_out[head] = updates[head]
    for head in range(heads):
        span = slice(head * size, (head + 1) * size)
        result = reads[head][BLOCK:] + mm(scores[head], residues[head])
        effective_out[:, span] = result[:, :size]
        local_out[:, span] = result[:, size:]


def output_kernel(effective, local, entering, gain, mixed_out, headed_out, rounded_out):
    heads, size = entering.shape[0], entering.shape[1]
    for head in range(heads):
        span = slice(head * size, (head + 1) * size)
        mixed = local[:, span] + mm(effective[:, span], entering[head])
        mixed_out[:, span] = mixed
        scale = lax.rsqrt(jnp.mean(mixed * mixed, axis=1, keepdims=True) + 1e-5)
        headed = mixed * scale * gain[...]
        headed_out[:, span] = headed
        rounded_out[:, span] = headed.astype(rounded_out.dtype)


def norm_back_kernel(headed_grad, mixed_rows, effective, gain, grad_out, gain_out, local_out):
    heads, size = local_out.shape[0], local_out.shape[1]
    step = pl.program_id(0)

    @pl.when(step == 0)
    def _():
        gain_out[...] = jnp.zeros_like(gain_out)
        local_out[...] = jnp.zeros_like(local_out)

    for head in range(heads):
        span = slice(head * size, (head + 1) * size)
        mixed = mixed_rows[:, span]
        scale = lax.rsqrt(jnp.mean(mixed * mixed, axis=1, keepdims=True) + 1e-5)
        given = headed_grad[:, span]
        gain_out[...] += jnp.sum(given * mixed * scale, axis=0, keepdims=True)
        scaled = gain[...] * given
        along = jnp.mean(mixed * scaled, axis=1, keepdims=True)
        grad = scale * scaled - mixed * (scale * scale * scale * along)
        grad_out[:, span] = grad
        local_out[head] += mm(effective[:, span], grad, 0, 0)


def backward_kernel(
    starts,
    base,
    lin_query,
    lin_key,
    lin_value,
    prior_query,
    prior_key,
    prior_value,
    edge,
    taps_query,
    taps_key,
    taps_value,
    rates,
    inverse_in,
    memory_in,
    entering,
    leaving,
    mixed_grad,
    query_out,
    key_out,
    value_out,
    edge_out,
    logit_out,
    taps_query_out,
    taps_key_out,
    taps_value_out,
    after,
    memory_grad,
):
    heads, size = entering.shape[0], entering.shape[1]
    width = heads * size
    step = pl.program_id(0)
    blocks = pl.num_programs(0)
    here = blocks - 1 - step
    count = starts.shape[0]
    every = range(heads)
    spans = [slice(head * size, (head + 1) * size) for head in every]

    @pl.when(step == 0)
    def _():
        after[...] = jnp.zeros_like(after)
        memory_grad[...] = leaving[...]
        taps_query_out[...] = jnp.zeros_like(taps_query_out)
        taps_key_out[...] = jnp.zeros_like(taps_key_out)
        taps_value_out[...] = jnp.zeros_like(taps_value_out)

    first = base[0] + here * BLOCK
    rows, columns, same, carried, final, through, reach = block_masks(first, starts, count)
    below = jnp.logical_and(same, columns < rows)
    upto = jnp.logical_and(same, columns <= rows)

    def convolved(number, lin, prior, taps, head):
        place = slice(number * width + head * size, number * width + (head + 1) * size)
        border = jnp.where(here == 0, edge[:, place], prior[:, spans[head]])
        joined = jnp.concatenate([border, lin[:, spans[head]]], axis=0)
        conv = short_conv(joined, taps[:, spans[head]], reach)
        return joined, conv, sigmoid(conv)

    def unit_scale(piece):
        return lax.rsqrt(jnp.sum(piece * piece, axis=1, keepdims=True) + 1e-6)

    query_parts = [convolved(0, lin_query, prior_query, taps_query, head) for head in every]
    key_parts = [convolved(1, lin_key, prior_key, taps_key, head) for head in every]
    value_parts = [convolved(2, lin_value, prior_value, taps_value, head) for head in every]
    query_scales = [unit_scale(conv * gate) for _, conv, gate in query_parts]
    key_scales = [unit_scale(conv * gate) for _, conv, gate in key_parts]
    queries = [conv * gate * scale for (_, conv, gate), scale in zip(query_parts, query_scales)]
    keys = [conv * gate * scale for (_, conv, gate), scale in zip(key_parts, key_scales)]
    values = [conv * gate for _, conv, gate in value_parts]
    rate_columns = [rates[:, head : head + 1] for head in every]
    rate_wide = [jnp.broadcast_to(column, (BLOCK, size)) for column in rate_columns]
    products = [
        mm(jnp.concatenate([queries[head], keys[head]], axis=0), keys[head], 1, 1)
        for head in every
    ]
    scores = [jnp.where(upto, part[:BLOCK], 0.0) for part in products]
    grams = [part[BLOCK:] for part in products]
    inverses = [inverse_in[0, head] for head in every]
    memories = [
        mm(memory_in[0, head][:, :size], entering[head]) + memory_in[0, head][:, size:]
        for head in every
    ]
    lefts = [carried * key for key in keys]
    wanted = [values[head] - mm(lefts[head], memories[head]) for head in every]
    residues = [mm(inverses[head], rate_wide[head] * wanted[head]) for head in every]
    given = [mixed_grad[:, span] for span in spans]
    score_sides = [mm(scores[head], given[head], 0, 0) for head in every]
    state_grads = [memory_grad[head] for head in every]
    last_keys = [final * key for key in keys]
    residue_grads = [
        score_sides[head] + mm(last_keys[head], state_grads[head]) for head in every
    ]
    solved_grads = [mm(inverses[head], residue_grads[head], 0, 0) for head in every]
    wanted_grads = [rate_wide[head] * solved_grads[head] for head in every]
    updates = [
        through * state_grads[head]
        + mm(
            jnp.concatenate([carried * queries[head], -lefts[head]], axis=0),
            jnp.concatenate([given[head], wanted_grads[head]], axis=0),
            0,
            0,
        )
        for head in every
    ]
    for head in every:
        memory_grad[head] = updates[head]
    outers = [
        mm(jnp.concatenate([given[head], solved_grads[head]], axis=0), residues[head], 1, 1)
        for head in every
    ]
    state_sides = [
        mm(jnp.concatenate([given[head], wanted_grads[head]], axis=0), memories[head], 1, 1)
        for head in every
    ]
    final_sides = [final * mm(residues[head], state_grads[head], 1, 1) for head in every]
    score_grads = [jnp.where(upto, part[:BLOCK], 0.0) for part in outers]
    strict_grads = [jnp.where(below, -part[BLOCK:], 0.0) for part in outers]
    gram_grads = [rate_wide[head] * strict_grads[head] for head in every]
    pairs = [
        jnp.concatenate([score_grads[head], gram_grads[head]], axis=0) for head in every
    ]
    key_sides = [mm(pairs[head], keys[head]) for head in every]
    turned_sides = [
        mm(pairs[head], jnp.concatenate([queries[head], keys[head]], axis=0), 0, 0)
        for head in every
    ]
    rate_grads = [
        jnp.sum(
            solved_grads[head] * wanted[head] + strict_grads[head] * grams[head],
            axis=1,
            keepdims=True,
        )
        for head in every
    ]
    lanes = lax.broadcasted_iota(jnp.int32, (BLOCK, rates.shape[1]), 1)
    logit_grad = jnp.zeros((BLOCK, rates.shape[1]), F32)
    for head in every:
        column = rate_columns[head]
        logit_grad = jnp.where(
            lanes == head, rate_grads[head] * column * (1.0 - column), logit_grad
        )
    logit_out[...] = logit_grad
    query_grads = [
        carried * state_sides[head][:BLOCK] + key_sides[head][:BLOCK] for head in every
    ]
    key_grads = [
        key_sides[head][BLOCK:]
        - carried * state_sides[head][BLOCK:]
        + turned_sides[head]
        + final_sides[head]
        for head in every
    ]
    query_grads = [
        scale * (grad - query * jnp.sum(query * grad, axis=1, keepdims=True))
        for scale, grad, query in zip(query_scales, query_grads, queries)
    ]
    key_grads = [
        scale * (grad - key * jnp.sum(key * grad, axis=1, keepdims=True))
        for scale, grad, key in zip(key_scales, key_grads, keys)
    ]
    spare = jnp.zeros((EDGE, size), F32)
    for number, (grads, parts, taps, lin_out, taps_out) in enumerate(
        (
            (query_grads, query_parts, taps_query, query_out, taps_query_out),
            (key_grads, key_parts, taps_key, key_out, taps_key_out),
            (wanted_grads, value_parts, taps_value, value_out, taps_value_out),
        )
    ):
        for head in every:
            span = spans[head]
            place = slice(number * width + head * size, number * width + (head + 1) * size)
            joined, conv, gate = parts[head]
            conv_grad = grads[head] * gate * (1.0 + conv * (1.0 - gate))
            lin_grad = taps[3:4, span] * conv_grad
            tail = spare
            taps_grad = [jnp.sum(conv_grad * joined[EDGE:], axis=0, keepdims=True)]
            for back in range(1, 4):
                part = conv_grad * reach[back]
                tap = taps[3 - back : 4 - back, span]
                lin_grad = lin_grad + tap * jnp.concatenate([part, spare], axis=0)[
                    back : back + BLOCK
                ]
                tail = tail + tap * jnp.concatenate([spare, part[:EDGE]], axis=0)[
                    back : back + EDGE
                ]
                taps_grad.append(
                    jnp.sum(part * joined[EDGE - back : EDGE - back + BLOCK], axis=0, keepdims=True)
                )
            taps_out[:, span] += jnp.concatenate(taps_grad[::-1], axis=0)
            lin_out[: BLOCK - EDGE, span] = lin_grad[: BLOCK - EDGE]
            lin_out[BLOCK - EDGE :, span] = lin_grad[BLOCK - EDGE :] + after[:, place]
            after[:, place] = tail
            edge_out[:, place] = tail


def on_chip(kernel, name, **settings):
    return pl.pallas_call(
        kernel,
        name=name,
        cost_estimate=pl.CostEstimate(flops=1, bytes_accessed=1, transcendentals=0),
        compiler_params=pltpu.CompilerParams(
            dimension_semantics=("arbitrary",), vmem_limit_bytes=48 * 1024 * 1024
        ),
        **settings,
    )


def whole(shape):
    return pl.BlockSpec(shape, lambda i: (0,) * len(shape))


def scalars():
    return pl.BlockSpec(memory_space=pltpu.SMEM)


def delta_forward(starts, base, lins, edge, taps, rates, heads, size):
    length, width = lins[0].shape
    blocks = length // BLOCK
    row_block = pl.BlockSpec((BLOCK, width), lambda i: (i, 0))
    return on_chip(
        forward_kernel,
        "delta_forward",
        grid=(blocks,),
        in_specs=[scalars(), scalars()]
        + [row_block] * 3
        + [whole((EDGE, 3 * width))]
        + [whole((4, width))] * 3
        + [pl.BlockSpec((BLOCK, heads), lambda i: (i, 0))],
        out_specs=[
            pl.BlockSpec((1, heads, BLOCK, BLOCK), lambda i: (i, 0, 0, 0)),
            row_block,
            row_block,
            pl.BlockSpec((1, heads, size, 2 * size), lambda i: (i, 0, 0, 0)),
            whole((heads, size, 2 * size)),
        ],
        out_shape=[
            jax.ShapeDtypeStruct((blocks, heads, BLOCK, BLOCK), F32),
            jax.ShapeDtypeStruct((length, width), F32),
            jax.ShapeDtypeStruct((length, width), F32),
            jax.ShapeDtypeStruct((blocks, heads, size, 2 * size), F32),
            jax.ShapeDtypeStruct((heads, size, 2 * size), F32),
        ],
        scratch_shapes=[
            pltpu.VMEM((EDGE, 3 * width), F32),
            pltpu.VMEM((heads, size, 2 * size), F32),
        ],
    )(starts, base, *lins, edge, *taps, rates)


def delta_output(effective, local, entering, gain):
    length, width = local.shape
    heads, size = entering.shape[0], entering.shape[1]
    rows = min(length, 256)
    row_block = pl.BlockSpec((rows, width), lambda i: (i, 0))
    return on_chip(
        output_kernel,
        "delta_output",
        grid=(length // rows,),
        in_specs=[row_block, row_block, whole((heads, size, size)), whole((1, size))],
        out_specs=[row_block, row_block, row_block],
        out_shape=[
            jax.ShapeDtypeStruct((length, width), F32),
            jax.ShapeDtypeStruct((length, width), F32),
            jax.ShapeDtypeStruct((length, width), BF16),
        ],
    )(effective, local, entering, gain)


def norm_back(headed_grad, mixed_rows, effective, gain, heads, size):
    length, width = headed_grad.shape
    rows = min(length, 256)
    row_block = pl.BlockSpec((rows, width), lambda i: (i, 0))
    return on_chip(
        norm_back_kernel,
        "norm_back",
        grid=(length // rows,),
        in_specs=[row_block, row_block, row_block, whole((1, size))],
        out_specs=[row_block, whole((1, size)), whole((heads, size, size))],
        out_shape=[
            jax.ShapeDtypeStruct((length, width), F32),
            jax.ShapeDtypeStruct((1, size), F32),
            jax.ShapeDtypeStruct((heads, size, size), F32),
        ],
    )(headed_grad, mixed_rows, effective, gain)


def norm_pull_kernel(odd, part, other, values, gain, given, grad_out, rounded_out, gain_out):
    step = pl.program_id(0)
    second = step * 2 // pl.num_programs(0)

    @pl.when(step == 0)
    def _():
        gain_out[...] = jnp.zeros_like(gain_out)

    grad = jnp.where(second == odd[0], part[...], other[...])
    value = values[...]
    scale = lax.rsqrt(jnp.mean(value * value, axis=1, keepdims=True) + 1e-5)
    gain_out[...] += jnp.sum(grad * value * scale, axis=0, keepdims=True)
    scaled = gain[...] * grad
    along = jnp.mean(value * scaled, axis=1, keepdims=True)
    result = given[...] + (scale * scaled - value * (scale * scale * scale * along))
    grad_out[...] = result
    rounded_out[...] = result.astype(rounded_out.dtype)


def norm_pulled(halves, values, gain, given):
    length, width = values.shape
    rows = length // 8
    odd = (lax.axis_index("head") % 2).astype(jnp.int32).reshape(1)
    row_block = pl.BlockSpec((rows, width), lambda i: (i, 0))
    half_block = pl.BlockSpec((rows, width), lambda i: (i % 4, 0))
    return on_chip(
        norm_pull_kernel,
        "norm_pull",
        grid=(8,),
        in_specs=[scalars(), half_block, half_block, row_block, whole((1, width)), row_block],
        out_specs=[row_block, row_block, whole((1, width))],
        out_shape=[
            jax.ShapeDtypeStruct((length, width), F32),
            jax.ShapeDtypeStruct((length, width), BF16),
            jax.ShapeDtypeStruct((1, width), F32),
        ],
    )(odd, *halves, values, gain.reshape(1, width), given)


def beside_kernel(first, second, out):
    width = first.shape[1]
    out[:, :width] = first[...].astype(out.dtype)
    out[:, width:] = second[...].astype(out.dtype)


def above_kernel(first, second, out):
    rows = first.shape[0]
    out[:rows] = first[...].astype(out.dtype)
    out[rows:] = second[...].astype(out.dtype)


def rounded_beside(first, second):
    length, width = first.shape
    rows = min(length, 256)
    block = pl.BlockSpec((rows, width), lambda i: (i, 0))
    return on_chip(
        beside_kernel,
        "rounded_beside",
        grid=(length // rows,),
        in_specs=[block, block],
        out_specs=pl.BlockSpec((rows, 2 * width), lambda i: (i, 0)),
        out_shape=jax.ShapeDtypeStruct((length, 2 * width), BF16),
    )(first, second)


def rounded_above(first, second):
    rows, width = first.shape
    columns = min(width, 256)
    block = pl.BlockSpec((rows, columns), lambda i: (0, i))
    return on_chip(
        above_kernel,
        "rounded_above",
        grid=(width // columns,),
        in_specs=[block, block],
        out_specs=pl.BlockSpec((2 * rows, columns), lambda i: (0, i)),
        out_shape=jax.ShapeDtypeStruct((2 * rows, width), BF16),
    )(first, second)


def delta_backward(
    starts, base, lins, edge, taps, rates, inverse, memories, entering, leaving, mixed_grad
):
    length, width = lins[0].shape
    heads, size = entering.shape[0], entering.shape[1]
    blocks = length // BLOCK
    ratio = BLOCK // EDGE
    row_block = pl.BlockSpec((BLOCK, width), lambda i: (blocks - 1 - i, 0))
    prior = pl.BlockSpec(
        (EDGE, width), lambda i: (jnp.maximum((blocks - 1 - i) * ratio - 1, 0), 0)
    )
    rate_block = pl.BlockSpec((BLOCK, heads), lambda i: (blocks - 1 - i, 0))
    return on_chip(
        backward_kernel,
        "delta_backward",
        grid=(blocks,),
        in_specs=[scalars(), scalars()]
        + [row_block] * 3
        + [prior] * 3
        + [whole((EDGE, 3 * width))]
        + [whole((4, width))] * 3
        + [
            rate_block,
            pl.BlockSpec((1, heads, BLOCK, BLOCK), lambda i: (blocks - 1 - i, 0, 0, 0)),
            pl.BlockSpec((1, heads, size, 2 * size), lambda i: (blocks - 1 - i, 0, 0, 0)),
            whole((heads, size, size)),
            whole((heads, size, size)),
            row_block,
        ],
        out_specs=[row_block] * 3
        + [whole((EDGE, 3 * width)), rate_block]
        + [whole((4, width))] * 3,
        out_shape=[jax.ShapeDtypeStruct((length, width), F32)] * 3
        + [
            jax.ShapeDtypeStruct((EDGE, 3 * width), F32),
            jax.ShapeDtypeStruct((length, heads), F32),
        ]
        + [jax.ShapeDtypeStruct((4, width), F32)] * 3,
        scratch_shapes=[
            pltpu.VMEM((EDGE, 3 * width), F32),
            pltpu.VMEM((heads, size, size), F32),
        ],
    )(starts, base, *lins, *lins, edge, *taps, rates, inverse, memories, entering, leaving, mixed_grad)


def swap(block, axis, bit):
    count = lax.axis_size(axis)
    return lax.ppermute(block, axis, [(i, i ^ bit) for i in range(count)])


def shift(block, axis, distance):
    devices = range(lax.axis_size(axis))
    route = [(i - distance, i) for i in devices if i - distance in devices]
    return lax.ppermute(block, axis, route)


def begun_over_head(term):
    odd = lax.axis_index("head") % 2
    half = term.shape[0] // 2
    keep = lax.dynamic_slice_in_dim(term, odd * half, half, 0)
    send = lax.dynamic_slice_in_dim(term, (1 - odd) * half, half, 0)
    return keep + swap(send, "head", 1)


def ended_over_head(part, *gates):
    part = part + after(swap(part, "head", 2), *gates)
    return part, swap(part, "head", 1)


def whole_rows(part, other):
    return jnp.where(
        lax.axis_index("head") % 2 == 0,
        jnp.concatenate([part, other], axis=0),
        jnp.concatenate([other, part], axis=0),
    )


def after(value, *others):
    return lax.optimization_barrier((value,) + others)[0] if others else value


def summed_everywhere(vector, axis):
    count = lax.axis_size(axis)
    bit = 1
    while bit < count:
        vector = vector + swap(vector, axis, bit)
        bit *= 2
    return vector


def relative_order(bits):
    if not bits:
        return [0]
    rest = relative_order(bits[1:])
    return [index ^ bits[0] for index in rest] + rest


def seq_bits():
    bits = []
    while 1 << len(bits) < lax.axis_size("seq"):
        bits.append(1 << len(bits))
    return bits


def arrange_kernel(places, rows, out):
    out[...] = rows[...]


def arranged(rows, places):
    length, size = rows.shape[0], rows.shape[1] // lax.axis_size("seq")
    if size % 128:
        return jnp.concatenate(
            [lax.dynamic_slice_in_dim(rows, place * size, size, 1) for place in places], axis=1
        )
    return pl.pallas_call(
        arrange_kernel,
        name="arrange",
        cost_estimate=pl.CostEstimate(flops=1, bytes_accessed=1, transcendentals=0),
        grid_spec=pltpu.PrefetchScalarGridSpec(
            num_scalar_prefetch=1,
            grid=(len(places),),
            in_specs=[pl.BlockSpec((length, size), lambda i, places: (0, places[i]))],
            out_specs=pl.BlockSpec((length, size), lambda i, places: (0, i)),
        ),
        out_shape=jax.ShapeDtypeStruct(rows.shape, rows.dtype),
        compiler_params=pltpu.CompilerParams(dimension_semantics=("arbitrary",)),
    )(jnp.stack(places).astype(jnp.int32), rows)


def relative_places():
    here = lax.axis_index("seq")
    return [here ^ index for index in relative_order(seq_bits())]


def product(rows, others, rows_first):
    return matmul(rows, others, 0, 0) if rows_first else matmul(others, rows, 0, 0)


def received(given, kept, axis, place):
    bits = seq_bits()
    kept = kept + swap(given, "seq", bits[place])
    if place + 1 == len(bits):
        return None, kept
    size = kept.shape[axis] // 2
    return lax.slice_in_dim(kept, 0, size, axis=axis), lax.slice_in_dim(
        kept, size, 2 * size, axis=axis
    )


def finished(given, kept, axis, place):
    while place < len(seq_bits()):
        given, kept = received(given, kept, axis, place)
        place += 1
    return kept


def chain(transfer, offset, distance, turned=False, between=()):
    hops = max(lax.axis_size("seq") // 2, 1)
    groups = 2
    count = offset.shape[0] // groups
    picks = [slice(index * count, (index + 1) * count) for index in range(groups)]
    form = "hji,hjk->hik" if turned else "hij,hjk->hik"
    states = [shift(offset[pick], "seq", distance) for pick in picks]
    for hop in range(hops - 1):
        if hop < len(between):
            states[0] = after(states[0], between[hop])
        moved = [
            jnp.einsum(form, transfer[pick], state, precision=lax.Precision.HIGH) + offset[pick]
            for pick, state in zip(picks, states)
        ]
        states = [shift(part, "seq", distance) for part in moved]
    return jnp.concatenate(states, axis=0)


def row_norm(values):
    return lax.rsqrt(jnp.mean(values * values, axis=-1, keepdims=True) + 1e-05)


def matmul(left, right, left_dim=1, right_dim=0):
    return lax.dot_general(
        left, right, (((left_dim,), (right_dim,)), ((), ())), preferred_element_type=F32
    )


def shards(
    hidden,
    doc_starts,
    norm_gain,
    w_query,
    w_key,
    w_value,
    w_strength,
    strength_bias,
    conv_query,
    conv_key,
    conv_value,
    head_gain,
    w_output,
    ffn_gain,
    w_gate,
    w_up,
    w_down,
    out_grad,
):
    length = hidden.shape[0]
    size = head_gain.shape[0]
    heads = strength_bias.shape[0]
    width = heads * size
    seq_rank = lax.axis_index("seq")
    seq_count = lax.axis_size("seq")
    base = (seq_rank * length).astype(jnp.int32).reshape(1)
    taps = tuple(part.astype(F32) for part in (conv_query, conv_key, conv_value))
    gain = head_gain.reshape(1, size)

    scale_one = row_norm(hidden)
    normed = (hidden * scale_one * norm_gain).astype(BF16)
    w_wide = w_output.astype(F32)
    w_across = swap(w_wide, "head", 2)
    lins = tuple(matmul(normed, part) for part in (w_query, w_key, w_value))
    tails = jnp.concatenate([part[-EDGE:] for part in lins], axis=1)
    edge = shift(tails, "seq", 1)
    rates = jax.nn.sigmoid(matmul(normed, w_strength) + strength_bias)
    inverse, effective, local, memories, last = delta_forward(
        doc_starts, base, lins, edge, taps, rates, heads, size
    )
    transfer, offset = last[:, :, :size], last[:, :, size:]
    entering = chain(transfer, offset, 1)
    mixed_rows, headed_wide, headed = delta_output(effective, local, entering, gain)
    h_across = swap(headed_wide, "head", 2)
    h_core = swap(headed_wide, "head", 1)
    w_late, w_across = after((w_wide, w_across), headed)
    w_near = rounded_above(w_late, swap(w_late, "head", 1))
    w_distant = rounded_above(w_across, swap(w_across, "head", 1))
    middle = hidden + matmul(rounded_beside(headed_wide, h_core), w_near)
    ffn_cot = after(out_grad, headed).astype(BF16)
    cot_ordered = arranged(ffn_cot, relative_places())
    h_across = after(h_across, middle, w_distant, cot_ordered)
    h_far = swap(h_across, "head", 1)
    middle = middle + matmul(rounded_beside(h_across, h_far), w_distant)
    scale_two = row_norm(middle)
    normed_two = (middle * scale_two * ffn_gain).astype(BF16)
    gate_rows = matmul(normed_two, w_gate)
    upward = matmul(normed_two, w_up)
    sigma = jax.nn.sigmoid(gate_rows)
    silu_gate = gate_rows * sigma
    active = (silu_gate * upward).astype(BF16)
    half = ffn_cot.shape[1] // 2
    split = active.shape[1] // 128 * 7 // 8 * 128
    lead, rest = active[:, :split], active[:, split:]
    lead_given = product(cot_ordered[:, :half], lead, False)
    ffn_cot = after(ffn_cot, lead_given)
    active_grad = matmul(ffn_cot, w_down, 1, 1)
    gate_cot = (active_grad * upward * sigma * (1.0 + gate_rows * (1.0 - sigma))).astype(BF16)
    up_cot = (active_grad * silu_gate).astype(BF16)
    both_term = matmul(normed_two, jnp.concatenate([gate_cot, up_cot], axis=1), 0, 0)
    both_grad = lax.psum_scatter(both_term, "seq", scatter_dimension=0, tiled=True)
    gate_late, up_late = after((gate_cot, up_cot), both_term)
    two_part = matmul(gate_late, w_gate, 1, 1) + matmul(up_late, w_up, 1, 1)
    two_begun = begun_over_head(two_part)
    ffn_begun = begun_over_head(matmul(after(active, two_begun), w_down))
    cot_ordered = after(cot_ordered, two_begun)
    lead_kept = product(cot_ordered[:, half:], lead, False)
    rest_given = product(cot_ordered[:, :half], rest, False)
    rest_kept = product(cot_ordered[:, half:], rest, False)
    middle_grad, branch_cot, ffn_gain_part = norm_pulled(
        ended_over_head(
            two_begun, ffn_begun, lead_kept, rest_given, rest_kept
        ),
        middle,
        ffn_gain,
        out_grad,
    )
    headed_grad = matmul(branch_cot, w_output, 1, 1)
    mixed_grad, head_gain_part, local_grad = norm_back(
        headed_grad, mixed_rows, effective, gain, heads, size
    )
    leaving = chain(transfer, local_grad, -1, True)
    lead_given, lead_kept = received(lead_given, lead_kept, 1, 0)
    lead_given = after(lead_given, leaving)
    leaving = after(leaving, lead_given)
    back = delta_backward(
        doc_starts, base, lins, edge, taps, rates, inverse, memories, entering, leaving, mixed_grad
    )
    ffn_halves = ended_over_head(ffn_begun)
    lead_given, lead_kept = received(lead_given, lead_kept, 1, 1)
    returned, logit_grad = after(
        (shift(back[3], "seq", -1), back[4]), lead_given, ffn_halves[0]
    )
    branch_ordered = arranged(after(branch_cot, back[3]), relative_places())
    mix_given = jnp.concatenate(
        [rest_given, product(branch_ordered[:, :half], headed, False)], axis=0
    )
    mix_given = after(mix_given, returned)
    cots = tuple(
        jnp.concatenate(
            [part[:-EDGE], part[-EDGE:] + returned[:, index * width : (index + 1) * width]], axis=0
        ).astype(BF16)
        for index, part in enumerate(back[:3])
    )
    strength_cot = logit_grad.astype(BF16)
    cot = after(jnp.concatenate(cots, axis=1), lead_given)
    lin_term = product(normed, cot, True)
    lin_grad = lax.psum_scatter(lin_term, "seq", scatter_dimension=0, tiled=True)
    mix_kept = jnp.concatenate(
        [rest_kept, product(branch_ordered[:, half:], headed, False)], axis=0
    )
    mix_given, mix_kept = received(mix_given, after(mix_kept, lin_term), 1, 0)
    late_cots, strength_cot = after((cots, strength_cot), lin_term, mix_given)
    first_part = matmul(late_cots[0], w_query, 1, 1)
    first_part = first_part + matmul(late_cots[1], w_key, 1, 1)
    first_part = first_part + matmul(late_cots[2], w_value, 1, 1)
    first_part = first_part + matmul(strength_cot, w_strength, 1, 1)
    norm_gain_part = jnp.sum(first_part * hidden * scale_one, axis=0)
    shared = summed_everywhere(
        jnp.concatenate([norm_gain_part, head_gain_part.reshape(-1)]), "head"
    )
    first_begun = after(begun_over_head(first_part), shared)
    lead_kept = finished(lead_given, lead_kept, 1, 2)
    mix_given, mix_kept = received(mix_given, after(mix_kept, first_begun), 1, 1)
    first_halves = ended_over_head(first_begun, mix_given, lead_kept, both_grad)
    hidden_grad = norm_pulled(first_halves, hidden, norm_gain, middle_grad)[0]
    block_output = middle + whole_rows(*ffn_halves)
    mix_kept = finished(mix_given, after(mix_kept, hidden_grad, block_output), 1, 2)
    hidden_units = gate_cot.shape[1]
    w_gate_grad, w_up_grad = both_grad[:, :hidden_units], both_grad[:, hidden_units:]
    lin_grad = after(lin_grad, hidden_grad, block_output, w_gate_grad, w_up_grad, mix_kept)
    lin_grads = tuple(lin_grad[:, index * width : (index + 1) * width] for index in range(3))
    rest_rows = rest.shape[1]
    w_down_grad = jnp.concatenate([lead_kept, mix_kept[:rest_rows]], axis=0)
    w_output_grad = mix_kept[rest_rows:]
    strength_term = matmul(strength_cot, normed, 0, 0)

    small = jnp.concatenate(
        [
            shared,
            strength_term.reshape(-1),
            ffn_gain_part.reshape(-1),
        ]
        + [part.reshape(-1) for part in back[5:8]]
        + [jnp.sum(logit_grad, axis=0)]
    )
    small = summed_everywhere(small, "seq")
    features = norm_gain.shape[0]
    block = features // seq_count
    cut = [features, size, heads * features, features] + [4 * width] * 3 + [heads]
    parts, at = [], 0
    for extent in cut:
        parts.append(small[at : at + extent])
        at += extent

    def own(vector, axis=0):
        return lax.dynamic_slice_in_dim(vector, seq_rank * block, block, axis)

    return (
        block_output,
        hidden_grad,
        own(parts[0]),
        lin_grads[0],
        lin_grads[1],
        lin_grads[2],
        own(parts[2].reshape(heads, features), 1).T,
        parts[7],
        parts[4].reshape(4, width),
        parts[5].reshape(4, width),
        parts[6].reshape(4, width),
        parts[1],
        w_output_grad,
        own(parts[3]),
        w_gate_grad,
        w_up_grad,
        w_down_grad,
    )


def solution(mesh):
    return jax.shard_map(
        shards,
        mesh=mesh,
        in_specs=(
            P("seq", None),
            P(),
            P(),
            P(None, "head"),
            P(None, "head"),
            P(None, "head"),
            P(None, "head"),
            P("head"),
            P(None, "head"),
            P(None, "head"),
            P(None, "head"),
            P(),
            P("head", None),
            P(),
            P(None, "head"),
            P(None, "head"),
            P("head", None),
            P("seq", None),
        ),
        out_specs=(
            P("seq", None),
            P("seq", None),
            P("seq"),
            P("seq", "head"),
            P("seq", "head"),
            P("seq", "head"),
            P("seq", "head"),
            P("head"),
            P(None, "head"),
            P(None, "head"),
            P(None, "head"),
            P(),
            P("head", "seq"),
            P("seq"),
            P("seq", "head"),
            P("seq", "head"),
            P("head", "seq"),
        ),
        check_vma=False,
    )
```
